32 devices in a mesh: subj: 4 (over x, core), row: 4 (over z), col: 2 (over y).
Axes of the slice: x: 2, y: 2, z: 4, core: 2. Of those that a mesh axis runs over, the one named last changes fastest.
Arguments:
- series: float32 [8, 5120, 1200], P('subj', ('row', 'col')), may hold values from -4000 to 4000
- block_start: int32 [5], replicated, may hold values from 0 to 4096, as said below
Outputs:
- connectome: float32 [5120, 5120], P(('row', 'col'), 'subj')
The draws below stay inside these ranges and needn't reach their ends.
Inputs may be any that keep to these rules, and one draw needn't show every extreme that they name: `block_start`: each entry is a multiple of 1024 and no two entries are equal.
All inputs are finite; a program needn't handle non-finite values.
Results may differ from the reference program's by a relative error of at most 0.0012.
Values may be sent and summed in bfloat16 or wider, within the bound.
No kernel may reach another device: no remote copies, remote signals or barrier semaphores. Data moves between devices by JAX's collectives and lax.ppermute only.
A program may use at most 192 MiB of HBM per device.

```python
import jax
import jax.numpy as jnp
from jax import lax

T_SIZE = 1200
B = 1024
NB = 5
SUBJECTS = 8
G = 5120


def draw_series(key, part):
    key = jax.random.fold_in(key, 7)
    subkeys = jax.random.split(key, 8)
    network_count = 64
    member = jax.random.randint(subkeys[0], (G,), 0, network_count)
    loading = jax.random.normal(subkeys[1], (G,)) * 1.2
    global_loading = jax.random.uniform(subkeys[2], (G,), minval=0.2, maxval=1.2)
    signal = jax.random.normal(subkeys[3], (SUBJECTS, network_count, T_SIZE))
    common = jax.random.normal(subkeys[4], (SUBJECTS, 1, T_SIZE))
    noise_part = jax.random.normal(subkeys[5], (SUBJECTS, G, T_SIZE))
    row_scale = jnp.exp(jax.random.uniform(subkeys[6], (SUBJECTS, G, 1), minval=jnp.log(0.5), maxval=jnp.log(8.0)))
    offset = jax.random.uniform(subkeys[7], (SUBJECTS, G, 1), minval=-3.0, maxval=3.0)
    mixture = noise_part + global_loading[None, :, None] * common + loading[None, :, None] * jnp.take(signal, member, axis=1)
    return (offset + row_scale * mixture).astype(jnp.float32)


def draw_block_start(key, part):
    key = jax.random.fold_in(key, 3)
    return (jax.random.permutation(key, NB) * B).astype(jnp.int32)


def setup_inputs(seed: int = 0) -> dict:
    seeds = jax.random.split(jax.random.key(seed), 3)
    return {
        "series": draw_series(jax.random.fold_in(seeds[2], 71), 0),
        "block_start": draw_block_start(jax.random.fold_in(seeds[2], 71), 0),
    }


clip_limit = 0.99
epsilon = 1e-05

def normalize(raw_rows):
    values = raw_rows.astype(jnp.float32)
    center = lax.optimization_barrier(jnp.mean(values, axis=-1, keepdims=True))
    spread = lax.optimization_barrier(jnp.mean((values - center) ** 2, axis=-1, keepdims=True))
    return ((values - center) * lax.rsqrt(spread + epsilon)).astype(jnp.bfloat16)

def fisher(products, length):
    scaled = jnp.clip(products / length, -clip_limit, clip_limit)
    return (0.5 * (jnp.log1p(scaled) - jnp.log1p(-scaled))).astype(jnp.bfloat16)

def reference(series, block_start):
    block_order = (block_start // B).astype(jnp.int32)

    def one_subject(subject, running):
        normed = normalize(series[subject])
        ordered = jnp.take(normed.reshape(NB, B, T_SIZE), block_order, axis=0).reshape(NB * B, T_SIZE)
        products = jnp.dot(ordered, ordered.T, preferred_element_type=jnp.float32)
        scores = lax.optimization_barrier(fisher(products, T_SIZE))
        return running + scores.astype(jnp.float32)
    running = lax.fori_loop(0, SUBJECTS, one_subject, jnp.zeros((NB * B, NB * B), jnp.float32))
    return running / SUBJECTS
```

```python
import functools
import math

import jax
import jax.numpy as jnp
import numpy as np
from jax import lax
from jax.experimental import pallas as pl
from jax.experimental.pallas import tpu as pltpu
from jax.sharding import PartitionSpec as P

clip_limit = 0.99
epsilon = 1e-05
SLABS = ("row", "col")


def cycle(rows, cols):
    if cols == 1:
        return list(range(rows))
    walk = [(r, 0) for r in range(rows)]
    for i, r in enumerate(reversed(range(rows))):
        back = list(range(1, cols))
        walk += [(r, c) for c in (back if i % 2 == 0 else back[::-1])]
    return [r * cols + c for r, c in walk]


def normalize_kernel(x_ref, o_ref):
    values = x_ref[...]
    center = jnp.mean(values, axis=-1, keepdims=True)
    away = values - center
    spread = jnp.mean(away * away, axis=-1, keepdims=True)
    o_ref[...] = (away * lax.rsqrt(spread + epsilon)).astype(jnp.bfloat16)


def normalize(series, subject, half, half_rows):
    duration = series.shape[2]
    step = max(d for d in range(16, 161, 16) if half_rows % d == 0)
    steps = half_rows // step
    return pl.pallas_call(
        normalize_kernel,
        grid=(steps,),
        in_specs=[pl.BlockSpec((None, step, duration), lambda i: (subject, half * steps + i, 0))],
        out_specs=pl.BlockSpec((step, duration), lambda i: (i, 0)),
        out_shape=jax.ShapeDtypeStruct((half_rows, duration), jnp.bfloat16),
    )(series)


def scores_kernel(
    source_ref, block_start_ref, place_ref, *refs, slab, half_rows, granule, block_rows, chips, chunk, duration
):
    count = source_ref.shape[0]
    pieces, (same_ref, other_ref, ordered, place_of, sem) = refs[: 2 * count], refs[2 * count :]
    blocks = block_start_ref.shape[0]
    for a in range(blocks):
        place_of[block_start_ref[a] // block_rows] = a

    for slot in range(count):
        for half in range(2):
            piece = pieces[2 * slot + half]
            first = source_ref[slot] * slab + half * half_rows

            def start(g, _, piece=piece, first=first):
                stored = first + g * granule
                block = stored // block_rows
                row = place_of[block] * block_rows + (stored - block * block_rows)
                pltpu.make_async_copy(
                    piece.at[pl.ds(pl.multiple_of(g * granule, granule), granule)],
                    ordered.at[pl.ds(pl.multiple_of(row, granule), granule)],
                    sem,
                ).start()
                return 0

            lax.fori_loop(0, half_rows // granule, start, 0)
    pltpu.make_async_copy(ordered, ordered, sem).wait()

    position, subj = place_ref[0], place_ref[1]
    chip, core = subj // 2, subj % 2
    limit = clip_limit * duration
    width = math.gcd(chunk, 256)
    for away in range(chips):
        for flip, out_ref in ((0, same_ref), (1, other_ref)):
            owner = (chip + away) % chips * 2 + (core + flip) % 2

            def tile(k, _, away=away, out_ref=out_ref, owner=owner):
                own = ordered[pl.ds(pl.multiple_of(position * slab, granule), slab)]
                first = pl.multiple_of(owner * chunk + k * width, width)
                columns = ordered[pl.ds(first, width)]
                products = lax.dot_general(
                    own, columns, (((1,), (1,)), ((), ())), preferred_element_type=jnp.float32
                )
                products = jnp.clip(products, -limit, limit)
                score = 0.5 * (jnp.log(duration + products) - jnp.log(duration - products))
                out_ref[away, :, pl.ds(pl.multiple_of(k * width, width), width)] = score.astype(jnp.bfloat16)
                return 0

            lax.fori_loop(0, chunk // width, tile, 0)


def scores(source, block_start, place, pieces, slab, window, chips):
    half_rows, duration = pieces[0].shape
    block_rows = window // block_start.shape[0]
    granule = math.gcd(half_rows, block_rows)
    chunk = window // (2 * chips)
    out = jax.ShapeDtypeStruct((chips, slab, chunk), jnp.bfloat16)
    smem = pl.BlockSpec(memory_space=pltpu.SMEM)
    return pl.pallas_call(
        functools.partial(
            scores_kernel,
            slab=slab,
            half_rows=half_rows,
            granule=granule,
            block_rows=block_rows,
            chips=chips,
            chunk=chunk,
            duration=duration,
        ),
        in_specs=[smem, smem, smem] + [pl.BlockSpec(memory_space=pl.ANY)] * len(pieces),
        out_shape=[out, out],
        scratch_shapes=[
            pltpu.VMEM((window, duration), jnp.bfloat16),
            pltpu.SMEM((block_start.shape[0],), jnp.int32),
            pltpu.SemaphoreType.DMA,
        ],
        compiler_params=pltpu.CompilerParams(vmem_limit_bytes=48 * 2**20),
        cost_estimate=pl.CostEstimate(
            flops=2 * slab * window * duration,
            bytes_accessed=2 * window * (duration + slab),
            transcendentals=2 * slab * window,
        ),
    )(source, block_start, place, *pieces)


def on_device(series, block_start):
    local_subjects, slab, duration = series.shape
    rows, cols = lax.axis_size("row"), lax.axis_size("col")
    count = rows * cols
    window = count * slab
    subjs = lax.axis_size("subj")
    chips = subjs // 2
    half_rows = slab // 2
    order = cycle(rows, cols)
    onward = [(order[i], order[(i + 1) % count]) for i in range(count)]
    backward = [(b, a) for a, b in onward]
    reach = count // 2
    offsets = [0]
    for d in range(1, reach):
        offsets += [d, -d]
    offsets.append(reach)
    table = np.zeros((count, count), np.int32)
    for i, device in enumerate(order):
        table[device] = [order[(i - d) % count] for d in offsets]
    position = lax.axis_index(SLABS)
    source = jnp.asarray(table)[position]
    place = jnp.stack([position, lax.axis_index("subj")]).astype(jnp.int32)

    def gather(own):
        got = [own]
        ahead, behind = list(own), list(own)
        for d in range(1, reach):
            ahead = [lax.ppermute(piece, SLABS, onward) for piece in ahead]
            behind = [lax.ppermute(piece, SLABS, backward) for piece in behind]
            got += [ahead, behind]
        got.append([lax.ppermute(ahead[0], SLABS, onward), lax.ppermute(behind[1], SLABS, backward)])
        return [piece for pair in got for piece in pair]

    swap = [(s, s ^ 1) for s in range(subjs)]

    def share(subject, own):
        same, other = scores(source, block_start, place, gather(own), slab, window, chips)
        crossed = lax.ppermute(other, "subj", swap)
        mine = same[0].astype(jnp.float32) + crossed[0].astype(jnp.float32)
        for d in range(1, chips):
            part = same[d].astype(jnp.float32) + crossed[d].astype(jnp.float32)
            mine = mine + lax.ppermute(part, "subj", [(s, (s + 2 * d) % subjs) for s in range(subjs)])
        return mine

    owns = [[normalize(series, a, half, half_rows) for half in range(2)] for a in range(local_subjects)]
    total = share(0, owns[0])
    for a in range(1, local_subjects):
        total = total + share(a, owns[a])
    return total / (local_subjects * subjs)


def solution(mesh):
    return jax.shard_map(
        on_device,
        mesh=mesh,
        in_specs=(P("subj", SLABS, None), P()),
        out_specs=P(SLABS, "subj"),
        check_vma=False,
    )
```

```python
import functools
import math

import jax
import jax.numpy as jnp
import numpy as np
from jax import lax
from jax.experimental import pallas as pl
from jax.experimental.pallas import tpu as pltpu
from jax.sharding import PartitionSpec as P

clip_limit = 0.99
epsilon = 1e-05
SLABS = ("row", "col")
LANES = 128
VMEM = pltpu.CompilerParams(vmem_limit_bytes=56 * 2**20)
ANY = pl.BlockSpec(memory_space=pl.ANY)


def cycle(rows, cols):
    if cols == 1:
        return list(range(rows))
    walk = [(r, 0) for r in range(rows)]
    for i, r in enumerate(reversed(range(rows))):
        back = list(range(1, cols))
        walk += [(r, c) for c in (back if i % 2 == 0 else back[::-1])]
    return [r * cols + c for r, c in walk]


def normalize_kernel(x_ref, first_ref, *other_refs):
    subjects, rows, duration = x_ref.shape
    body = duration // LANES * LANES
    tail = duration - body
    tails = []
    for a in range(subjects):
        values = x_ref[a]
        center = jnp.mean(values, axis=-1, keepdims=True)
        away = values - center
        spread = jnp.mean(away * away, axis=-1, keepdims=True)
        normed = (away * lax.rsqrt(spread + epsilon)).astype(jnp.bfloat16)
        (first_ref if a == 0 else other_refs[a - 1])[:, :body] = normed[:, :body]
        tails.append(normed[:, body:])
    tails.append(jnp.zeros((rows, LANES - subjects * tail), jnp.bfloat16))
    first_ref[:, body:] = jnp.concatenate(tails, axis=1)


def normalize(series, half, half_rows):
    subjects, _, duration = series.shape
    body = duration // LANES * LANES
    step = max(d for d in range(16, 161, 16) if half_rows % d == 0)
    steps = half_rows // step
    widths = [body + LANES] + [body] * (subjects - 1)
    return pl.pallas_call(
        normalize_kernel,
        grid=(steps,),
        in_specs=[pl.BlockSpec((subjects, step, duration), lambda i: (0, half * steps + i, 0))],
        out_specs=[pl.BlockSpec((step, w), lambda i: (i, 0)) for w in widths],
        out_shape=[jax.ShapeDtypeStruct((half_rows, w), jnp.bfloat16) for w in widths],
        compiler_params=VMEM,
    )(series)


def after(piece, *others):
    def nothing(*refs):
        pass

    return pl.pallas_call(
        nothing,
        in_specs=[ANY] * (1 + len(others)),
        out_specs=ANY,
        out_shape=jax.ShapeDtypeStruct(piece.shape, piece.dtype),
        input_output_aliases={0: 0},
    )(piece, *others)


def scores_kernel(
    source_ref, block_start_ref, place_ref, *refs, subject, away, pieces, slab, granule, block_rows, chips, duration
):
    count = source_ref.shape[0]
    bodies, tails = refs[:pieces], refs[pieces : 2 * pieces]
    same_ref, other_ref, ordered, own_rows, products_a, products_b, place_of, sem = refs[-8:]
    half_rows = slab // 2
    body = duration // LANES * LANES
    tail = duration - body
    for a in range(block_start_ref.shape[0]):
        place_of[block_start_ref[a] // block_rows] = a

    for slot in range(count):
        for half in range(2):
            piece = 2 * slot + half
            first = source_ref[slot] * slab + half * half_rows

            def start(g, _, piece=piece, first=first):
                stored = first + g * granule
                block = stored // block_rows
                row = place_of[block] * block_rows + (stored - block * block_rows)
                here = pl.ds(pl.multiple_of(g * granule, granule), granule)
                there = pl.ds(pl.multiple_of(row, granule), granule)
                if subject == 0:
                    pltpu.make_async_copy(tails[piece].at[here], ordered.at[there], sem).start()
                else:
                    pltpu.make_async_copy(bodies[piece].at[here], ordered.at[there, :body], sem).start()
                    pltpu.make_async_copy(tails[piece].at[here, body:], ordered.at[there, body:], sem).start()
                return 0

            lax.fori_loop(0, half_rows // granule, start, 0)
    pltpu.make_async_copy(ordered, ordered, sem).wait()

    position, subj = place_ref[0], place_ref[1]
    chip, core = subj // 2, subj % 2
    rows = pl.ds(pl.multiple_of(position * slab, granule), slab)
    own_rows[:, :body] = ordered[rows, :body]
    lane = lax.broadcasted_iota(jnp.int32, (slab, LANES), 1)
    kept = (lane >= subject * tail) & (lane < (subject + 1) * tail)
    own_rows[:, body:] = jnp.where(kept, ordered[rows, body:].astype(jnp.float32), 0.0).astype(jnp.bfloat16)

    limit = clip_limit * duration
    chunk = same_ref.shape[1]
    width = math.gcd(chunk, 256)
    tiles = []
    for flip, out_ref in ((1, other_ref), (0, same_ref)):
        owner = (chip + away) % chips * 2 + (core + flip) % 2
        tiles += [(owner * chunk + k * width, k * width, out_ref) for k in range(chunk // width)]
    buffers = (products_a, products_b)

    def multiply(i):
        columns = ordered[pl.ds(pl.multiple_of(tiles[i][0], width), width)]
        buffers[i % 2][...] = lax.dot_general(
            own_rows[...], columns, (((1,), (1,)), ((), ())), preferred_element_type=jnp.float32
        )

    def score(i):
        products = jnp.clip(buffers[i % 2][...], -limit, limit)
        fisher = 0.5 * (jnp.log(duration + products) - jnp.log(duration - products))
        tiles[i][2][:, pl.ds(tiles[i][1], width)] = fisher.astype(jnp.bfloat16)

    multiply(0)
    for i in range(1, len(tiles)):
        multiply(i)
        score(i - 1)
    score(len(tiles) - 1)


def scores(source, block_start, place, subject, away, bodies, tails, slab, window, chips, duration, late=()):
    block_rows = window // block_start.shape[0]
    granule = math.gcd(slab // 2, block_rows)
    chunk = window // (2 * chips)
    width = math.gcd(chunk, 256)
    padded = tails[0].shape[1]
    out = jax.ShapeDtypeStruct((slab, chunk), jnp.bfloat16)
    smem = pl.BlockSpec(memory_space=pltpu.SMEM)
    return pl.pallas_call(
        functools.partial(
            scores_kernel,
            subject=subject,
            away=away,
            pieces=len(tails),
            slab=slab,
            granule=granule,
            block_rows=block_rows,
            chips=chips,
            duration=duration,
        ),
        in_specs=[smem, smem, smem] + [ANY] * (2 * len(tails) + len(late)),
        out_shape=[out, out],
        scratch_shapes=[
            pltpu.VMEM((window, padded), jnp.bfloat16),
            pltpu.VMEM((slab, padded), jnp.bfloat16),
            pltpu.VMEM((slab, width), jnp.float32),
            pltpu.VMEM((slab, width), jnp.float32),
            pltpu.SMEM((block_start.shape[0],), jnp.int32),
            pltpu.SemaphoreType.DMA,
        ],
        compiler_params=pltpu.CompilerParams(vmem_limit_bytes=48 * 2**20),
        cost_estimate=pl.CostEstimate(
            flops=4 * slab * chunk * padded,
            bytes_accessed=2 * window * padded + 4 * slab * chunk,
            transcendentals=4 * slab * chunk,
        ),
    )(source, block_start, place, *bodies, *tails, *late)


def on_device(series, block_start):
    local_subjects, slab, duration = series.shape
    rows, cols = lax.axis_size("row"), lax.axis_size("col")
    count = rows * cols
    window = count * slab
    subjs = lax.axis_size("subj")
    chips = subjs // 2
    half_rows = slab // 2
    order = cycle(rows, cols)
    onward = [(order[i], order[(i + 1) % count]) for i in range(count)]
    backward = [(b, a) for a, b in onward]
    reach = count // 2
    offsets = [0]
    for d in range(1, reach):
        offsets += [d, -d]
    offsets.append(reach)
    table = np.zeros((count, count), np.int32)
    for i, device in enumerate(order):
        table[device] = [order[(i - d) % count] for d in offsets]
    position = lax.axis_index(SLABS)
    source = jnp.asarray(table)[position]
    place = jnp.stack([position, lax.axis_index("subj")]).astype(jnp.int32)

    def gather(own):
        got = [own]
        ahead, behind = list(own), list(own)
        for _ in range(1, reach):
            ahead = [lax.ppermute(piece, SLABS, onward) for piece in ahead]
            behind = [lax.ppermute(piece, SLABS, backward) for piece in behind]
            got += [ahead, behind]
        got.append([lax.ppermute(ahead[0], SLABS, onward), lax.ppermute(behind[1], SLABS, backward)])
        return got

    def flat(pairs):
        return [piece for pair in pairs for piece in pair]

    swap = [(s, s ^ 1) for s in range(subjs)]
    normed = [normalize(series, half, half_rows) for half in range(2)]
    gathered = []
    for a in range(local_subjects):
        own = [normed[half][a] for half in range(2)]
        if a:
            before = gathered[-1]
            own = [after(own[half], before[-3][half], before[-2][half]) for half in range(2)]
        gathered.append(gather(own))

    terms = []
    for a in range(local_subjects):
        last = a == local_subjects - 1
        for n, d in enumerate([*range(1, chips), 0]):
            late = () if last else gathered[a + 1][min(2 * n + 1, len(gathered[a + 1]) - 1)][:1]
            same, other = scores(
                source, block_start, place, a, d, flat(gathered[a]), flat(gathered[0]), slab, window, chips, duration, late
            )
            crossed = lax.ppermute(other, "subj", swap)
            part = same.astype(jnp.float32) + crossed.astype(jnp.float32)
            if d:
                part = part.astype(jnp.bfloat16) if last else part
                part = lax.ppermute(part, "subj", [(s, (s + 2 * d) % subjs) for s in range(subjs)])
                part = part.astype(jnp.float32)
            terms.append(part)
    return sum(terms[1:], terms[0]) / (local_subjects * subjs)


def solution(mesh):
    return jax.shard_map(
        on_device,
        mesh=mesh,
        in_specs=(P("subj", SLABS, None), P()),
        out_specs=P(SLABS, "subj"),
        check_vma=False,
    )
```

```python
import functools
import math

import jax
import jax.numpy as jnp
import numpy as np
from jax import lax
from jax.experimental import pallas as pl
from jax.experimental.pallas import tpu as pltpu
from jax.sharding import PartitionSpec as P

clip_limit = 0.99
epsilon = 1e-05
SLABS = ("row", "col")
LANES = 128
HINT = pl.CostEstimate(flops=1024, bytes_accessed=1024, transcendentals=0)
ANY = pl.BlockSpec(memory_space=pl.ANY)


def cycle(rows, cols):
    if cols == 1:
        return list(range(rows))
    walk = [(r, 0) for r in range(rows)]
    for i, r in enumerate(reversed(range(rows))):
        back = list(range(1, cols))
        walk += [(r, c) for c in (back if i % 2 == 0 else back[::-1])]
    return [r * cols + c for r, c in walk]


def normalize_kernel(series_ref, first_ref, *refs, begin, lead):
    other_refs, (raw, columns, sems) = refs[:-3], refs[-3:]
    subjects, duration, lanes = raw.shape
    body = duration // LANES * LANES
    tail = duration - body
    rows = first_ref.shape[0]
    width = LANES if lanes % LANES == 0 else lanes
    steps = lanes // width

    def copy(i):
        a, here = i % subjects, pl.ds(i // subjects * width, width)
        there = pl.ds(begin + i // subjects * width, width)
        return pltpu.make_async_copy(series_ref.at[a, :, there], raw.at[a, :, here], sems.at[i])

    for i in range(subjects * steps):
        copy(i).start()
    columns[:, duration + (subjects - 1) * tail :] = jnp.zeros(
        (subjects, LANES - subjects * tail, width), jnp.float32
    )
    for n in range(steps):
        here = pl.ds(n * width, width)
        for a in range(subjects):
            copy(n * subjects + a).wait()
            values = raw[a, :, here]
            center = jnp.mean(values, axis=0, keepdims=True)
            away = values - center
            spread = jnp.mean(away * away, axis=0, keepdims=True)
            normed = away * lax.rsqrt(spread + epsilon)
            columns[a, :duration] = normed
            if a:
                columns[0, duration + (a - 1) * tail : duration + a * tail] = normed[body:]
        kept = min(width, rows - n * width)
        for a, out_ref in enumerate((first_ref, *other_refs)):
            out = columns[a, : out_ref.shape[1]].astype(jnp.bfloat16).T
            out_ref[pl.ds(n * width, kept)] = out[lead : lead + kept]


def normalize(series, begin, end):
    subjects, duration, slab = series.shape
    body = duration // LANES * LANES
    low, high = begin // LANES * LANES, min(-(-end // LANES) * LANES, slab)
    lanes = high - low
    width = LANES if lanes % LANES == 0 else lanes
    widths = [body + LANES] + [body] * (subjects - 1)
    return pl.pallas_call(
        functools.partial(normalize_kernel, begin=low, lead=begin - low),
        in_specs=[pl.BlockSpec(memory_space=pltpu.HBM)],
        out_shape=[jax.ShapeDtypeStruct((end - begin, w), jnp.bfloat16) for w in widths],
        scratch_shapes=[
            pltpu.VMEM((subjects, duration, lanes), jnp.float32),
            pltpu.VMEM((subjects, body + LANES, width), jnp.float32),
            pltpu.SemaphoreType.DMA((subjects * (lanes // width),)),
        ],
        compiler_params=pltpu.CompilerParams(vmem_limit_bytes=48 * 2**20),
        cost_estimate=HINT,
    )(series)


def after(piece, *others):
    def nothing(*refs):
        pass

    return pl.pallas_call(
        nothing,
        in_specs=[ANY] * (1 + len(others)),
        out_specs=ANY,
        out_shape=jax.ShapeDtypeStruct(piece.shape, piece.dtype),
        input_output_aliases={0: 0},
        cost_estimate=HINT,
    )(piece, *others)


def scores_kernel(
    source_ref, block_start_ref, place_ref, *refs, subject, away, cuts, slab, granule, block_rows, chips, duration
):
    count = source_ref.shape[0]
    bodies, tails = refs[: 2 * count], refs[2 * count : 4 * count]
    same_ref, other_ref, ordered, own_rows, products_a, products_b, place_of, sem = refs[-8:]
    body = duration // LANES * LANES
    tail = duration - body
    for a in range(block_start_ref.shape[0]):
        place_of[block_start_ref[a] // block_rows] = a

    for slot in range(count):
        for half in range(2):
            piece = 2 * slot + half
            first = source_ref[slot] * slab + cuts[half]

            def start(g, _, piece=piece, first=first):
                stored = first + g * granule
                block = stored // block_rows
                row = place_of[block] * block_rows + (stored - block * block_rows)
                here = pl.ds(pl.multiple_of(g * granule, granule), granule)
                there = pl.ds(pl.multiple_of(row, granule), granule)
                if subject == 0:
                    pltpu.make_async_copy(tails[piece].at[here], ordered.at[there], sem).start()
                else:
                    pltpu.make_async_copy(bodies[piece].at[here], ordered.at[there, :body], sem).start()
                    pltpu.make_async_copy(tails[piece].at[here, body:], ordered.at[there, body:], sem).start()
                return 0

            lax.fori_loop(0, (cuts[half + 1] - cuts[half]) // granule, start, 0)
    pltpu.make_async_copy(ordered, ordered, sem).wait()

    position, subj = place_ref[0], place_ref[1]
    chip, core = subj // 2, subj % 2
    rows = pl.ds(pl.multiple_of(position * slab, granule), slab)
    own_rows[:, :body] = ordered[rows, :body]
    lane = lax.broadcasted_iota(jnp.int32, (slab, LANES), 1)
    kept = (lane >= subject * tail) & (lane < (subject + 1) * tail)
    own_rows[:, body:] = jnp.where(kept, ordered[rows, body:].astype(jnp.float32), 0.0).astype(jnp.bfloat16)

    limit = clip_limit * duration
    chunk = same_ref.shape[1]
    width = math.gcd(chunk, 256)
    tiles = []
    for flip, out_ref in ((1, other_ref), (0, same_ref)):
        owner = (chip + away) % chips * 2 + (core + flip) % 2
        tiles += [(owner * chunk + k * width, k * width, out_ref) for k in range(chunk // width)]
    buffers = (products_a, products_b)

    def multiply(i):
        columns = ordered[pl.ds(pl.multiple_of(tiles[i][0], width), width)]
        buffers[i % 2][...] = lax.dot_general(
            own_rows[...], columns, (((1,), (1,)), ((), ())), preferred_element_type=jnp.float32
        )

    def score(i):
        products = jnp.clip(buffers[i % 2][...], -limit, limit)
        fisher = 0.5 * (jnp.log(duration + products) - jnp.log(duration - products))
        tiles[i][2][:, pl.ds(tiles[i][1], width)] = fisher.astype(jnp.bfloat16)

    multiply(0)
    for i in range(1, len(tiles)):
        multiply(i)
        score(i - 1)
    score(len(tiles) - 1)


def scores(source, block_start, place, subject, away, bodies, tails, cuts, window, chips, duration, late=()):
    slab = cuts[-1]
    block_rows = window // block_start.shape[0]
    granule = math.gcd(*cuts, block_rows)
    chunk = window // (2 * chips)
    width = math.gcd(chunk, 256)
    padded = tails[0].shape[1]
    out = jax.ShapeDtypeStruct((slab, chunk), jnp.bfloat16)
    smem = pl.BlockSpec(memory_space=pltpu.SMEM)
    return pl.pallas_call(
        functools.partial(
            scores_kernel,
            subject=subject,
            away=away,
            cuts=cuts,
            slab=slab,
            granule=granule,
            block_rows=block_rows,
            chips=chips,
            duration=duration,
        ),
        in_specs=[smem, smem, smem] + [ANY] * (2 * len(tails) + len(late)),
        out_shape=[out, out],
        scratch_shapes=[
            pltpu.VMEM((window, padded), jnp.bfloat16),
            pltpu.VMEM((slab, padded), jnp.bfloat16),
            pltpu.VMEM((slab, width), jnp.float32),
            pltpu.VMEM((slab, width), jnp.float32),
            pltpu.SMEM((block_start.shape[0],), jnp.int32),
            pltpu.SemaphoreType.DMA,
        ],
        compiler_params=pltpu.CompilerParams(vmem_limit_bytes=48 * 2**20),
        cost_estimate=HINT,
    )(source, block_start, place, *bodies, *tails, *late)


def on_device(series, block_start):
    local_subjects, slab, duration = series.shape
    rows, cols = lax.axis_size("row"), lax.axis_size("col")
    count = rows * cols
    window = count * slab
    subjs = lax.axis_size("subj")
    chips = subjs // 2
    half = -(-slab // (2 * LANES)) * LANES if slab % LANES == 0 and slab > LANES else slab // 2
    cuts = (0, half, slab)
    order = cycle(rows, cols)
    onward = [(order[i], order[(i + 1) % count]) for i in range(count)]
    backward = [(b, a) for a, b in onward]
    reach = count // 2
    offsets = [0]
    for d in range(1, reach):
        offsets += [d, -d]
    offsets.append(reach)
    table = np.zeros((count, count), np.int32)
    for i, device in enumerate(order):
        table[device] = [order[(i - d) % count] for d in offsets]
    position = lax.axis_index(SLABS)
    source = jnp.asarray(table)[position]
    place = jnp.stack([position, lax.axis_index("subj")]).astype(jnp.int32)

    def gather(a, gate=None):
        got = [[normed[0][a], normed[1][a]]]
        for d in range(1, reach):
            ahead, behind = got[max(2 * d - 3, 0)], got[max(2 * d - 2, 0)]
            got += [[None, None], [None, None]]
            for half in range(2):
                waits = gate(d, half, got) if gate else ()
                if waits:
                    ahead[half] = after(ahead[half], *waits)
                    if behind is not ahead:
                        behind[half] = after(behind[half], *waits)
                got[-2][half] = lax.ppermute(ahead[half], SLABS, onward)
                got[-1][half] = lax.ppermute(behind[half], SLABS, backward)
        last = [None, None]
        for half in range(2):
            side, way = (-2, onward) if half == a % 2 else (-1, backward)
            last[half] = lax.ppermute(got[side][half], SLABS, way)
        got.append(last)
        return got

    def flat(pairs):
        return [piece for pair in pairs for piece in pair]

    swap = [(s, s ^ 1) for s in range(subjs)]
    columns = jnp.swapaxes(series, 1, 2)
    normed = [normalize(columns, cuts[half], cuts[half + 1]) for half in range(2)]
    everything = [gather(0)]
    terms, sums = [], []
    aways = [*range(1, chips), 0]

    def share(a, d, late=()):
        last = a == local_subjects - 1
        same, other = scores(
            source, block_start, place, a, d, flat(everything[a]), flat(everything[0]), cuts, window, chips, duration, late
        )
        crossed = lax.ppermute(other, "subj", swap)
        part = same.astype(jnp.float32) + crossed.astype(jnp.float32)
        if d:
            part = part.astype(jnp.bfloat16) if last else part
            sums.append(part)
            part = lax.ppermute(part, "subj", [(s, (s + 2 * d) % subjs) for s in range(subjs)])
            part = part.astype(jnp.float32)
        terms.append(part)
        return other

    for a in range(1, local_subjects):

        def gate(d, half, got, a=a, before=everything[-1]):
            if d == 1:
                return [before[-3][half], before[-2][half]]
            if half == 0:
                return sums[-1:] if d == 3 else ()
            if d - 2 < chips:
                return [share(a - 1, aways[d - 2], [got[2 * d - 3][0], got[2 * d - 2][0]])]
            return ()

        everything.append(gather(a, gate))
    for n, d in enumerate(aways):
        share(local_subjects - 1, d, terms[:1] if n == 0 else ())
    return sum(terms[1:], terms[0]) / (local_subjects * subjs)


def solution(mesh):
    return jax.shard_map(
        on_device,
        mesh=mesh,
        in_specs=(P("subj", SLABS, None), P()),
        out_specs=P(SLABS, "subj"),
        check_vma=False,
    )
```

```python
import functools
import math

import jax
import jax.numpy as jnp
import numpy as np
from jax import lax
from jax.experimental import pallas as pl
from jax.experimental.pallas import tpu as pltpu
from jax.sharding import PartitionSpec as P

clip_limit = 0.99
epsilon = 1e-05
SLABS = ("row", "col")
LANES = 128
AFTER = 36 * 2**20
ANY = pl.BlockSpec(memory_space=pl.ANY)


def cycle(rows, cols):
    if cols == 1:
        return list(range(rows))
    walk = [(r, 0) for r in range(rows)]
    for i, r in enumerate(reversed(range(rows))):
        back = list(range(1, cols))
        walk += [(r, c) for c in (back if i % 2 == 0 else back[::-1])]
    return [r * cols + c for r, c in walk]


def normalize_kernel(series_ref, first_ref, *refs, begin, lead):
    other_refs, (raw, columns, sems) = refs[:-3], refs[-3:]
    subjects, duration, lanes = raw.shape
    body = duration // LANES * LANES
    tail = duration - body
    rows = first_ref.shape[0]
    width = LANES if lanes % LANES == 0 else lanes
    steps = lanes // width

    def copy(i):
        a, here = i % subjects, pl.ds(i // subjects * width, width)
        there = pl.ds(begin + i // subjects * width, width)
        return pltpu.make_async_copy(series_ref.at[a, :, there], raw.at[a, :, here], sems.at[i])

    for i in range(subjects * steps):
        copy(i).start()
    columns[:, duration + (subjects - 1) * tail :] = jnp.zeros(
        (subjects, LANES - subjects * tail, width), jnp.float32
    )
    for n in range(steps):
        here = pl.ds(n * width, width)
        for a in range(subjects):
            copy(n * subjects + a).wait()
            values = raw[a, :, here]
            center = jnp.mean(values, axis=0, keepdims=True)
            away = values - center
            spread = jnp.mean(away * away, axis=0, keepdims=True)
            normed = away * lax.rsqrt(spread + epsilon)
            columns[a, :duration] = normed
            if a:
                columns[0, duration + (a - 1) * tail : duration + a * tail] = normed[body:]
        low, high = max(n * width, lead), min((n + 1) * width, lead + rows)
        for a, out_ref in enumerate((first_ref, *other_refs)):
            out = columns[a, : out_ref.shape[1]].astype(jnp.bfloat16).T
            out_ref[low - lead : high - lead] = out[low - n * width : high - n * width]


def normalize(series, begin, end):
    subjects, duration, slab = series.shape
    body = duration // LANES * LANES
    low, high = begin // LANES * LANES, min(-(-end // LANES) * LANES, slab)
    lanes = high - low
    width = LANES if lanes % LANES == 0 else lanes
    widths = [body + LANES] + [body] * (subjects - 1)
    return pl.pallas_call(
        functools.partial(normalize_kernel, begin=low, lead=begin - low),
        in_specs=[pl.BlockSpec(memory_space=pltpu.HBM)],
        out_shape=[jax.ShapeDtypeStruct((end - begin, w), jnp.bfloat16) for w in widths],
        scratch_shapes=[
            pltpu.VMEM((subjects, duration, lanes), jnp.float32),
            pltpu.VMEM((subjects, body + LANES, width), jnp.float32),
            pltpu.SemaphoreType.DMA((subjects * (lanes // width),)),
        ],
        compiler_params=pltpu.CompilerParams(vmem_limit_bytes=48 * 2**20),
        cost_estimate=pl.CostEstimate(
            flops=0, bytes_accessed=6 * subjects * duration * (end - begin), transcendentals=0
        ),
    )(series)


def after(pieces, others):
    def nothing(*refs):
        pass

    return pl.pallas_call(
        nothing,
        in_specs=[ANY] * (len(pieces) + len(others)),
        out_specs=[ANY] * len(pieces),
        out_shape=[jax.ShapeDtypeStruct(piece.shape, piece.dtype) for piece in pieces],
        input_output_aliases={i: i for i in range(len(pieces))},
        cost_estimate=pl.CostEstimate(flops=0, bytes_accessed=AFTER, transcendentals=0),
    )(*pieces, *others)


def finish_kernel(total_ref, *refs, scale):
    *last_refs, out_ref = refs
    first = 0
    for last_ref in last_refs:
        here = pl.ds(first, last_ref.shape[1])
        out_ref[:, here] = (total_ref[:, here] + last_ref[...].astype(jnp.float32)) * scale
        first += last_ref.shape[1]


def finish(total, lasts, scale):
    slab, chunk = total.shape
    step = math.gcd(slab, 128)
    return pl.pallas_call(
        functools.partial(finish_kernel, scale=scale),
        grid=(slab // step,),
        in_specs=[pl.BlockSpec((step, piece.shape[1]), lambda i: (i, 0)) for piece in (total, *lasts)],
        out_specs=pl.BlockSpec((step, chunk), lambda i: (i, 0)),
        out_shape=jax.ShapeDtypeStruct(total.shape, jnp.float32),
    )(total, *lasts)


def scores_kernel(
    source_ref, block_start_ref, place_ref, *refs, subject, away, part, cuts, slab, granule, block_rows, chips, chunk, duration
):
    count = source_ref.shape[0]
    bodies, tails = refs[: 2 * count], refs[2 * count : 4 * count]
    same_ref, other_ref, ordered, own_rows, products_a, products_b, place_of, sem = refs[-8:]
    body = duration // LANES * LANES
    tail = duration - body
    for a in range(block_start_ref.shape[0]):
        place_of[block_start_ref[a] // block_rows] = a

    for slot in range(count):
        for half in range(2):
            piece = 2 * slot + half
            first = source_ref[slot] * slab + cuts[half]

            def start(g, _, piece=piece, first=first):
                stored = first + g * granule
                block = stored // block_rows
                row = place_of[block] * block_rows + (stored - block * block_rows)
                here = pl.ds(pl.multiple_of(g * granule, granule), granule)
                there = pl.ds(pl.multiple_of(row, granule), granule)
                if subject == 0:
                    pltpu.make_async_copy(tails[piece].at[here], ordered.at[there], sem).start()
                else:
                    pltpu.make_async_copy(bodies[piece].at[here], ordered.at[there, :body], sem).start()
                    pltpu.make_async_copy(tails[piece].at[here, body:], ordered.at[there, body:], sem).start()
                return 0

            lax.fori_loop(0, (cuts[half + 1] - cuts[half]) // granule, start, 0)
    pltpu.make_async_copy(ordered, ordered, sem).wait()

    position, subj = place_ref[0], place_ref[1]
    chip, core = subj // 2, subj % 2
    rows = pl.ds(pl.multiple_of(position * slab, granule), slab)
    own_rows[:, :body] = ordered[rows, :body]
    lane = lax.broadcasted_iota(jnp.int32, (slab, LANES), 1)
    kept = (lane >= subject * tail) & (lane < (subject + 1) * tail)
    own_rows[:, body:] = jnp.where(kept, ordered[rows, body:].astype(jnp.float32), 0.0).astype(jnp.bfloat16)

    limit = clip_limit * duration
    width = math.gcd(chunk, 256)
    first, columns = part
    tiles = []
    for flip, out_ref in ((1, other_ref), (0, same_ref)):
        owner = (chip + away) % chips * 2 + (core + flip) % 2
        tiles += [(owner * chunk + first + k, k, out_ref) for k in range(0, columns, width)]
    buffers = (products_a, products_b)

    def multiply(i):
        columns = ordered[pl.ds(pl.multiple_of(tiles[i][0], width), width)]
        buffers[i % 2][...] = lax.dot_general(
            own_rows[...], columns, (((1,), (1,)), ((), ())), preferred_element_type=jnp.float32
        )

    def score(i):
        products = jnp.clip(buffers[i % 2][...], -limit, limit)
        fisher = 0.5 * (jnp.log(duration + products) - jnp.log(duration - products))
        tiles[i][2][:, pl.ds(tiles[i][1], width)] = fisher.astype(jnp.bfloat16)

    multiply(0)
    for i in range(1, len(tiles)):
        multiply(i)
        score(i - 1)
    score(len(tiles) - 1)


def scores(source, block_start, place, subject, away, part, bodies, tails, cuts, window, chips, duration, late=()):
    slab = cuts[-1]
    block_rows = window // block_start.shape[0]
    granule = math.gcd(*cuts, block_rows)
    chunk = window // (2 * chips)
    width = math.gcd(chunk, 256)
    padded = tails[0].shape[1]
    columns = part[1]
    out = jax.ShapeDtypeStruct((slab, columns), jnp.bfloat16)
    smem = pl.BlockSpec(memory_space=pltpu.SMEM)
    return pl.pallas_call(
        functools.partial(
            scores_kernel,
            subject=subject,
            away=away,
            part=part,
            cuts=cuts,
            slab=slab,
            granule=granule,
            block_rows=block_rows,
            chips=chips,
            chunk=chunk,
            duration=duration,
        ),
        in_specs=[smem, smem, smem] + [ANY] * (2 * len(tails) + len(late)),
        out_shape=[out, out],
        scratch_shapes=[
            pltpu.VMEM((window, padded), jnp.bfloat16),
            pltpu.VMEM((slab, padded), jnp.bfloat16),
            pltpu.VMEM((slab, width), jnp.float32),
            pltpu.VMEM((slab, width), jnp.float32),
            pltpu.SMEM((block_start.shape[0],), jnp.int32),
            pltpu.SemaphoreType.DMA,
        ],
        compiler_params=pltpu.CompilerParams(vmem_limit_bytes=48 * 2**20),
        cost_estimate=pl.CostEstimate(
            flops=4 * slab * columns * padded,
            bytes_accessed=2 * window * padded + 4 * slab * columns,
            transcendentals=4 * slab * columns,
        ),
    )(source, block_start, place, *bodies, *tails, *late)


def on_device(series, block_start):
    local_subjects, slab, duration = series.shape
    rows, cols = lax.axis_size("row"), lax.axis_size("col")
    count = rows * cols
    window = count * slab
    subjs = lax.axis_size("subj")
    chips = subjs // 2
    cuts = (0, slab // 2, slab)
    order = cycle(rows, cols)
    onward = [(order[i], order[(i + 1) % count]) for i in range(count)]
    backward = [(b, a) for a, b in onward]
    reach = count // 2
    offsets = [0]
    for d in range(1, reach):
        offsets += [d, -d]
    offsets.append(reach)
    table = np.zeros((count, count), np.int32)
    for i, device in enumerate(order):
        table[device] = [order[(i - d) % count] for d in offsets]
    position = lax.axis_index(SLABS)
    source = jnp.asarray(table)[position]
    place = jnp.stack([position, lax.axis_index("subj")]).astype(jnp.int32)

    def gather(a, gate=None):
        got = [[normed[0][a], normed[1][a]]]
        for d in range(1, reach):
            ahead, behind = got[max(2 * d - 3, 0)], got[max(2 * d - 2, 0)]
            got += [[None, None], [None, None]]
            for half in range(2):
                waits = gate(d, half, got) if gate else ()
                if d > 1:
                    ahead[half], behind[half] = after([ahead[half], behind[half]], waits)
                elif waits:
                    (ahead[half],) = after([ahead[half]], waits)
                got[-2][half] = lax.ppermute(ahead[half], SLABS, onward)
                got[-1][half] = lax.ppermute(behind[half], SLABS, backward)
        waits = gate(reach, 0, got) if gate else ()
        last = []
        for half, side, way in ((0, -2, onward), (1, -1, backward)):
            if waits:
                (got[side][half],) = after([got[side][half]], waits)
            last.append(lax.ppermute(got[side][half], SLABS, way))
        got.append(last)
        return got

    def flat(pairs):
        return [piece for pair in pairs for piece in pair]

    swap = [(s, s ^ 1) for s in range(subjs)]
    columns = jnp.swapaxes(series, 1, 2)
    normed = [normalize(columns, cuts[half], cuts[half + 1]) for half in range(2)]
    everything = [gather(0)]
    chunk = window // subjs
    width = math.gcd(chunk, 256)
    early = chunk // width // 2 * width
    aways = [*range(1, chips), 0]

    def share(a, d, part, late=(), hold=()):
        same, other = scores(
            source,
            block_start,
            place,
            a,
            d,
            part,
            flat(everything[a]),
            flat(everything[0]),
            cuts,
            window,
            chips,
            duration,
            late,
        )
        if hold:
            (other,) = after([other], hold)
        crossed = lax.ppermute(other, "subj", swap)
        summed = same.astype(jnp.float32) + crossed.astype(jnp.float32)
        if not d:
            return same, summed, d
        return same, summed.astype(jnp.bfloat16), d

    def send(summed, d):
        return lax.ppermute(summed, "subj", [(s, (s + 2 * d) % subjs) for s in range(subjs)])

    terms = []
    for a in range(1, local_subjects):
        shares = []

        def gate(d, half, got, a=a, before=everything[-1], shares=shares):
            if d == 1:
                return [before[-3][half], before[-2][half]]
            n = d - 2
            if half == 0 and n < chips:
                late = [*got[2 * n - 1], *got[2 * n]] if n else [got[1][0], got[2][0]]
                hold = () if n else [got[1][1], got[2][1]]
                shares.append(share(a - 1, aways[n], (0, chunk), late, hold=hold))
            waits = [shares[n][0]] if n < chips else []
            if (d, half) == (reach, 0):
                for _, summed, away in shares[:-1]:
                    (held,) = after([summed], [*got[3], *got[4]])
                    terms.append(send(held, away))
                waits += terms[-len(shares) + 1 :]
            return waits

        everything.append(gather(a, gate))
        terms.append(shares[-1][1])
    last = local_subjects - 1
    received, late = [], ()
    for d in aways[:-1]:
        parts = []
        for part in ((0, early), (early, chunk - early)):
            _, summed, _ = share(last, d, part, late)
            parts.append(send(summed, d))
            late = [summed]
        received.append(parts)
    late += [*terms[: chips - 1], received[-1][0]]
    terms.append(share(last, 0, (0, chunk), late)[1])
    terms += [jnp.concatenate(parts, axis=1).astype(jnp.float32) for parts in received[:-1]]
    total = lax.optimization_barrier(sum(term.astype(jnp.float32) for term in terms))
    return finish(total, received[-1], 1 / (local_subjects * subjs))


def solution(mesh):
    return jax.shard_map(
        on_device,
        mesh=mesh,
        in_specs=(P("subj", SLABS, None), P()),
        out_specs=P(SLABS, "subj"),
        check_vma=False,
    )
```

```python
import functools
import math

import jax
import jax.numpy as jnp
import numpy as np
from jax import lax
from jax.experimental import pallas as pl
from jax.experimental.pallas import tpu as pltpu
from jax.sharding import PartitionSpec as P

clip_limit = 0.99
epsilon = 1e-05
SLABS = ("row", "col")
LANES = 128
HINT = pl.CostEstimate(flops=0, bytes_accessed=1024, transcendentals=0)
SHORT = pl.CostEstimate(flops=0, bytes_accessed=2**25, transcendentals=0)
LONG = pl.CostEstimate(flops=0, bytes_accessed=2**27, transcendentals=0)
ANY = pl.BlockSpec(memory_space=pl.ANY)


def cycle(rows, cols):
    if cols == 1:
        return list(range(rows))
    walk = [(r, 0) for r in range(rows)]
    for i, r in enumerate(reversed(range(rows))):
        back = list(range(1, cols))
        walk += [(r, c) for c in (back if i % 2 == 0 else back[::-1])]
    return [r * cols + c for r, c in walk]


def normalize_kernel(series_ref, first_ref, *refs, begin, lead):
    other_refs, (raw, columns, sems) = refs[:-3], refs[-3:]
    subjects, duration, lanes = raw.shape
    body = duration // LANES * LANES
    tail = duration - body
    rows = first_ref.shape[0]
    width = LANES if lanes % LANES == 0 else lanes
    steps = lanes // width

    def copy(i):
        a, here = i % subjects, pl.ds(i // subjects * width, width)
        there = pl.ds(begin + i // subjects * width, width)
        return pltpu.make_async_copy(series_ref.at[a, :, there], raw.at[a, :, here], sems.at[i])

    for i in range(subjects * steps):
        copy(i).start()
    columns[:, duration + (subjects - 1) * tail :] = jnp.zeros(
        (subjects, LANES - subjects * tail, width), jnp.float32
    )
    for n in range(steps):
        here = pl.ds(n * width, width)
        for a in range(subjects):
            copy(n * subjects + a).wait()
            values = raw[a, :, here]
            center = jnp.mean(values, axis=0, keepdims=True)
            away = values - center
            spread = jnp.mean(away * away, axis=0, keepdims=True)
            normed = away * lax.rsqrt(spread + epsilon)
            columns[a, :duration] = normed
            if a:
                columns[0, duration + (a - 1) * tail : duration + a * tail] = normed[body:]
        low, high = max(n * width, lead), min((n + 1) * width, lead + rows)
        for a, out_ref in enumerate((first_ref, *other_refs)):
            out = columns[a, : out_ref.shape[1]].astype(jnp.bfloat16).T
            out_ref[low - lead : high - lead] = out[low - n * width : high - n * width]


def normalize(series, begin, end):
    subjects, duration, slab = series.shape
    body = duration // LANES * LANES
    low, high = begin // LANES * LANES, min(-(-end // LANES) * LANES, slab)
    lanes = high - low
    width = LANES if lanes % LANES == 0 else lanes
    widths = [body + LANES] + [body] * (subjects - 1)
    return pl.pallas_call(
        functools.partial(normalize_kernel, begin=low, lead=begin - low),
        in_specs=[pl.BlockSpec(memory_space=pltpu.HBM)],
        out_shape=[jax.ShapeDtypeStruct((end - begin, w), jnp.bfloat16) for w in widths],
        scratch_shapes=[
            pltpu.VMEM((subjects, duration, lanes), jnp.float32),
            pltpu.VMEM((subjects, body + LANES, width), jnp.float32),
            pltpu.SemaphoreType.DMA((subjects * (lanes // width),)),
        ],
        compiler_params=pltpu.CompilerParams(vmem_limit_bytes=48 * 2**20),
        cost_estimate=HINT,
    )(series)


def after(pieces, others, cost=HINT):
    def nothing(*refs):
        pass

    return pl.pallas_call(
        nothing,
        in_specs=[ANY] * (len(pieces) + len(others)),
        out_specs=[ANY] * len(pieces),
        out_shape=[jax.ShapeDtypeStruct(piece.shape, piece.dtype) for piece in pieces],
        input_output_aliases={i: i for i in range(len(pieces))},
        cost_estimate=cost,
    )(*pieces, *others)


def finish_kernel(total_ref, *refs, scale):
    *last_refs, out_ref = refs
    first = 0
    for last_ref in last_refs:
        here = pl.ds(first, last_ref.shape[1])
        out_ref[:, here] = (total_ref[:, here] + last_ref[...].astype(jnp.float32)) * scale
        first += last_ref.shape[1]


def finish(total, lasts, scale):
    slab, chunk = total.shape
    step = math.gcd(slab, 128)
    return pl.pallas_call(
        functools.partial(finish_kernel, scale=scale),
        grid=(slab // step,),
        in_specs=[pl.BlockSpec((step, piece.shape[1]), lambda i: (i, 0)) for piece in (total, *lasts)],
        out_specs=pl.BlockSpec((step, chunk), lambda i: (i, 0)),
        out_shape=jax.ShapeDtypeStruct(total.shape, jnp.float32),
    )(total, *lasts)


def scores_kernel(
    source_ref, block_start_ref, place_ref, *refs, subject, away, part, cuts, slab, granule, block_rows, chips, chunk, duration
):
    count = source_ref.shape[0]
    bodies, tails = refs[: 2 * count], refs[2 * count : 4 * count]
    same_ref, other_ref, ordered, own_rows, products_a, products_b, place_of, sem = refs[-8:]
    body = duration // LANES * LANES
    tail = duration - body
    for a in range(block_start_ref.shape[0]):
        place_of[block_start_ref[a] // block_rows] = a

    for slot in range(count):
        for half in range(2):
            piece = 2 * slot + half
            first = source_ref[slot] * slab + cuts[half]

            def start(g, _, piece=piece, first=first):
                stored = first + g * granule
                block = stored // block_rows
                row = place_of[block] * block_rows + (stored - block * block_rows)
                here = pl.ds(pl.multiple_of(g * granule, granule), granule)
                there = pl.ds(pl.multiple_of(row, granule), granule)
                if subject == 0:
                    pltpu.make_async_copy(tails[piece].at[here], ordered.at[there], sem).start()
                else:
                    pltpu.make_async_copy(bodies[piece].at[here], ordered.at[there, :body], sem).start()
                    pltpu.make_async_copy(tails[piece].at[here, body:], ordered.at[there, body:], sem).start()
                return 0

            lax.fori_loop(0, (cuts[half + 1] - cuts[half]) // granule, start, 0)
    pltpu.make_async_copy(ordered, ordered, sem).wait()

    position, subj = place_ref[0], place_ref[1]
    chip, core = subj // 2, subj % 2
    rows = pl.ds(pl.multiple_of(position * slab, granule), slab)
    own_rows[:, :body] = ordered[rows, :body]
    lane = lax.broadcasted_iota(jnp.int32, (slab, LANES), 1)
    kept = (lane >= subject * tail) & (lane < (subject + 1) * tail)
    own_rows[:, body:] = jnp.where(kept, ordered[rows, body:].astype(jnp.float32), 0.0).astype(jnp.bfloat16)

    limit = clip_limit * duration
    width = math.gcd(chunk, 256)
    first, columns = part
    tiles = []
    for flip, out_ref in ((1, other_ref), (0, same_ref)):
        owner = (chip + away) % chips * 2 + (core + flip) % 2
        tiles += [(owner * chunk + first + k, k, out_ref) for k in range(0, columns, width)]
    buffers = (products_a, products_b)

    def multiply(i):
        columns = ordered[pl.ds(pl.multiple_of(tiles[i][0], width), width)]
        buffers[i % 2][...] = lax.dot_general(
            own_rows[...], columns, (((1,), (1,)), ((), ())), preferred_element_type=jnp.float32
        )

    def score(i):
        products = jnp.clip(buffers[i % 2][...], -limit, limit)
        fisher = 0.5 * (jnp.log(duration + products) - jnp.log(duration - products))
        tiles[i][2][:, pl.ds(tiles[i][1], width)] = fisher.astype(jnp.bfloat16)

    multiply(0)
    for i in range(1, len(tiles)):
        multiply(i)
        score(i - 1)
    score(len(tiles) - 1)


def scores(source, block_start, place, subject, away, part, bodies, tails, cuts, window, chips, duration, late=()):
    slab = cuts[-1]
    block_rows = window // block_start.shape[0]
    granule = math.gcd(*cuts, block_rows)
    chunk = window // (2 * chips)
    width = math.gcd(chunk, 256)
    padded = tails[0].shape[1]
    columns = part[1]
    out = jax.ShapeDtypeStruct((slab, columns), jnp.bfloat16)
    smem = pl.BlockSpec(memory_space=pltpu.SMEM)
    return pl.pallas_call(
        functools.partial(
            scores_kernel,
            subject=subject,
            away=away,
            part=part,
            cuts=cuts,
            slab=slab,
            granule=granule,
            block_rows=block_rows,
            chips=chips,
            chunk=chunk,
            duration=duration,
        ),
        in_specs=[smem, smem, smem] + [ANY] * (2 * len(tails) + len(late)),
        out_shape=[out, out],
        scratch_shapes=[
            pltpu.VMEM((window, padded), jnp.bfloat16),
            pltpu.VMEM((slab, padded), jnp.bfloat16),
            pltpu.VMEM((slab, width), jnp.float32),
            pltpu.VMEM((slab, width), jnp.float32),
            pltpu.SMEM((block_start.shape[0],), jnp.int32),
            pltpu.SemaphoreType.DMA,
        ],
        compiler_params=pltpu.CompilerParams(vmem_limit_bytes=48 * 2**20),
        cost_estimate=HINT,
    )(source, block_start, place, *bodies, *tails, *late)


def on_device(series, block_start):
    local_subjects, slab, duration = series.shape
    rows, cols = lax.axis_size("row"), lax.axis_size("col")
    count = rows * cols
    window = count * slab
    subjs = lax.axis_size("subj")
    chips = subjs // 2
    cuts = (0, slab // 2, slab)
    order = cycle(rows, cols)
    onward = [(order[i], order[(i + 1) % count]) for i in range(count)]
    backward = [(b, a) for a, b in onward]
    reach = count // 2
    offsets = [0]
    for d in range(1, reach):
        offsets += [d, -d]
    offsets.append(reach)
    table = np.zeros((count, count), np.int32)
    for i, device in enumerate(order):
        table[device] = [order[(i - d) % count] for d in offsets]
    position = lax.axis_index(SLABS)
    source = jnp.asarray(table)[position]
    place = jnp.stack([position, lax.axis_index("subj")]).astype(jnp.int32)

    def gather(a, gate=None):
        got = [[normed[0][a], normed[1][a]]]
        for d in range(1, reach):
            ahead, behind = got[max(2 * d - 3, 0)], got[max(2 * d - 2, 0)]
            got += [[None, None], [None, None]]
            for half in range(2):
                waits = gate(d, half, got) if gate else ()
                if d > 1:
                    ahead[half], behind[half] = after([ahead[half], behind[half]], waits)
                elif waits:
                    (ahead[half],) = after([ahead[half]], waits)
                got[-2][half] = lax.ppermute(ahead[half], SLABS, onward)
                got[-1][half] = lax.ppermute(behind[half], SLABS, backward)
        waits = gate(reach, 0, got) if gate else ()
        last = []
        for half, side, way in ((0, -2, onward), (1, -1, backward)):
            if waits:
                (got[side][half],) = after([got[side][half]], waits)
            last.append(lax.ppermute(got[side][half], SLABS, way))
        got.append(last)
        return got

    def flat(pairs):
        return [piece for pair in pairs for piece in pair]

    swap = [(s, s ^ 1) for s in range(subjs)]
    columns = jnp.swapaxes(series, 1, 2)
    normed = [normalize(columns, cuts[half], cuts[half + 1]) for half in range(2)]
    everything = [gather(0)]
    chunk = window // subjs
    width = math.gcd(chunk, 256)
    early = -(-chunk // width // 2) * width
    aways = [*range(1, chips), 0]

    def share(a, d, part, late=(), hold=()):
        same, other = scores(
            source,
            block_start,
            place,
            a,
            d,
            part,
            flat(everything[a]),
            flat(everything[0]),
            cuts,
            window,
            chips,
            duration,
            late,
        )
        if hold:
            (other,) = after([other], hold)
        crossed = lax.ppermute(other, "subj", swap)
        summed = same.astype(jnp.float32) + crossed.astype(jnp.float32)
        if not d:
            return same, summed, d
        return same, summed.astype(jnp.bfloat16) if a == local_subjects - 1 else summed, d

    def send(summed, d, cost):
        there = lax.ppermute(summed, "subj", [(s, (s + 2 * d) % subjs) for s in range(subjs)])
        return after([there], (), cost)[0]

    terms = []
    for a in range(1, local_subjects):
        shares = []

        def gate(d, half, got, a=a, before=everything[-1], shares=shares):
            if d == 1:
                return [before[-3][half], before[-2][half]]
            n = d - 2
            if half == 0 and n < chips:
                late = [*got[2 * n - 1], *got[2 * n]] if n else ()
                hold = () if n else [*got[1], *got[2]]
                shares.append(share(a - 1, aways[n], (0, chunk), late, hold))
            return [shares[n][0]] if n < chips else ()

        everything.append(gather(a, gate))
        terms += [send(summed, d, SHORT) if d else summed for _, summed, d in shares]
    last = local_subjects - 1
    received, late = [], terms[: chips - 1]
    for d in aways[:-1]:
        parts = []
        for part in ((0, early), (early, chunk - early)):
            _, summed, _ = share(last, d, part, late)
            parts.append(send(summed, d, LONG))
            late = [summed]
        received.append(parts)
    terms.append(share(last, 0, (0, chunk), late, received[-1][:1])[1])
    terms += [jnp.concatenate(parts, axis=1).astype(jnp.float32) for parts in received[:-1]]
    total = lax.optimization_barrier(sum(term.astype(jnp.float32) for term in terms))
    return finish(total, received[-1], 1 / (local_subjects * subjs))


def solution(mesh):
    return jax.shard_map(
        on_device,
        mesh=mesh,
        in_specs=(P("subj", SLABS, None), P()),
        out_specs=P(SLABS, "subj"),
        check_vma=False,
    )
```

```python
import functools
import math

import jax
import jax.numpy as jnp
import numpy as np
from jax import lax
from jax.experimental import pallas as pl
from jax.experimental.pallas import tpu as pltpu
from jax.sharding import PartitionSpec as P

clip_limit = 0.99
epsilon = 1e-05
SLABS = ("row", "col")
LANES = 128
HINT = pl.CostEstimate(flops=0, bytes_accessed=1024, transcendentals=0)
SHORT = pl.CostEstimate(flops=0, bytes_accessed=1024, transcendentals=0)
LONG = pl.CostEstimate(flops=0, bytes_accessed=2**27, transcendentals=0)
ANY = pl.BlockSpec(memory_space=pl.ANY)


def cycle(rows, cols):
    if cols == 1:
        return list(range(rows))
    walk = [(r, 0) for r in range(rows)]
    for i, r in enumerate(reversed(range(rows))):
        back = list(range(1, cols))
        walk += [(r, c) for c in (back if i % 2 == 0 else back[::-1])]
    return [r * cols + c for r, c in walk]


def normalize_kernel(series_ref, first_ref, *refs, begin, lead):
    other_refs, (raw, columns, sems) = refs[:-3], refs[-3:]
    subjects, duration, lanes = raw.shape
    body = duration // LANES * LANES
    tail = duration - body
    rows = first_ref.shape[0]
    width = LANES if lanes % LANES == 0 else lanes
    steps = lanes // width

    def copy(i):
        a, here = i % subjects, pl.ds(i // subjects * width, width)
        there = pl.ds(begin + i // subjects * width, width)
        return pltpu.make_async_copy(series_ref.at[a, :, there], raw.at[a, :, here], sems.at[i])

    for i in range(subjects * steps):
        copy(i).start()
    columns[:, duration + (subjects - 1) * tail :] = jnp.zeros(
        (subjects, LANES - subjects * tail, width), jnp.float32
    )
    for n in range(steps):
        here = pl.ds(n * width, width)
        for a in range(subjects):
            copy(n * subjects + a).wait()
            values = raw[a, :, here]
            center = jnp.mean(values, axis=0, keepdims=True)
            away = values - center
            spread = jnp.mean(away * away, axis=0, keepdims=True)
            normed = away * lax.rsqrt(spread + epsilon)
            columns[a, :duration] = normed
            if a:
                columns[0, duration + (a - 1) * tail : duration + a * tail] = normed[body:]
        low, high = max(n * width, lead), min((n + 1) * width, lead + rows)
        for a, out_ref in enumerate((first_ref, *other_refs)):
            out = columns[a, : out_ref.shape[1]].astype(jnp.bfloat16).T
            out_ref[low - lead : high - lead] = out[low - n * width : high - n * width]


def normalize(series, begin, end):
    subjects, duration, slab = series.shape
    body = duration // LANES * LANES
    low, high = begin // LANES * LANES, min(-(-end // LANES) * LANES, slab)
    lanes = high - low
    width = LANES if lanes % LANES == 0 else lanes
    widths = [body + LANES] + [body] * (subjects - 1)
    return pl.pallas_call(
        functools.partial(normalize_kernel, begin=low, lead=begin - low),
        in_specs=[pl.BlockSpec(memory_space=pltpu.HBM)],
        out_shape=[jax.ShapeDtypeStruct((end - begin, w), jnp.bfloat16) for w in widths],
        scratch_shapes=[
            pltpu.VMEM((subjects, duration, lanes), jnp.float32),
            pltpu.VMEM((subjects, body + LANES, width), jnp.float32),
            pltpu.SemaphoreType.DMA((subjects * (lanes // width),)),
        ],
        compiler_params=pltpu.CompilerParams(vmem_limit_bytes=48 * 2**20),
        cost_estimate=HINT,
    )(series)


def after(pieces, others, cost=HINT):
    def nothing(*refs):
        pass

    return pl.pallas_call(
        nothing,
        in_specs=[ANY] * (len(pieces) + len(others)),
        out_specs=[ANY] * len(pieces),
        out_shape=[jax.ShapeDtypeStruct(piece.shape, piece.dtype) for piece in pieces],
        input_output_aliases={i: i for i in range(len(pieces))},
        cost_estimate=cost,
    )(*pieces, *others)


def combine_kernel(*refs, starts, scale):
    *in_refs, out_ref = refs
    total = jnp.zeros(out_ref.shape, jnp.float32)
    for ref, start in zip(in_refs, starts):
        if start is None:
            total = total + ref[...].astype(jnp.float32)
    out_ref[...] = total * scale
    for ref, start in zip(in_refs, starts):
        if start is not None:
            here = pl.ds(start, ref.shape[1])
            out_ref[:, here] = out_ref[:, here] + ref[...].astype(jnp.float32) * scale


def combine(terms, starts, slab, columns, scale):
    step = max(d for d in range(16, 161, 16) if slab % d == 0)
    return pl.pallas_call(
        functools.partial(combine_kernel, starts=starts, scale=scale),
        grid=(slab // step,),
        in_specs=[pl.BlockSpec((step, term.shape[1]), lambda i: (i, 0)) for term in terms],
        out_specs=pl.BlockSpec((step, columns), lambda i: (i, 0)),
        out_shape=jax.ShapeDtypeStruct((slab, columns), jnp.float32),
        compiler_params=pltpu.CompilerParams(vmem_limit_bytes=48 * 2**20),
        cost_estimate=HINT,
    )(*terms)


def finish_kernel(part_ref, before_ref, out_ref, *, scale):
    out_ref[...] = before_ref[...] + part_ref[...].astype(jnp.float32) * scale


def finish(part, before, first, scale):
    slab = before.shape[0]
    width = math.gcd(part.shape[1], first)
    block = (slab // 2 if slab % 32 == 0 else slab, width)
    there = pl.BlockSpec(block, lambda i, j: (i, first // width + j))
    return pl.pallas_call(
        functools.partial(finish_kernel, scale=scale),
        grid=(slab // block[0], part.shape[1] // width),
        in_specs=[pl.BlockSpec(block, lambda i, j: (i, j)), there],
        out_specs=there,
        out_shape=jax.ShapeDtypeStruct(before.shape, jnp.float32),
        input_output_aliases={1: 0},
        cost_estimate=HINT,
    )(part, before)


def scores_kernel(
    source_ref, block_start_ref, place_ref, *refs, subject, away, part, cuts, slab, granule, block_rows, chips, chunk, duration
):
    count = source_ref.shape[0]
    bodies, tails = refs[: 2 * count], refs[2 * count : 4 * count]
    same_ref, other_ref, own_rows, other_columns, same_columns, products_a, products_b, place_of, sems = refs[-9:]
    body = duration // LANES * LANES
    tail = duration - body
    for a in range(block_start_ref.shape[0]):
        place_of[block_start_ref[a] // block_rows] = a

    position, subj = place_ref[0], place_ref[1]
    chip, core = subj // 2, subj % 2
    first, columns = part
    wanted = [(position * slab, own_rows)]
    for flip, columns_ref in ((1, other_columns), (0, same_columns)):
        owner = (chip + away) % chips * 2 + (core + flip) % 2
        wanted.append((owner * chunk + first, columns_ref))

    for slot in range(count):
        for half in range(2):
            piece = 2 * slot + half
            low = source_ref[slot] * slab + cuts[half]

            def start(g, _, piece=piece, low=low):
                stored = low + g * granule
                block = stored // block_rows
                row = place_of[block] * block_rows + (stored - block * block_rows)
                here = pl.ds(pl.multiple_of(g * granule, granule), granule)
                for n, (begin, to_ref) in enumerate(wanted):

                    @pl.when((row >= begin) & (row < begin + to_ref.shape[0]))
                    def _():
                        there = pl.ds(pl.multiple_of(row - begin, granule), granule)
                        if subject == 0:
                            pltpu.make_async_copy(tails[piece].at[here], to_ref.at[there], sems.at[n]).start()
                        else:
                            pltpu.make_async_copy(
                                bodies[piece].at[here], to_ref.at[there, :body], sems.at[n]
                            ).start()
                            pltpu.make_async_copy(
                                tails[piece].at[here, body:], to_ref.at[there, body:], sems.at[n]
                            ).start()

                return 0

            lax.fori_loop(0, (cuts[half + 1] - cuts[half]) // granule, start, 0)

    def arrived(n):
        to_ref = wanted[n][1]
        pltpu.make_async_copy(to_ref, to_ref, sems.at[n]).wait()

    arrived(0)
    lane = lax.broadcasted_iota(jnp.int32, (slab, LANES), 1)
    kept = (lane >= subject * tail) & (lane < (subject + 1) * tail)
    own_rows[:, body:] = jnp.where(kept, own_rows[:, body:].astype(jnp.float32), 0.0).astype(jnp.bfloat16)

    limit = clip_limit * duration
    width = math.gcd(columns, 256)
    tiles = []
    for n, out_ref in ((1, other_ref), (2, same_ref)):
        tiles += [(n, k, out_ref) for k in range(0, columns, width)]
    buffers = (products_a, products_b)

    def multiply(i):
        n, k, _ = tiles[i]
        if k == 0:
            arrived(n)
        buffers[i % 2][...] = lax.dot_general(
            own_rows[...], wanted[n][1][pl.ds(k, width)], (((1,), (1,)), ((), ())), preferred_element_type=jnp.float32
        )

    def score(i):
        products = jnp.clip(buffers[i % 2][...], -limit, limit)
        fisher = 0.5 * (jnp.log(duration + products) - jnp.log(duration - products))
        tiles[i][2][:, pl.ds(tiles[i][1], width)] = fisher.astype(jnp.bfloat16)

    multiply(0)
    for i in range(1, len(tiles)):
        multiply(i)
        score(i - 1)
    score(len(tiles) - 1)


def scores(source, block_start, place, subject, away, part, bodies, tails, cuts, window, chips, duration, late=()):
    slab = cuts[-1]
    block_rows = window // block_start.shape[0]
    granule = math.gcd(*cuts, *part, block_rows)
    chunk = window // (2 * chips)
    padded = tails[0].shape[1]
    columns = part[1]
    width = math.gcd(columns, 256)
    out = jax.ShapeDtypeStruct((slab, columns), jnp.bfloat16)
    smem = pl.BlockSpec(memory_space=pltpu.SMEM)
    return pl.pallas_call(
        functools.partial(
            scores_kernel,
            subject=subject,
            away=away,
            part=part,
            cuts=cuts,
            slab=slab,
            granule=granule,
            block_rows=block_rows,
            chips=chips,
            chunk=chunk,
            duration=duration,
        ),
        in_specs=[smem, smem, smem] + [ANY] * (2 * len(tails) + len(late)),
        out_shape=[out, out],
        scratch_shapes=[
            pltpu.VMEM((slab, padded), jnp.bfloat16),
            pltpu.VMEM((columns, padded), jnp.bfloat16),
            pltpu.VMEM((columns, padded), jnp.bfloat16),
            pltpu.VMEM((slab, width), jnp.float32),
            pltpu.VMEM((slab, width), jnp.float32),
            pltpu.SMEM((block_start.shape[0],), jnp.int32),
            pltpu.SemaphoreType.DMA((3,)),
        ],
        compiler_params=pltpu.CompilerParams(vmem_limit_bytes=48 * 2**20),
        cost_estimate=HINT,
    )(source, block_start, place, *bodies, *tails, *late)


def on_device(series, block_start):
    local_subjects, slab, duration = series.shape
    rows, cols = lax.axis_size("row"), lax.axis_size("col")
    count = rows * cols
    window = count * slab
    subjs = lax.axis_size("subj")
    chips = subjs // 2
    cuts = (0, slab // 2, slab)
    order = cycle(rows, cols)
    onward = [(order[i], order[(i + 1) % count]) for i in range(count)]
    backward = [(b, a) for a, b in onward]
    reach = count // 2
    offsets = [0]
    for d in range(1, reach):
        offsets += [d, -d]
    offsets.append(reach)
    table = np.zeros((count, count), np.int32)
    for i, device in enumerate(order):
        table[device] = [order[(i - d) % count] for d in offsets]
    position = lax.axis_index(SLABS)
    source = jnp.asarray(table)[position]
    place = jnp.stack([position, lax.axis_index("subj")]).astype(jnp.int32)

    def gather(a, gate=None):
        got = [[normed[0][a], normed[1][a]]]
        for d in range(1, reach):
            ahead, behind = got[max(2 * d - 3, 0)], got[max(2 * d - 2, 0)]
            got += [[None, None], [None, None]]
            for half in range(2):
                waits = gate(d, half, got) if gate else ()
                if d > 1:
                    ahead[half], behind[half] = after([ahead[half], behind[half]], waits)
                elif waits:
                    (ahead[half],) = after([ahead[half]], waits)
                got[-2][half] = lax.ppermute(ahead[half], SLABS, onward)
                got[-1][half] = lax.ppermute(behind[half], SLABS, backward)
        waits = gate(reach, 0, got) if gate else ()
        last = []
        for half, side, way in ((0, -2, onward), (1, -1, backward)):
            if waits:
                (got[side][half],) = after([got[side][half]], waits)
            last.append(lax.ppermute(got[side][half], SLABS, way))
        got.append(last)
        return got

    def flat(pairs):
        return [piece for pair in pairs for piece in pair]

    swap = [(s, s ^ 1) for s in range(subjs)]
    columns = jnp.swapaxes(series, 1, 2)
    normed = [normalize(columns, cuts[half], cuts[half + 1]) for half in range(2)]
    everything = [gather(0)]
    chunk = window // subjs
    width = math.gcd(chunk, 256)
    early = -(-chunk // width // 2) * width
    aways = [*range(1, chips), 0]

    def share(a, d, part, late=(), hold=()):
        same, other = scores(
            source,
            block_start,
            place,
            a,
            d,
            part,
            flat(everything[a]),
            flat(everything[0]),
            cuts,
            window,
            chips,
            duration,
            late,
        )
        if hold:
            (other,) = after([other], hold)
        crossed = lax.ppermute(other, "subj", swap)
        return same, crossed

    def send(summed, d, cost, before=()):
        there = lax.ppermute(summed, "subj", [(s, (s + 2 * d) % subjs) for s in range(subjs)])
        return after([there], before, cost)[0]

    def added(same, crossed):
        return (same.astype(jnp.float32) + crossed.astype(jnp.float32)).astype(jnp.bfloat16)

    terms, starts = [], []
    for a in range(1, local_subjects):
        shares = []

        def gate(d, half, got, a=a, before=everything[-1], shares=shares):
            if d == 1:
                return [before[-3][half], before[-2][half]]
            n = d - 2
            if half == 0 and n < chips:
                late = [*got[2 * n - 1], *got[2 * n]] if n else ()
                hold = () if n else [*got[1], *got[2]]
                shares.append(share(a - 1, aways[n], (0, chunk), late, hold))
            return [shares[n][0]] if n < chips else ()

        everything.append(gather(a, gate))
        for d, (same, crossed) in zip(aways[:-1], shares):
            terms.append(send(added(same, crossed), d, SHORT))
            starts.append(None)
        terms += shares[-1]
        starts += [None, None]
    last = local_subjects - 1
    scale = 1 / (local_subjects * subjs)
    cut = ((0, early), (early, chunk - early))
    late, received = terms[: chips - 1], []
    for d in aways[:-1]:
        shares = []
        for part in cut:
            shares.append(added(*share(last, d, part, late)))
            late = [shares[-1]]
        received.append(shares)
    for d, shares in zip(aways[:-2], received[:-1]):
        terms += [send(summed, d, LONG) for summed in shares]
        starts += [0, early]
    d = aways[-2]
    there = send(received[-1][0], d, LONG)
    terms += [*share(last, 0, (0, chunk), late, [there]), there]
    starts += [None, None, 0]
    out = combine(terms, starts, slab, chunk, scale)
    return finish(send(received[-1][1], d, LONG, [out]), out, early, scale)


def solution(mesh):
    return jax.shard_map(
        on_device,
        mesh=mesh,
        in_specs=(P("subj", SLABS, None), P()),
        out_specs=P(SLABS, "subj"),
        check_vma=False,
    )
```

```python
import functools
import math

import jax
import jax.numpy as jnp
import numpy as np
from jax import lax
from jax.experimental import pallas as pl
from jax.experimental.pallas import tpu as pltpu
from jax.sharding import PartitionSpec as P

clip_limit = 0.99
epsilon = 1e-05
SLABS = ("row", "col")
LANES = 128
HINT = pl.CostEstimate(flops=0, bytes_accessed=1024, transcendentals=0)
SHORT = pl.CostEstimate(flops=0, bytes_accessed=1024, transcendentals=0)
LONG = pl.CostEstimate(flops=0, bytes_accessed=2**27, transcendentals=0)
ANY = pl.BlockSpec(memory_space=pl.ANY)


def cycle(rows, cols):
    if cols == 1:
        return list(range(rows))
    walk = [(r, 0) for r in range(rows)]
    for i, r in enumerate(reversed(range(rows))):
        back = list(range(1, cols))
        walk += [(r, c) for c in (back if i % 2 == 0 else back[::-1])]
    return [r * cols + c for r, c in walk]


def normalize_kernel(series_ref, first_ref, *refs, begin, lead):
    other_refs, (raw, columns, sems) = refs[:-3], refs[-3:]
    subjects, duration, lanes = raw.shape
    body = duration // LANES * LANES
    tail = duration - body
    rows = first_ref.shape[0]
    width = LANES if lanes % LANES == 0 else lanes
    steps = lanes // width

    def copy(i):
        a, here = i % subjects, pl.ds(i // subjects * width, width)
        there = pl.ds(begin + i // subjects * width, width)
        return pltpu.make_async_copy(series_ref.at[a, :, there], raw.at[a, :, here], sems.at[i])

    for i in range(subjects * steps):
        copy(i).start()
    columns[:, duration + (subjects - 1) * tail :] = jnp.zeros(
        (subjects, LANES - subjects * tail, width), jnp.float32
    )
    for n in range(steps):
        here = pl.ds(n * width, width)
        for a in range(subjects):
            copy(n * subjects + a).wait()
            values = raw[a, :, here]
            center = jnp.mean(values, axis=0, keepdims=True)
            away = values - center
            spread = jnp.mean(away * away, axis=0, keepdims=True)
            normed = away * lax.rsqrt(spread + epsilon)
            columns[a, :duration] = normed
            if a:
                columns[0, duration + (a - 1) * tail : duration + a * tail] = normed[body:]
        low, high = max(n * width, lead), min((n + 1) * width, lead + rows)
        for a, out_ref in enumerate((first_ref, *other_refs)):
            out = columns[a, : out_ref.shape[1]].astype(jnp.bfloat16).T
            out_ref[low - lead : high - lead] = out[low - n * width : high - n * width]


def normalize(series, begin, end):
    subjects, duration, slab = series.shape
    body = duration // LANES * LANES
    low, high = begin // LANES * LANES, min(-(-end // LANES) * LANES, slab)
    lanes = high - low
    width = LANES if lanes % LANES == 0 else lanes
    widths = [body + LANES] + [body] * (subjects - 1)
    return pl.pallas_call(
        functools.partial(normalize_kernel, begin=low, lead=begin - low),
        in_specs=[pl.BlockSpec(memory_space=pltpu.HBM)],
        out_shape=[jax.ShapeDtypeStruct((end - begin, w), jnp.bfloat16) for w in widths],
        scratch_shapes=[
            pltpu.VMEM((subjects, duration, lanes), jnp.float32),
            pltpu.VMEM((subjects, body + LANES, width), jnp.float32),
            pltpu.SemaphoreType.DMA((subjects * (lanes // width),)),
        ],
        compiler_params=pltpu.CompilerParams(vmem_limit_bytes=48 * 2**20),
        cost_estimate=HINT,
    )(series)


def after(pieces, others, cost=HINT):
    def nothing(*refs):
        pass

    return pl.pallas_call(
        nothing,
        in_specs=[ANY] * (len(pieces) + len(others)),
        out_specs=[ANY] * len(pieces),
        out_shape=[jax.ShapeDtypeStruct(piece.shape, piece.dtype) for piece in pieces],
        input_output_aliases={i: i for i in range(len(pieces))},
        cost_estimate=cost,
    )(*pieces, *others)


def combine_kernel(*refs, starts, scale):
    *in_refs, out_ref = refs
    total = jnp.zeros(out_ref.shape, jnp.float32)
    for ref, start in zip(in_refs, starts):
        if start is None:
            total = total + ref[...].astype(jnp.float32)
    out_ref[...] = total * scale
    for ref, start in zip(in_refs, starts):
        if start is not None:
            here = pl.ds(start, ref.shape[1])
            out_ref[:, here] = out_ref[:, here] + ref[...].astype(jnp.float32) * scale


def combine(terms, starts, slab, columns, scale):
    step = max(d for d in range(16, 161, 16) if slab % d == 0)
    return pl.pallas_call(
        functools.partial(combine_kernel, starts=starts, scale=scale),
        grid=(slab // step,),
        in_specs=[pl.BlockSpec((step, term.shape[1]), lambda i: (i, 0)) for term in terms],
        out_specs=pl.BlockSpec((step, columns), lambda i: (i, 0)),
        out_shape=jax.ShapeDtypeStruct((slab, columns), jnp.float32),
        compiler_params=pltpu.CompilerParams(vmem_limit_bytes=48 * 2**20),
        cost_estimate=HINT,
    )(*terms)


def finish_kernel(part_ref, before_ref, out_ref, *, scale):
    out_ref[...] = before_ref[...] + part_ref[...].astype(jnp.float32) * scale


def finish(part, before, first, scale):
    slab = before.shape[0]
    width = math.gcd(part.shape[1], first)
    block = (slab, width)
    there = pl.BlockSpec(block, lambda i, j: (i, first // width + j))
    return pl.pallas_call(
        functools.partial(finish_kernel, scale=scale),
        grid=(slab // block[0], part.shape[1] // width),
        in_specs=[pl.BlockSpec(block, lambda i, j: (i, j)), there],
        out_specs=there,
        out_shape=jax.ShapeDtypeStruct(before.shape, jnp.float32),
        input_output_aliases={1: 0},
        cost_estimate=HINT,
    )(part, before)


def scores_kernel(
    source_ref, block_start_ref, place_ref, *refs, subject, targets, cuts, slab, granule, block_rows, chips, chunk, duration
):
    count = source_ref.shape[0]
    bodies, tails = refs[: 2 * count], refs[2 * count : 4 * count]
    own_rows, products_a, products_b, place_of, sems = refs[-5:]
    refs = refs[-5 - 2 * len(targets) : -5]
    out_refs, columns_refs = refs[: len(targets)], refs[len(targets) :]
    body = duration // LANES * LANES
    tail = duration - body
    for a in range(block_start_ref.shape[0]):
        place_of[block_start_ref[a] // block_rows] = a

    position, subj = place_ref[0], place_ref[1]
    chip, core = subj // 2, subj % 2
    wanted = [(position * slab, own_rows)]
    for (away, flip, first, _), columns_ref in zip(targets, columns_refs):
        owner = (chip + away) % chips * 2 + (core + flip) % 2
        wanted.append((owner * chunk + first, columns_ref))

    for slot in range(count):
        for half in range(2):
            piece = 2 * slot + half
            low = source_ref[slot] * slab + cuts[half]

            def start(g, _, piece=piece, low=low):
                stored = low + g * granule
                block = stored // block_rows
                row = place_of[block] * block_rows + (stored - block * block_rows)
                here = pl.ds(pl.multiple_of(g * granule, granule), granule)
                for n, (begin, to_ref) in enumerate(wanted):

                    @pl.when((row >= begin) & (row < begin + to_ref.shape[0]))
                    def _():
                        there = pl.ds(pl.multiple_of(row - begin, granule), granule)
                        if subject == 0:
                            pltpu.make_async_copy(tails[piece].at[here], to_ref.at[there], sems.at[n]).start()
                        else:
                            pltpu.make_async_copy(
                                bodies[piece].at[here], to_ref.at[there, :body], sems.at[n]
                            ).start()
                            pltpu.make_async_copy(
                                tails[piece].at[here, body:], to_ref.at[there, body:], sems.at[n]
                            ).start()

                return 0

            lax.fori_loop(0, (cuts[half + 1] - cuts[half]) // granule, start, 0)

    def arrived(n):
        to_ref = wanted[n][1]
        pltpu.make_async_copy(to_ref, to_ref, sems.at[n]).wait()

    arrived(0)
    lane = lax.broadcasted_iota(jnp.int32, (slab, LANES), 1)
    kept = (lane >= subject * tail) & (lane < (subject + 1) * tail)
    own_rows[:, body:] = jnp.where(kept, own_rows[:, body:].astype(jnp.float32), 0.0).astype(jnp.bfloat16)

    limit = clip_limit * duration
    width = products_a.shape[1]
    tiles = []
    for n, out_ref in enumerate(out_refs):
        tiles += [(n + 1, k, out_ref) for k in range(0, out_ref.shape[1], width)]
    buffers = (products_a, products_b)

    def multiply(i):
        n, k, _ = tiles[i]
        if k == 0:
            arrived(n)
        buffers[i % 2][...] = lax.dot_general(
            own_rows[...], wanted[n][1][pl.ds(k, width)], (((1,), (1,)), ((), ())), preferred_element_type=jnp.float32
        )

    def score(i):
        products = jnp.clip(buffers[i % 2][...], -limit, limit)
        fisher = 0.5 * (jnp.log(duration + products) - jnp.log(duration - products))
        tiles[i][2][:, pl.ds(tiles[i][1], width)] = fisher.astype(jnp.bfloat16)

    multiply(0)
    for i in range(1, len(tiles)):
        multiply(i)
        score(i - 1)
    score(len(tiles) - 1)


def scores(source, block_start, place, subject, targets, bodies, tails, cuts, window, chips, duration, late=()):
    slab = cuts[-1]
    block_rows = window // block_start.shape[0]
    chunk = window // (2 * chips)
    sizes = [columns for _, _, _, columns in targets]
    granule = math.gcd(*cuts, *sizes, *(first for _, _, first, _ in targets), block_rows)
    width = math.gcd(*sizes, 256)
    padded = tails[0].shape[1]
    smem = pl.BlockSpec(memory_space=pltpu.SMEM)
    return pl.pallas_call(
        functools.partial(
            scores_kernel,
            subject=subject,
            targets=targets,
            cuts=cuts,
            slab=slab,
            granule=granule,
            block_rows=block_rows,
            chips=chips,
            chunk=chunk,
            duration=duration,
        ),
        in_specs=[smem, smem, smem] + [ANY] * (2 * len(tails) + len(late)),
        out_shape=[jax.ShapeDtypeStruct((slab, columns), jnp.bfloat16) for columns in sizes],
        scratch_shapes=[pltpu.VMEM((columns, padded), jnp.bfloat16) for columns in sizes]
        + [
            pltpu.VMEM((slab, padded), jnp.bfloat16),
            pltpu.VMEM((slab, width), jnp.float32),
            pltpu.VMEM((slab, width), jnp.float32),
            pltpu.SMEM((block_start.shape[0],), jnp.int32),
            pltpu.SemaphoreType.DMA((1 + len(targets),)),
        ],
        compiler_params=pltpu.CompilerParams(vmem_limit_bytes=48 * 2**20),
        cost_estimate=HINT,
    )(source, block_start, place, *bodies, *tails, *late)


def on_device(series, block_start):
    local_subjects, slab, duration = series.shape
    rows, cols = lax.axis_size("row"), lax.axis_size("col")
    count = rows * cols
    window = count * slab
    subjs = lax.axis_size("subj")
    chips = subjs // 2
    cuts = (0, slab // 2, slab)
    order = cycle(rows, cols)
    onward = [(order[i], order[(i + 1) % count]) for i in range(count)]
    backward = [(b, a) for a, b in onward]
    reach = count // 2
    offsets = [0]
    for d in range(1, reach):
        offsets += [d, -d]
    offsets.append(reach)
    table = np.zeros((count, count), np.int32)
    for i, device in enumerate(order):
        table[device] = [order[(i - d) % count] for d in offsets]
    position = lax.axis_index(SLABS)
    source = jnp.asarray(table)[position]
    place = jnp.stack([position, lax.axis_index("subj")]).astype(jnp.int32)

    def gather(a, gate=None):
        got = [[normed[0][a], normed[1][a]]]
        for d in range(1, reach):
            ahead, behind = got[max(2 * d - 3, 0)], got[max(2 * d - 2, 0)]
            got += [[None, None], [None, None]]
            for half in range(2):
                waits = gate(d, half, got) if gate else ()
                if d > 1:
                    ahead[half], behind[half] = after([ahead[half], behind[half]], waits)
                elif waits:
                    (ahead[half],) = after([ahead[half]], waits)
                got[-2][half] = lax.ppermute(ahead[half], SLABS, onward)
                got[-1][half] = lax.ppermute(behind[half], SLABS, backward)
        waits = gate(reach, 0, got) if gate else ()
        last = []
        for half, side, way in ((0, -2, onward), (1, -1, backward)):
            if waits:
                (got[side][half],) = after([got[side][half]], waits)
            last.append(lax.ppermute(got[side][half], SLABS, way))
        got.append(last)
        return got

    def flat(pairs):
        return [piece for pair in pairs for piece in pair]

    swap = [(s, s ^ 1) for s in range(subjs)]
    columns = jnp.swapaxes(series, 1, 2)
    normed = [normalize(columns, cuts[half], cuts[half + 1]) for half in range(2)]
    everything = [gather(0)]
    chunk = window // subjs
    width = math.gcd(chunk, 256)
    early = -(-chunk // width // 2) * width
    cut = ((0, early), (early, chunk - early))
    aways = [*range(1, chips), 0]

    def share(a, targets, late=()):
        bodies, tails = flat(everything[a]), flat(everything[0])
        return scores(source, block_start, place, a, targets, bodies, tails, cuts, window, chips, duration, late)

    def cross(other, hold=()):
        if hold:
            (other,) = after([other], hold)
        return lax.ppermute(other, "subj", swap)

    def send(summed, d, cost, before=()):
        there = lax.ppermute(summed, "subj", [(s, (s + 2 * d) % subjs) for s in range(subjs)])
        return after([there], before, cost)[0]

    def added(same, crossed):
        return (same.astype(jnp.float32) + crossed.astype(jnp.float32)).astype(jnp.bfloat16)

    terms, starts = [], []
    for a in range(1, local_subjects):
        shares, sums = [], []

        def gate(d, half, got, a=a, before=everything[-1], shares=shares, sums=sums):
            if d == 1:
                return [before[-3][half], before[-2][half]]
            n = d - 2
            if half == 0 and n < chips:
                late = [*got[2 * n - 1], *got[2 * n]] if n else ()
                parts = cut if aways[n] else ((0, chunk),)
                shares.append(share(a - 1, [(aways[n], flip, *part) for part in parts for flip in (0, 1)], late))
            waits = [shares[n][0]] if n < chips else []
            if (d, half) == (reach, 0):
                for m, (away, arrays) in enumerate(zip(aways[:-1], shares)):
                    hold = [*got[2 * m + 1], *got[2 * m + 2]]
                    for (start, _), same, other in zip(cut, arrays[::2], arrays[1::2]):
                        sums.append((added(same, cross(other, hold)), away, start))
            if d >= reach:
                waits += [summed for summed, _, _ in sums]
            return waits

        everything.append(gather(a, gate))
        for summed, d, start in sums:
            terms.append(send(summed, d, SHORT))
            starts.append(start)
        same, other = shares[-1]
        gone = list(terms)
        terms += [same, cross(other)]
        starts += [None, None]
    last = local_subjects - 1
    scale = 1 / (local_subjects * subjs)
    late = gone
    for d in aways[:-2]:
        same, other = share(last, [(d, 0, 0, chunk), (d, 1, 0, chunk)], late)
        late = [added(same, cross(other))]
        terms.append(send(late[0], d, LONG))
        starts.append(None)
    d = aways[-2]
    same, other = share(last, [(d, 0, 0, early), (d, 1, 0, early)], late)
    summed = added(same, cross(other))
    there = send(summed, d, LONG)
    rest = chunk - early
    other, same, others = share(last, [(d, 1, early, rest), (d, 0, early, rest), (0, 1, 0, chunk)], [summed])
    summed = added(same, cross(other))
    (same,) = share(last, [(0, 0, 0, chunk)], [summed, there])
    terms += [same, cross(others), there]
    starts += [None, None, 0]
    out = combine(terms, starts, slab, chunk, scale)
    return finish(send(summed, d, LONG, [out]), out, early, scale)


def solution(mesh):
    return jax.shard_map(
        on_device,
        mesh=mesh,
        in_specs=(P("subj", SLABS, None), P()),
        out_specs=P(SLABS, "subj"),
        check_vma=False,
    )
```

```python
import functools
import math

import jax
import jax.numpy as jnp
import numpy as np
from jax import lax
from jax.experimental import pallas as pl
from jax.experimental.pallas import tpu as pltpu
from jax.sharding import PartitionSpec as P

clip_limit = 0.99
epsilon = 1e-05
SLABS = ("row", "col")
LANES = 128
HINT = pl.CostEstimate(flops=0, bytes_accessed=1024, transcendentals=0)
SHORT = pl.CostEstimate(flops=0, bytes_accessed=1024, transcendentals=0)
LONG = pl.CostEstimate(flops=0, bytes_accessed=2**27, transcendentals=0)
ANY = pl.BlockSpec(memory_space=pl.ANY)


def cycle(rows, cols):
    if cols == 1:
        return list(range(rows))
    walk = [(r, 0) for r in range(rows)]
    for i, r in enumerate(reversed(range(rows))):
        back = list(range(1, cols))
        walk += [(r, c) for c in (back if i % 2 == 0 else back[::-1])]
    return [r * cols + c for r, c in walk]


def normalize_kernel(series_ref, first_ref, *refs, begin, lead):
    other_refs, (raw, columns, sems) = refs[:-3], refs[-3:]
    subjects, duration, lanes = raw.shape
    body = duration // LANES * LANES
    tail = duration - body
    rows = first_ref.shape[0]
    width = LANES if lanes % LANES == 0 else lanes
    steps = lanes // width

    def copy(i):
        a, here = i % subjects, pl.ds(i // subjects * width, width)
        there = pl.ds(begin + i // subjects * width, width)
        return pltpu.make_async_copy(series_ref.at[a, :, there], raw.at[a, :, here], sems.at[i])

    for i in range(subjects * steps):
        copy(i).start()
    columns[:, duration + (subjects - 1) * tail :] = jnp.zeros(
        (subjects, LANES - subjects * tail, width), jnp.float32
    )
    for n in range(steps):
        here = pl.ds(n * width, width)
        for a in range(subjects):
            copy(n * subjects + a).wait()
            values = raw[a, :, here]
            center = jnp.mean(values, axis=0, keepdims=True)
            away = values - center
            spread = jnp.mean(away * away, axis=0, keepdims=True)
            normed = away * lax.rsqrt(spread + epsilon)
            columns[a, :duration] = normed
            if a:
                columns[0, duration + (a - 1) * tail : duration + a * tail] = normed[body:]
        low, high = max(n * width, lead), min((n + 1) * width, lead + rows)
        for a, out_ref in enumerate((first_ref, *other_refs)):
            out = columns[a, : out_ref.shape[1]].astype(jnp.bfloat16).T
            out_ref[low - lead : high - lead] = out[low - n * width : high - n * width]


def normalize(series, begin, end):
    subjects, duration, slab = series.shape
    body = duration // LANES * LANES
    low, high = begin // LANES * LANES, min(-(-end // LANES) * LANES, slab)
    lanes = high - low
    width = LANES if lanes % LANES == 0 else lanes
    widths = [body + LANES] + [body] * (subjects - 1)
    return pl.pallas_call(
        functools.partial(normalize_kernel, begin=low, lead=begin - low),
        in_specs=[pl.BlockSpec(memory_space=pltpu.HBM)],
        out_shape=[jax.ShapeDtypeStruct((end - begin, w), jnp.bfloat16) for w in widths],
        scratch_shapes=[
            pltpu.VMEM((subjects, duration, lanes), jnp.float32),
            pltpu.VMEM((subjects, body + LANES, width), jnp.float32),
            pltpu.SemaphoreType.DMA((subjects * (lanes // width),)),
        ],
        compiler_params=pltpu.CompilerParams(vmem_limit_bytes=48 * 2**20),
        cost_estimate=HINT,
    )(series)


def after(pieces, others, cost=HINT):
    def nothing(*refs):
        pass

    return pl.pallas_call(
        nothing,
        in_specs=[ANY] * (len(pieces) + len(others)),
        out_specs=[ANY] * len(pieces),
        out_shape=[jax.ShapeDtypeStruct(piece.shape, piece.dtype) for piece in pieces],
        input_output_aliases={i: i for i in range(len(pieces))},
        cost_estimate=cost,
    )(*pieces, *others)


def combine_kernel(*refs, starts, scale):
    *in_refs, out_ref = refs
    total = jnp.zeros(out_ref.shape, jnp.float32)
    for ref, start in zip(in_refs, starts):
        if start is None:
            total = total + ref[...].astype(jnp.float32)
    out_ref[...] = total * scale
    for ref, start in zip(in_refs, starts):
        if start is not None:
            here = pl.ds(start, ref.shape[1])
            out_ref[:, here] = out_ref[:, here] + ref[...].astype(jnp.float32) * scale


def combine(terms, starts, slab, columns, scale):
    step = max(d for d in range(16, 161, 16) if slab % d == 0)
    return pl.pallas_call(
        functools.partial(combine_kernel, starts=starts, scale=scale),
        grid=(slab // step,),
        in_specs=[pl.BlockSpec((step, term.shape[1]), lambda i: (i, 0)) for term in terms],
        out_specs=pl.BlockSpec((step, columns), lambda i: (i, 0)),
        out_shape=jax.ShapeDtypeStruct((slab, columns), jnp.float32),
        compiler_params=pltpu.CompilerParams(vmem_limit_bytes=48 * 2**20),
        cost_estimate=HINT,
    )(*terms)


def finish_kernel(part_ref, before_ref, out_ref, *, scale):
    out_ref[...] = before_ref[...] + part_ref[...].astype(jnp.float32) * scale


def finish(part, before, first, scale):
    slab = before.shape[0]
    width = math.gcd(part.shape[1], first)
    block = (slab, width)
    there = pl.BlockSpec(block, lambda i, j: (i, first // width + j))
    return pl.pallas_call(
        functools.partial(finish_kernel, scale=scale),
        grid=(slab // block[0], part.shape[1] // width),
        in_specs=[pl.BlockSpec(block, lambda i, j: (i, j)), there],
        out_specs=there,
        out_shape=jax.ShapeDtypeStruct(before.shape, jnp.float32),
        input_output_aliases={1: 0},
        cost_estimate=HINT,
    )(part, before)


def scores_kernel(
    source_ref, block_start_ref, place_ref, *refs, subject, targets, cuts, slab, granule, block_rows, chips, chunk, duration
):
    count = source_ref.shape[0]
    bodies, tails = refs[: 2 * count], refs[2 * count : 4 * count]
    own_rows, products_a, products_b, place_of, sems = refs[-5:]
    refs = refs[-5 - 2 * len(targets) : -5]
    out_refs, columns_refs = refs[: len(targets)], refs[len(targets) :]
    body = duration // LANES * LANES
    tail = duration - body
    for a in range(block_start_ref.shape[0]):
        place_of[block_start_ref[a] // block_rows] = a

    position, subj = place_ref[0], place_ref[1]
    chip, core = subj // 2, subj % 2
    wanted = [(position * slab, own_rows)]
    for (away, flip, first, _), columns_ref in zip(targets, columns_refs):
        owner = (chip + away) % chips * 2 + (core + flip) % 2
        wanted.append((owner * chunk + first, columns_ref))

    for slot in range(count):
        for half in range(2):
            piece = 2 * slot + half
            low = source_ref[slot] * slab + cuts[half]

            def start(g, _, piece=piece, low=low):
                stored = low + g * granule
                block = stored // block_rows
                row = place_of[block] * block_rows + (stored - block * block_rows)
                here = pl.ds(pl.multiple_of(g * granule, granule), granule)
                for n, (begin, to_ref) in enumerate(wanted):

                    @pl.when((row >= begin) & (row < begin + to_ref.shape[0]))
                    def _():
                        there = pl.ds(pl.multiple_of(row - begin, granule), granule)
                        if subject == 0:
                            pltpu.make_async_copy(tails[piece].at[here], to_ref.at[there], sems.at[n]).start()
                        else:
                            pltpu.make_async_copy(
                                bodies[piece].at[here], to_ref.at[there, :body], sems.at[n]
                            ).start()
                            pltpu.make_async_copy(
                                tails[piece].at[here, body:], to_ref.at[there, body:], sems.at[n]
                            ).start()

                return 0

            lax.fori_loop(0, (cuts[half + 1] - cuts[half]) // granule, start, 0)

    def arrived(n):
        to_ref = wanted[n][1]
        pltpu.make_async_copy(to_ref, to_ref, sems.at[n]).wait()

    arrived(0)
    lane = lax.broadcasted_iota(jnp.int32, (slab, LANES), 1)
    kept = (lane >= subject * tail) & (lane < (subject + 1) * tail)
    own_rows[:, body:] = jnp.where(kept, own_rows[:, body:].astype(jnp.float32), 0.0).astype(jnp.bfloat16)

    limit = clip_limit * duration
    width = products_a.shape[1]
    tiles = []
    for n, out_ref in enumerate(out_refs):
        tiles += [(n + 1, k, out_ref) for k in range(0, out_ref.shape[1], width)]
    buffers = (products_a, products_b)

    def multiply(i):
        n, k, _ = tiles[i]
        if k == 0:
            arrived(n)
        buffers[i % 2][...] = lax.dot_general(
            own_rows[...], wanted[n][1][pl.ds(k, width)], (((1,), (1,)), ((), ())), preferred_element_type=jnp.float32
        )

    def score(i):
        products = jnp.clip(buffers[i % 2][...], -limit, limit)
        fisher = 0.5 * (jnp.log(duration + products) - jnp.log(duration - products))
        tiles[i][2][:, pl.ds(tiles[i][1], width)] = fisher.astype(jnp.bfloat16)

    multiply(0)
    for i in range(1, len(tiles)):
        multiply(i)
        score(i - 1)
    score(len(tiles) - 1)


def scores(source, block_start, place, subject, targets, bodies, tails, cuts, window, chips, duration, late=()):
    slab = cuts[-1]
    block_rows = window // block_start.shape[0]
    chunk = window // (2 * chips)
    sizes = [columns for _, _, _, columns in targets]
    granule = math.gcd(*cuts, *sizes, *(first for _, _, first, _ in targets), block_rows)
    width = math.gcd(*sizes, 256)
    padded = tails[0].shape[1]
    smem = pl.BlockSpec(memory_space=pltpu.SMEM)
    return pl.pallas_call(
        functools.partial(
            scores_kernel,
            subject=subject,
            targets=targets,
            cuts=cuts,
            slab=slab,
            granule=granule,
            block_rows=block_rows,
            chips=chips,
            chunk=chunk,
            duration=duration,
        ),
        in_specs=[smem, smem, smem] + [ANY] * (2 * len(tails) + len(late)),
        out_shape=[jax.ShapeDtypeStruct((slab, columns), jnp.bfloat16) for columns in sizes],
        scratch_shapes=[pltpu.VMEM((columns, padded), jnp.bfloat16) for columns in sizes]
        + [
            pltpu.VMEM((slab, padded), jnp.bfloat16),
            pltpu.VMEM((slab, width), jnp.float32),
            pltpu.VMEM((slab, width), jnp.float32),
            pltpu.SMEM((block_start.shape[0],), jnp.int32),
            pltpu.SemaphoreType.DMA((1 + len(targets),)),
        ],
        compiler_params=pltpu.CompilerParams(vmem_limit_bytes=48 * 2**20),
        cost_estimate=HINT,
    )(source, block_start, place, *bodies, *tails, *late)


def on_device(series, block_start):
    local_subjects, slab, duration = series.shape
    rows, cols = lax.axis_size("row"), lax.axis_size("col")
    count = rows * cols
    window = count * slab
    subjs = lax.axis_size("subj")
    chips = subjs // 2
    cuts = (0, slab // 2, slab)
    order = cycle(rows, cols)
    onward = [(order[i], order[(i + 1) % count]) for i in range(count)]
    backward = [(b, a) for a, b in onward]
    reach = count // 2
    offsets = [0]
    for d in range(1, reach):
        offsets += [d, -d]
    offsets.append(reach)
    table = np.zeros((count, count), np.int32)
    for i, device in enumerate(order):
        table[device] = [order[(i - d) % count] for d in offsets]
    position = lax.axis_index(SLABS)
    source = jnp.asarray(table)[position]
    place = jnp.stack([position, lax.axis_index("subj")]).astype(jnp.int32)

    def gather(a, gate=None):
        got = [[normed[0][a], normed[1][a]]]
        for d in range(1, reach):
            ahead, behind = got[max(2 * d - 3, 0)], got[max(2 * d - 2, 0)]
            got += [[None, None], [None, None]]
            for half in range(2):
                waits = gate(d, half, got) if gate else ()
                if d > 1:
                    ahead[half], behind[half] = after([ahead[half], behind[half]], waits)
                elif waits:
                    (ahead[half],) = after([ahead[half]], waits)
                got[-2][half] = lax.ppermute(ahead[half], SLABS, onward)
                got[-1][half] = lax.ppermute(behind[half], SLABS, backward)
        waits = gate(reach, 0, got) if gate else ()
        last = []
        for half, side, way in ((0, -2, onward), (1, -1, backward)):
            if waits:
                (got[side][half],) = after([got[side][half]], waits)
            last.append(lax.ppermute(got[side][half], SLABS, way))
        got.append(last)
        return got

    def flat(pairs):
        return [piece for pair in pairs for piece in pair]

    swap = [(s, s ^ 1) for s in range(subjs)]
    columns = jnp.swapaxes(series, 1, 2)
    normed = [normalize(columns, cuts[half], cuts[half + 1]) for half in range(2)]
    everything = [gather(0)]
    chunk = window // subjs
    width = math.gcd(chunk, 256)
    early = -(-chunk // width // 2) * width
    cut = ((0, early), (early, chunk - early))
    aways = [*range(1, chips), 0]

    def share(a, targets, late=()):
        bodies, tails = flat(everything[a]), flat(everything[0])
        return scores(source, block_start, place, a, targets, bodies, tails, cuts, window, chips, duration, late)

    def cross(other, hold=()):
        if hold:
            (other,) = after([other], hold)
        return lax.ppermute(other, "subj", swap)

    def send(summed, d, cost, before=()):
        there = lax.ppermute(summed, "subj", [(s, (s + 2 * d) % subjs) for s in range(subjs)])
        return after([there], before, cost)[0]

    def added(same, crossed):
        return (same.astype(jnp.float32) + crossed.astype(jnp.float32)).astype(jnp.bfloat16)

    terms, starts = [], []
    for a in range(1, local_subjects):
        shares, sums = [], []

        def gate(d, half, got, a=a, before=everything[-1], shares=shares, sums=sums):
            if d == 1:
                return [before[-3][half], before[-2][half]]
            n = d - 2
            if half == 0 and n < chips - 1:
                late = [*got[2 * n - 1], *got[2 * n]] if n else ()
                shares.append(share(a - 1, [(aways[n], flip, *part) for part in cut for flip in (0, 1)], late))
            waits = [shares[n][0]] if n < chips - 1 else []
            if (d, half) == (reach, 0):
                for m, (away, arrays) in enumerate(zip(aways[:-1], shares)):
                    hold = [*got[2 * m + 1], *got[2 * m + 2]]
                    for (start, _), same, other in zip(cut, arrays[::2], arrays[1::2]):
                        sums.append((added(same, cross(other, hold)), away, start))
            if d >= reach:
                waits += [summed for summed, _, _ in sums]
            return waits

        everything.append(gather(a, gate))
        for summed, d, start in sums:
            terms.append(send(summed, d, SHORT))
            starts.append(start)
        same, other = share(a - 1, [(0, flip, 0, chunk) for flip in (0, 1)], [*everything[a][-3], *everything[a][-2]])
        gone = [*terms, same]
        terms += [same, cross(other)]
        starts += [None, None]
    last = local_subjects - 1
    scale = 1 / (local_subjects * subjs)
    late = gone
    for d in aways[:-2]:
        same, other = share(last, [(d, 0, 0, chunk), (d, 1, 0, chunk)], late)
        late = [added(same, cross(other))]
        terms.append(send(late[0], d, LONG))
        starts.append(None)
    d = aways[-2]
    same, other = share(last, [(d, 0, 0, early), (d, 1, 0, early)], late)
    leading = added(same, cross(other))
    rest = chunk - early
    other, same, others = share(last, [(d, 1, early, rest), (d, 0, early, rest), (0, 1, 0, chunk)], [leading])
    summed = added(same, cross(other))
    (same,) = share(last, [(0, 0, 0, chunk)], [summed])
    there = send(leading, d, LONG, [same])
    terms += [same, cross(others, [there]), there]
    starts += [None, None, 0]
    out = combine(terms, starts, slab, chunk, scale)
    return finish(send(summed, d, LONG, [out]), out, early, scale)


def solution(mesh):
    return jax.shard_map(
        on_device,
        mesh=mesh,
        in_specs=(P("subj", SLABS, None), P()),
        out_specs=P(SLABS, "subj"),
        check_vma=False,
    )
```

```python
import functools
import math

import jax
import jax.numpy as jnp
import numpy as np
from jax import lax
from jax.experimental import pallas as pl
from jax.experimental.pallas import tpu as pltpu
from jax.sharding import PartitionSpec as P

clip_limit = 0.99
epsilon = 1e-05
SLABS = ("row", "col")
LANES = 128
HINT = pl.CostEstimate(flops=0, bytes_accessed=1024, transcendentals=0)
SHORT = pl.CostEstimate(flops=0, bytes_accessed=1024, transcendentals=0)
LONG = pl.CostEstimate(flops=0, bytes_accessed=2**27, transcendentals=0)
ANY = pl.BlockSpec(memory_space=pl.ANY)


def cycle(rows, cols):
    if cols == 1:
        return list(range(rows))
    walk = [(r, 0) for r in range(rows)]
    for i, r in enumerate(reversed(range(rows))):
        back = list(range(1, cols))
        walk += [(r, c) for c in (back if i % 2 == 0 else back[::-1])]
    return [r * cols + c for r, c in walk]


def normalize_kernel(series_ref, first_ref, *refs, begin, lead):
    other_refs, (raw, columns, sems) = refs[:-3], refs[-3:]
    subjects, duration, lanes = raw.shape
    body = duration // LANES * LANES
    tail = duration - body
    rows = first_ref.shape[0]
    width = LANES if lanes % LANES == 0 else lanes
    steps = lanes // width

    def copy(i):
        a, here = i % subjects, pl.ds(i // subjects * width, width)
        there = pl.ds(begin + i // subjects * width, width)
        return pltpu.make_async_copy(series_ref.at[a, :, there], raw.at[a, :, here], sems.at[i])

    for i in range(subjects * steps):
        copy(i).start()
    columns[:, duration + (subjects - 1) * tail :] = jnp.zeros(
        (subjects, LANES - subjects * tail, width), jnp.float32
    )
    for n in range(steps):
        here = pl.ds(n * width, width)
        for a in range(subjects):
            copy(n * subjects + a).wait()
            values = raw[a, :, here]
            center = jnp.mean(values, axis=0, keepdims=True)
            away = values - center
            spread = jnp.mean(away * away, axis=0, keepdims=True)
            normed = away * lax.rsqrt(spread + epsilon)
            columns[a, :duration] = normed
            if a:
                columns[0, duration + (a - 1) * tail : duration + a * tail] = normed[body:]
        low, high = max(n * width, lead), min((n + 1) * width, lead + rows)
        for a, out_ref in enumerate((first_ref, *other_refs)):
            out = columns[a, : out_ref.shape[1]].astype(jnp.bfloat16).T
            out_ref[low - lead : high - lead] = out[low - n * width : high - n * width]


def normalize(series, begin, end):
    subjects, duration, slab = series.shape
    body = duration // LANES * LANES
    low, high = begin // LANES * LANES, min(-(-end // LANES) * LANES, slab)
    lanes = high - low
    width = LANES if lanes % LANES == 0 else lanes
    widths = [body + LANES] + [body] * (subjects - 1)
    return pl.pallas_call(
        functools.partial(normalize_kernel, begin=low, lead=begin - low),
        in_specs=[pl.BlockSpec(memory_space=pltpu.HBM)],
        out_shape=[jax.ShapeDtypeStruct((end - begin, w), jnp.bfloat16) for w in widths],
        scratch_shapes=[
            pltpu.VMEM((subjects, duration, lanes), jnp.float32),
            pltpu.VMEM((subjects, body + LANES, width), jnp.float32),
            pltpu.SemaphoreType.DMA((subjects * (lanes // width),)),
        ],
        compiler_params=pltpu.CompilerParams(vmem_limit_bytes=48 * 2**20),
        cost_estimate=HINT,
    )(series)


def after(pieces, others, cost=HINT):
    def nothing(*refs):
        pass

    return pl.pallas_call(
        nothing,
        in_specs=[ANY] * (len(pieces) + len(others)),
        out_specs=[ANY] * len(pieces),
        out_shape=[jax.ShapeDtypeStruct(piece.shape, piece.dtype) for piece in pieces],
        input_output_aliases={i: i for i in range(len(pieces))},
        cost_estimate=cost,
    )(*pieces, *others)


def combine_kernel(*refs, starts, scale):
    *in_refs, out_ref = refs
    total = jnp.zeros(out_ref.shape, jnp.float32)
    for ref, start in zip(in_refs, starts):
        if start is None:
            total = total + ref[...].astype(jnp.float32)
    out_ref[...] = total * scale
    for ref, start in zip(in_refs, starts):
        if start is not None:
            here = pl.ds(start, ref.shape[1])
            out_ref[:, here] = out_ref[:, here] + ref[...].astype(jnp.float32) * scale


def combine(terms, starts, slab, columns, scale):
    step = max(d for d in range(16, 161, 16) if slab % d == 0)
    return pl.pallas_call(
        functools.partial(combine_kernel, starts=starts, scale=scale),
        grid=(slab // step,),
        in_specs=[pl.BlockSpec((step, term.shape[1]), lambda i: (i, 0)) for term in terms],
        out_specs=pl.BlockSpec((step, columns), lambda i: (i, 0)),
        out_shape=jax.ShapeDtypeStruct((slab, columns), jnp.float32),
        compiler_params=pltpu.CompilerParams(vmem_limit_bytes=48 * 2**20),
        cost_estimate=HINT,
    )(*terms)


def finish_kernel(part_ref, before_ref, out_ref, *, scale):
    out_ref[...] = before_ref[...] + part_ref[...].astype(jnp.float32) * scale


def finish(part, before, first, scale):
    slab = before.shape[0]
    width = math.gcd(part.shape[1], first)
    block = (slab, width)
    there = pl.BlockSpec(block, lambda i, j: (i, first // width + j))
    return pl.pallas_call(
        functools.partial(finish_kernel, scale=scale),
        grid=(slab // block[0], part.shape[1] // width),
        in_specs=[pl.BlockSpec(block, lambda i, j: (i, j)), there],
        out_specs=there,
        out_shape=jax.ShapeDtypeStruct(before.shape, jnp.float32),
        input_output_aliases={1: 0},
        cost_estimate=HINT,
    )(part, before)


def scores_kernel(
    source_ref, block_start_ref, place_ref, *refs, subject, targets, cuts, slab, granule, block_rows, chips, chunk, duration
):
    count = source_ref.shape[0]
    bodies, tails = refs[: 2 * count], refs[2 * count : 4 * count]
    own_rows, products_a, products_b, place_of, sems = refs[-5:]
    refs = refs[-5 - 2 * len(targets) : -5]
    out_refs, columns_refs = refs[: len(targets)], refs[len(targets) :]
    body = duration // LANES * LANES
    tail = duration - body
    for a in range(block_start_ref.shape[0]):
        place_of[block_start_ref[a] // block_rows] = a

    position, subj = place_ref[0], place_ref[1]
    chip, core = subj // 2, subj % 2
    wanted = [(position * slab, own_rows)]
    for (away, flip, first, _), columns_ref in zip(targets, columns_refs):
        owner = (chip + away) % chips * 2 + (core + flip) % 2
        wanted.append((owner * chunk + first, columns_ref))

    for slot in range(count):
        for half in range(2):
            piece = 2 * slot + half
            low = source_ref[slot] * slab + cuts[half]

            def start(g, _, piece=piece, low=low):
                stored = low + g * granule
                block = stored // block_rows
                row = place_of[block] * block_rows + (stored - block * block_rows)
                here = pl.ds(pl.multiple_of(g * granule, granule), granule)
                for n, (begin, to_ref) in enumerate(wanted):

                    @pl.when((row >= begin) & (row < begin + to_ref.shape[0]))
                    def _():
                        there = pl.ds(pl.multiple_of(row - begin, granule), granule)
                        if subject == 0:
                            pltpu.make_async_copy(tails[piece].at[here], to_ref.at[there], sems.at[n]).start()
                        else:
                            pltpu.make_async_copy(
                                bodies[piece].at[here], to_ref.at[there, :body], sems.at[n]
                            ).start()
                            pltpu.make_async_copy(
                                tails[piece].at[here, body:], to_ref.at[there, body:], sems.at[n]
                            ).start()

                return 0

            lax.fori_loop(0, (cuts[half + 1] - cuts[half]) // granule, start, 0)

    def arrived(n):
        to_ref = wanted[n][1]
        pltpu.make_async_copy(to_ref, to_ref, sems.at[n]).wait()

    arrived(0)
    lane = lax.broadcasted_iota(jnp.int32, (slab, LANES), 1)
    kept = (lane >= subject * tail) & (lane < (subject + 1) * tail)
    own_rows[:, body:] = jnp.where(kept, own_rows[:, body:].astype(jnp.float32), 0.0).astype(jnp.bfloat16)

    limit = clip_limit * duration
    width = products_a.shape[1]
    tiles = []
    for n, out_ref in enumerate(out_refs):
        tiles += [(n + 1, k, out_ref) for k in range(0, out_ref.shape[1], width)]
    buffers = (products_a, products_b)

    def multiply(i):
        n, k, _ = tiles[i]
        if k == 0:
            arrived(n)
        buffers[i % 2][...] = lax.dot_general(
            own_rows[...], wanted[n][1][pl.ds(k, width)], (((1,), (1,)), ((), ())), preferred_element_type=jnp.float32
        )

    def score(i):
        products = jnp.clip(buffers[i % 2][...], -limit, limit)
        fisher = 0.5 * (jnp.log(duration + products) - jnp.log(duration - products))
        tiles[i][2][:, pl.ds(tiles[i][1], width)] = fisher.astype(jnp.bfloat16)

    multiply(0)
    for i in range(1, len(tiles)):
        multiply(i)
        score(i - 1)
    score(len(tiles) - 1)


def scores(source, block_start, place, subject, targets, bodies, tails, cuts, window, chips, duration, late=()):
    slab = cuts[-1]
    block_rows = window // block_start.shape[0]
    chunk = window // (2 * chips)
    sizes = [columns for _, _, _, columns in targets]
    granule = math.gcd(*cuts, *sizes, *(first for _, _, first, _ in targets), block_rows)
    width = math.gcd(*sizes, 256)
    padded = tails[0].shape[1]
    smem = pl.BlockSpec(memory_space=pltpu.SMEM)
    return pl.pallas_call(
        functools.partial(
            scores_kernel,
            subject=subject,
            targets=targets,
            cuts=cuts,
            slab=slab,
            granule=granule,
            block_rows=block_rows,
            chips=chips,
            chunk=chunk,
            duration=duration,
        ),
        in_specs=[smem, smem, smem] + [ANY] * (2 * len(tails) + len(late)),
        out_shape=[jax.ShapeDtypeStruct((slab, columns), jnp.bfloat16) for columns in sizes],
        scratch_shapes=[pltpu.VMEM((columns, padded), jnp.bfloat16) for columns in sizes]
        + [
            pltpu.VMEM((slab, padded), jnp.bfloat16),
            pltpu.VMEM((slab, width), jnp.float32),
            pltpu.VMEM((slab, width), jnp.float32),
            pltpu.SMEM((block_start.shape[0],), jnp.int32),
            pltpu.SemaphoreType.DMA((1 + len(targets),)),
        ],
        compiler_params=pltpu.CompilerParams(vmem_limit_bytes=48 * 2**20),
        cost_estimate=HINT,
    )(source, block_start, place, *bodies, *tails, *late)


def on_device(series, block_start):
    local_subjects, slab, duration = series.shape
    rows, cols = lax.axis_size("row"), lax.axis_size("col")
    count = rows * cols
    window = count * slab
    subjs = lax.axis_size("subj")
    chips = subjs // 2
    cuts = (0, slab // 2, slab)
    order = cycle(rows, cols)
    onward = [(order[i], order[(i + 1) % count]) for i in range(count)]
    backward = [(b, a) for a, b in onward]
    reach = count // 2
    offsets = [0]
    for d in range(1, reach):
        offsets += [d, -d]
    offsets.append(reach)
    table = np.zeros((count, count), np.int32)
    for i, device in enumerate(order):
        table[device] = [order[(i - d) % count] for d in offsets]
    position = lax.axis_index(SLABS)
    source = jnp.asarray(table)[position]
    place = jnp.stack([position, lax.axis_index("subj")]).astype(jnp.int32)

    def gather(a, gate=None):
        got = [[normed[0][a], normed[1][a]]]
        for d in range(1, reach):
            ahead, behind = got[max(2 * d - 3, 0)], got[max(2 * d - 2, 0)]
            got += [[None, None], [None, None]]
            for half in range(2):
                waits = gate(d, half, got) if gate else ()
                if d > 1:
                    ahead[half], behind[half] = after([ahead[half], behind[half]], waits)
                elif waits:
                    (ahead[half],) = after([ahead[half]], waits)
                got[-2][half] = lax.ppermute(ahead[half], SLABS, onward)
                got[-1][half] = lax.ppermute(behind[half], SLABS, backward)
        waits = gate(reach, 0, got) if gate else ()
        last = []
        for half, side, way in ((0, -2, onward), (1, -1, backward)):
            if waits:
                (got[side][half],) = after([got[side][half]], waits)
            last.append(lax.ppermute(got[side][half], SLABS, way))
        got.append(last)
        return got

    def flat(pairs):
        return [piece for pair in pairs for piece in pair]

    swap = [(s, s ^ 1) for s in range(subjs)]
    columns = jnp.swapaxes(series, 1, 2)
    normed = [normalize(columns, cuts[half], cuts[half + 1]) for half in range(2)]
    everything = [gather(0)]
    chunk = window // subjs
    width = math.gcd(chunk, 256)
    early = -(-chunk // width // 2) * width
    cut = ((0, early), (early, chunk - early))
    aways = [*range(1, chips), 0]

    def share(a, targets, late=()):
        bodies, tails = flat(everything[a]), flat(everything[0])
        return scores(source, block_start, place, a, targets, bodies, tails, cuts, window, chips, duration, late)

    def cross(other, hold=()):
        if hold:
            (other,) = after([other], hold)
        return lax.ppermute(other, "subj", swap)

    def send(summed, d, cost, before=()):
        there = lax.ppermute(summed, "subj", [(s, (s + 2 * d) % subjs) for s in range(subjs)])
        return after([there], before, cost)[0]

    def added(same, crossed):
        return (same.astype(jnp.float32) + crossed.astype(jnp.float32)).astype(jnp.bfloat16)

    terms, starts = [], []
    for a in range(1, local_subjects):
        shares, sums = [], []

        def gate(d, half, got, a=a, before=everything[-1], shares=shares, sums=sums):
            if d == 1:
                return [before[-3][half], before[-2][half]]
            n = d - 2
            if half == 0 and n < chips - 1:
                late = [*got[2 * n - 1], *got[2 * n]] if n else ()
                shares.append(share(a - 1, [(aways[n], flip, *part) for part in cut for flip in (0, 1)], late))
            waits = [shares[n][0]] if n < chips - 1 else []
            if (d, half) == (reach, 0):
                for m, (away, arrays) in enumerate(zip(aways[:-1], shares)):
                    hold = [*got[2 * m + 1], *got[2 * m + 2]]
                    for (start, _), same, other in zip(cut, arrays[::2], arrays[1::2]):
                        sums.append((added(same, cross(other, hold)), away, start))
            if d >= reach:
                waits += [summed for summed, _, _ in sums]
            return waits

        everything.append(gather(a, gate))
        for summed, d, start in sums:
            terms.append(send(summed, d, SHORT))
            starts.append(start)
        same, other = share(a - 1, [(0, flip, 0, chunk) for flip in (0, 1)], [everything[a][-3][0], everything[a][-2][1]])
        gone = [*terms, same]
        terms += [same, cross(other)]
        starts += [None, None]
    last = local_subjects - 1
    scale = 1 / (local_subjects * subjs)
    late = gone
    for d in aways[:-2]:
        same, other = share(last, [(d, 0, 0, chunk), (d, 1, 0, chunk)], late)
        late = [added(same, cross(other))]
        terms.append(send(late[0], d, LONG))
        starts.append(None)
    d = aways[-2]
    same, other = share(last, [(d, 0, 0, early), (d, 1, 0, early)], late)
    leading = added(same, cross(other))
    rest = chunk - early
    other, same, others = share(last, [(d, 1, early, rest), (d, 0, early, rest), (0, 1, 0, chunk)], [leading])
    summed = added(same, cross(other))
    (same,) = share(last, [(0, 0, 0, chunk)], [summed])
    there = send(leading, d, LONG)
    terms += [same, cross(others, [there, summed]), there]
    starts += [None, None, 0]
    out = combine(terms, starts, slab, chunk, scale)
    return finish(send(summed, d, LONG, [out]), out, early, scale)


def solution(mesh):
    return jax.shard_map(
        on_device,
        mesh=mesh,
        in_specs=(P("subj", SLABS, None), P()),
        out_specs=P(SLABS, "subj"),
        check_vma=False,
    )
```

```python
import functools
import math

import jax
import jax.numpy as jnp
import numpy as np
from jax import lax
from jax.experimental import pallas as pl
from jax.experimental.pallas import tpu as pltpu
from jax.sharding import PartitionSpec as P

clip_limit = 0.99
epsilon = 1e-05
SLABS = ("row", "col")
LANES = 128
HINT = pl.CostEstimate(flops=0, bytes_accessed=1024, transcendentals=0)
SHORT = pl.CostEstimate(flops=0, bytes_accessed=1024, transcendentals=0)
LONG = pl.CostEstimate(flops=0, bytes_accessed=2**27, transcendentals=0)
ANY = pl.BlockSpec(memory_space=pl.ANY)


def cycle(rows, cols):
    if cols == 1:
        return list(range(rows))
    walk = [(r, 0) for r in range(rows)]
    for i, r in enumerate(reversed(range(rows))):
        back = list(range(1, cols))
        walk += [(r, c) for c in (back if i % 2 == 0 else back[::-1])]
    return [r * cols + c for r, c in walk]


def normalize_kernel(series_ref, first_ref, *refs, begin, lead):
    other_refs, (raw, columns, sems) = refs[:-3], refs[-3:]
    subjects, duration, lanes = raw.shape
    body = duration // LANES * LANES
    tail = duration - body
    rows = first_ref.shape[0]
    width = LANES if lanes % LANES == 0 else lanes
    steps = lanes // width

    def copy(i):
        a, here = i % subjects, pl.ds(i // subjects * width, width)
        there = pl.ds(begin + i // subjects * width, width)
        return pltpu.make_async_copy(series_ref.at[a, :, there], raw.at[a, :, here], sems.at[i])

    for i in range(subjects * steps):
        copy(i).start()
    columns[:, duration + (subjects - 1) * tail :] = jnp.zeros(
        (subjects, LANES - subjects * tail, width), jnp.float32
    )
    for n in range(steps):
        here = pl.ds(n * width, width)
        for a in range(subjects):
            copy(n * subjects + a).wait()
            values = raw[a, :, here]
            center = jnp.mean(values, axis=0, keepdims=True)
            away = values - center
            spread = jnp.mean(away * away, axis=0, keepdims=True)
            normed = away * lax.rsqrt(spread + epsilon)
            columns[a, :duration] = normed
            if a:
                columns[0, duration + (a - 1) * tail : duration + a * tail] = normed[body:]
        low, high = max(n * width, lead), min((n + 1) * width, lead + rows)
        for a, out_ref in enumerate((first_ref, *other_refs)):
            out = columns[a, : out_ref.shape[1]].astype(jnp.bfloat16).T
            out_ref[low - lead : high - lead] = out[low - n * width : high - n * width]


def normalize(series, begin, end):
    subjects, duration, slab = series.shape
    body = duration // LANES * LANES
    low, high = begin // LANES * LANES, min(-(-end // LANES) * LANES, slab)
    lanes = high - low
    width = LANES if lanes % LANES == 0 else lanes
    widths = [body + LANES] + [body] * (subjects - 1)
    return pl.pallas_call(
        functools.partial(normalize_kernel, begin=low, lead=begin - low),
        in_specs=[pl.BlockSpec(memory_space=pltpu.HBM)],
        out_shape=[jax.ShapeDtypeStruct((end - begin, w), jnp.bfloat16) for w in widths],
        scratch_shapes=[
            pltpu.VMEM((subjects, duration, lanes), jnp.float32),
            pltpu.VMEM((subjects, body + LANES, width), jnp.float32),
            pltpu.SemaphoreType.DMA((subjects * (lanes // width),)),
        ],
        compiler_params=pltpu.CompilerParams(vmem_limit_bytes=48 * 2**20),
        cost_estimate=HINT,
    )(series)


def after(pieces, others, cost=HINT):
    def nothing(*refs):
        pass

    return pl.pallas_call(
        nothing,
        in_specs=[ANY] * (len(pieces) + len(others)),
        out_specs=[ANY] * len(pieces),
        out_shape=[jax.ShapeDtypeStruct(piece.shape, piece.dtype) for piece in pieces],
        input_output_aliases={i: i for i in range(len(pieces))},
        cost_estimate=cost,
    )(*pieces, *others)


def combine_kernel(*refs, starts, scale):
    *in_refs, out_ref = refs
    total = jnp.zeros(out_ref.shape, jnp.float32)
    for ref, start in zip(in_refs, starts):
        if start is None:
            total = total + ref[...].astype(jnp.float32)
    out_ref[...] = total * scale
    for ref, start in zip(in_refs, starts):
        if start is not None:
            here = pl.ds(start, ref.shape[1])
            out_ref[:, here] = out_ref[:, here] + ref[...].astype(jnp.float32) * scale


def combine(terms, starts, slab, columns, scale):
    step = max(d for d in range(16, 161, 16) if slab % d == 0)
    return pl.pallas_call(
        functools.partial(combine_kernel, starts=starts, scale=scale),
        grid=(slab // step,),
        in_specs=[pl.BlockSpec((step, term.shape[1]), lambda i: (i, 0)) for term in terms],
        out_specs=pl.BlockSpec((step, columns), lambda i: (i, 0)),
        out_shape=jax.ShapeDtypeStruct((slab, columns), jnp.float32),
        compiler_params=pltpu.CompilerParams(vmem_limit_bytes=48 * 2**20),
        cost_estimate=HINT,
    )(*terms)


def finish_kernel(part_ref, before_ref, out_ref, *, scale):
    out_ref[...] = before_ref[...] + part_ref[...].astype(jnp.float32) * scale


def finish(part, before, first, scale):
    slab = before.shape[0]
    width = math.gcd(part.shape[1], first)
    block = (slab, width)
    there = pl.BlockSpec(block, lambda i, j: (i, first // width + j))
    return pl.pallas_call(
        functools.partial(finish_kernel, scale=scale),
        grid=(slab // block[0], part.shape[1] // width),
        in_specs=[pl.BlockSpec(block, lambda i, j: (i, j)), there],
        out_specs=there,
        out_shape=jax.ShapeDtypeStruct(before.shape, jnp.float32),
        input_output_aliases={1: 0},
        cost_estimate=HINT,
    )(part, before)


def scores_kernel(
    source_ref, block_start_ref, place_ref, *refs, subject, targets, cuts, slab, granule, block_rows, chips, chunk, duration
):
    count = source_ref.shape[0]
    bodies, tails = refs[: 2 * count], refs[2 * count : 4 * count]
    own_rows, products_a, products_b, place_of, sems = refs[-5:]
    refs = refs[-5 - 2 * len(targets) : -5]
    out_refs, columns_refs = refs[: len(targets)], refs[len(targets) :]
    body = duration // LANES * LANES
    tail = duration - body
    for a in range(block_start_ref.shape[0]):
        place_of[block_start_ref[a] // block_rows] = a

    position, subj = place_ref[0], place_ref[1]
    chip, core = subj // 2, subj % 2
    wanted = [(position * slab, own_rows)]
    for (away, flip, first, _), columns_ref in zip(targets, columns_refs):
        owner = (chip + away) % chips * 2 + (core + flip) % 2
        wanted.append((owner * chunk + first, columns_ref))

    for slot in range(count):
        for half in range(2):
            piece = 2 * slot + half
            low = source_ref[slot] * slab + cuts[half]

            def start(g, _, piece=piece, low=low):
                stored = low + g * granule
                block = stored // block_rows
                row = place_of[block] * block_rows + (stored - block * block_rows)
                here = pl.ds(pl.multiple_of(g * granule, granule), granule)
                for n, (begin, to_ref) in enumerate(wanted):

                    @pl.when((row >= begin) & (row < begin + to_ref.shape[0]))
                    def _():
                        there = pl.ds(pl.multiple_of(row - begin, granule), granule)
                        if subject == 0:
                            pltpu.make_async_copy(tails[piece].at[here], to_ref.at[there], sems.at[n]).start()
                        else:
                            pltpu.make_async_copy(
                                bodies[piece].at[here], to_ref.at[there, :body], sems.at[n]
                            ).start()
                            pltpu.make_async_copy(
                                tails[piece].at[here, body:], to_ref.at[there, body:], sems.at[n]
                            ).start()

                return 0

            lax.fori_loop(0, (cuts[half + 1] - cuts[half]) // granule, start, 0)

    def arrived(n):
        to_ref = wanted[n][1]
        pltpu.make_async_copy(to_ref, to_ref, sems.at[n]).wait()

    arrived(0)
    lane = lax.broadcasted_iota(jnp.int32, (slab, LANES), 1)
    kept = (lane >= subject * tail) & (lane < (subject + 1) * tail)
    own_rows[:, body:] = jnp.where(kept, own_rows[:, body:].astype(jnp.float32), 0.0).astype(jnp.bfloat16)

    limit = clip_limit * duration
    width = products_a.shape[1]
    tiles = []
    for n, out_ref in enumerate(out_refs):
        tiles += [(n + 1, k, out_ref) for k in range(0, out_ref.shape[1], width)]
    buffers = (products_a, products_b)

    def multiply(i):
        n, k, _ = tiles[i]
        if k == 0:
            arrived(n)
        buffers[i % 2][...] = lax.dot_general(
            own_rows[...], wanted[n][1][pl.ds(k, width)], (((1,), (1,)), ((), ())), preferred_element_type=jnp.float32
        )

    def score(i):
        products = jnp.clip(buffers[i % 2][...], -limit, limit)
        fisher = 0.5 * (jnp.log(duration + products) - jnp.log(duration - products))
        tiles[i][2][:, pl.ds(tiles[i][1], width)] = fisher.astype(jnp.bfloat16)

    multiply(0)
    for i in range(1, len(tiles)):
        multiply(i)
        score(i - 1)
    score(len(tiles) - 1)


def scores(source, block_start, place, subject, targets, bodies, tails, cuts, window, chips, duration, late=()):
    slab = cuts[-1]
    block_rows = window // block_start.shape[0]
    chunk = window // (2 * chips)
    sizes = [columns for _, _, _, columns in targets]
    granule = math.gcd(*cuts, *sizes, *(first for _, _, first, _ in targets), block_rows)
    width = math.gcd(*sizes, 256)
    padded = tails[0].shape[1]
    smem = pl.BlockSpec(memory_space=pltpu.SMEM)
    return pl.pallas_call(
        functools.partial(
            scores_kernel,
            subject=subject,
            targets=targets,
            cuts=cuts,
            slab=slab,
            granule=granule,
            block_rows=block_rows,
            chips=chips,
            chunk=chunk,
            duration=duration,
        ),
        in_specs=[smem, smem, smem] + [ANY] * (2 * len(tails) + len(late)),
        out_shape=[jax.ShapeDtypeStruct((slab, columns), jnp.bfloat16) for columns in sizes],
        scratch_shapes=[pltpu.VMEM((columns, padded), jnp.bfloat16) for columns in sizes]
        + [
            pltpu.VMEM((slab, padded), jnp.bfloat16),
            pltpu.VMEM((slab, width), jnp.float32),
            pltpu.VMEM((slab, width), jnp.float32),
            pltpu.SMEM((block_start.shape[0],), jnp.int32),
            pltpu.SemaphoreType.DMA((1 + len(targets),)),
        ],
        compiler_params=pltpu.CompilerParams(vmem_limit_bytes=48 * 2**20),
        cost_estimate=HINT,
    )(source, block_start, place, *bodies, *tails, *late)


def on_device(series, block_start):
    local_subjects, slab, duration = series.shape
    rows, cols = lax.axis_size("row"), lax.axis_size("col")
    count = rows * cols
    window = count * slab
    subjs = lax.axis_size("subj")
    chips = subjs // 2
    cuts = (0, slab // 2, slab)
    order = cycle(rows, cols)
    onward = [(order[i], order[(i + 1) % count]) for i in range(count)]
    backward = [(b, a) for a, b in onward]
    reach = count // 2
    offsets = [0]
    for d in range(1, reach):
        offsets += [d, -d]
    offsets.append(reach)
    table = np.zeros((count, count), np.int32)
    for i, device in enumerate(order):
        table[device] = [order[(i - d) % count] for d in offsets]
    position = lax.axis_index(SLABS)
    source = jnp.asarray(table)[position]
    place = jnp.stack([position, lax.axis_index("subj")]).astype(jnp.int32)

    def gather(a, gate=None):
        got = [[normed[0][a], normed[1][a]]]
        for d in range(1, reach):
            ahead, behind = got[max(2 * d - 3, 0)], got[max(2 * d - 2, 0)]
            got += [[None, None], [None, None]]
            for half in range(2):
                waits = gate(d, half, got) if gate else ()
                if d > 1:
                    ahead[half], behind[half] = after([ahead[half], behind[half]], waits)
                elif waits:
                    (ahead[half],) = after([ahead[half]], waits)
                got[-2][half] = lax.ppermute(ahead[half], SLABS, onward)
                got[-1][half] = lax.ppermute(behind[half], SLABS, backward)
        last = []
        for half, side, way in ((0, -2, onward), (1, -1, backward)):
            waits = gate(reach, half, got) if gate else ()
            (got[side][half],) = after([got[side][half]], [got[-3 - side][half], *waits])
            last.append(lax.ppermute(got[side][half], SLABS, way))
        got.append(last)
        return got

    def flat(pairs):
        return [piece for pair in pairs for piece in pair]

    swap = [(s, s ^ 1) for s in range(subjs)]
    columns = jnp.swapaxes(series, 1, 2)
    normed = [normalize(columns, cuts[half], cuts[half + 1]) for half in range(2)]
    everything = [gather(0)]
    chunk = window // subjs
    width = math.gcd(chunk, 256)
    early = -(-chunk // width // 2) * width
    cut = ((0, early), (early, chunk - early))
    aways = [*range(1, chips), 0]

    def share(a, targets, late=()):
        bodies, tails = flat(everything[a]), flat(everything[0])
        return scores(source, block_start, place, a, targets, bodies, tails, cuts, window, chips, duration, late)

    def cross(other, hold=()):
        if hold:
            (other,) = after([other], hold)
        return lax.ppermute(other, "subj", swap)

    def send(summed, d, cost, before=()):
        there = lax.ppermute(summed, "subj", [(s, (s + 2 * d) % subjs) for s in range(subjs)])
        return after([there], before, cost)[0]

    def added(same, crossed):
        return (same.astype(jnp.float32) + crossed.astype(jnp.float32)).astype(jnp.bfloat16)

    terms, starts = [], []
    for a in range(1, local_subjects):
        shares, sums, gone = [], [], []

        def gate(d, half, got, a=a, before=everything[-1], shares=shares, sums=sums, gone=gone):
            if d == 1:
                return [before[-3][half], before[-2][half]]
            n = d - 2
            if half == 0 and n < chips - 1:
                late = [*got[2 * n - 1], *got[2 * n]] if n else ()
                shares.append(share(a - 1, [(aways[n], flip, *part) for part in cut for flip in (0, 1)], late))
            waits = [shares[n][0]] if n < chips - 1 else []
            if d < reach:
                return waits
            if half == 0:
                for m, (away, arrays) in enumerate(zip(aways[:-1], shares)):
                    hold = [got[2 * m + 1][0], got[2 * m + 2][0]]
                    for (start, _), same, other in zip(cut, arrays[::2], arrays[1::2]):
                        sums.append(added(same, cross(other, hold)))
                        gone.append(send(sums[-1], away, SHORT))
                        starts.append(start)
                return sums
            return [*sums, *gone[1::2]]

        everything.append(gather(a, gate))
        terms += gone
        same, other = share(a - 1, [(0, flip, 0, chunk) for flip in (0, 1)], [everything[a][-3][0], everything[a][-2][1]])
        gone.append(same)
        terms += [same, cross(other)]
        starts += [None, None]
    last = local_subjects - 1
    scale = 1 / (local_subjects * subjs)
    late = gone
    for d in aways[:-2]:
        same, other = share(last, [(d, 0, 0, chunk), (d, 1, 0, chunk)], late)
        late = [added(same, cross(other))]
        terms.append(send(late[0], d, LONG))
        starts.append(None)
    d = aways[-2]
    same, other = share(last, [(d, 0, 0, early), (d, 1, 0, early)], late)
    leading = added(same, cross(other))
    rest = chunk - early
    other, same, others = share(last, [(d, 1, early, rest), (d, 0, early, rest), (0, 1, 0, chunk)], [leading])
    summed = added(same, cross(other))
    (same,) = share(last, [(0, 0, 0, chunk)], [summed])
    there = send(leading, d, LONG)
    terms += [same, cross(others, [there, summed]), there]
    starts += [None, None, 0]
    out = combine(terms, starts, slab, chunk, scale)
    return finish(send(summed, d, LONG, [out]), out, early, scale)


def solution(mesh):
    return jax.shard_map(
        on_device,
        mesh=mesh,
        in_specs=(P("subj", SLABS, None), P()),
        out_specs=P(SLABS, "subj"),
        check_vma=False,
    )
```

```python
import functools
import math

import jax
import jax.numpy as jnp
import numpy as np
from jax import lax
from jax.experimental import pallas as pl
from jax.experimental.pallas import tpu as pltpu
from jax.sharding import PartitionSpec as P

clip_limit = 0.99
epsilon = 1e-05
SLABS = ("row", "col")
LANES = 128
HINT = pl.CostEstimate(flops=0, bytes_accessed=1024, transcendentals=0)
SHORT = pl.CostEstimate(flops=0, bytes_accessed=1024, transcendentals=0)
LONG = pl.CostEstimate(flops=0, bytes_accessed=2**27, transcendentals=0)
ANY = pl.BlockSpec(memory_space=pl.ANY)


def cycle(rows, cols):
    if cols == 1:
        return list(range(rows))
    walk = [(r, 0) for r in range(rows)]
    for i, r in enumerate(reversed(range(rows))):
        back = list(range(1, cols))
        walk += [(r, c) for c in (back if i % 2 == 0 else back[::-1])]
    return [r * cols + c for r, c in walk]


def normalize_kernel(series_ref, first_ref, *refs, begin, lead):
    other_refs, (raw, columns, sems) = refs[:-3], refs[-3:]
    subjects, duration, lanes = raw.shape
    body = duration // LANES * LANES
    tail = duration - body
    rows = first_ref.shape[0]
    width = LANES if lanes % LANES == 0 else lanes
    steps = lanes // width

    def copy(i):
        a, here = i % subjects, pl.ds(i // subjects * width, width)
        there = pl.ds(begin + i // subjects * width, width)
        return pltpu.make_async_copy(series_ref.at[a, :, there], raw.at[a, :, here], sems.at[i])

    for i in range(subjects * steps):
        copy(i).start()
    columns[:, duration + (subjects - 1) * tail :] = jnp.zeros(
        (subjects, LANES - subjects * tail, width), jnp.float32
    )
    for n in range(steps):
        here = pl.ds(n * width, width)
        for a in range(subjects):
            copy(n * subjects + a).wait()
            values = raw[a, :, here]
            center = jnp.mean(values, axis=0, keepdims=True)
            away = values - center
            spread = jnp.mean(away * away, axis=0, keepdims=True)
            normed = away * lax.rsqrt(spread + epsilon)
            columns[a, :duration] = normed
            if a:
                columns[0, duration + (a - 1) * tail : duration + a * tail] = normed[body:]
        low, high = max(n * width, lead), min((n + 1) * width, lead + rows)
        for a, out_ref in enumerate((first_ref, *other_refs)):
            out = columns[a, : out_ref.shape[1]].astype(jnp.bfloat16).T
            out_ref[low - lead : high - lead] = out[low - n * width : high - n * width]


def normalize(series, begin, end):
    subjects, duration, slab = series.shape
    body = duration // LANES * LANES
    low, high = begin // LANES * LANES, min(-(-end // LANES) * LANES, slab)
    lanes = high - low
    width = LANES if lanes % LANES == 0 else lanes
    widths = [body + LANES] + [body] * (subjects - 1)
    return pl.pallas_call(
        functools.partial(normalize_kernel, begin=low, lead=begin - low),
        in_specs=[pl.BlockSpec(memory_space=pltpu.HBM)],
        out_shape=[jax.ShapeDtypeStruct((end - begin, w), jnp.bfloat16) for w in widths],
        scratch_shapes=[
            pltpu.VMEM((subjects, duration, lanes), jnp.float32),
            pltpu.VMEM((subjects, body + LANES, width), jnp.float32),
            pltpu.SemaphoreType.DMA((subjects * (lanes // width),)),
        ],
        compiler_params=pltpu.CompilerParams(vmem_limit_bytes=48 * 2**20),
        cost_estimate=HINT,
    )(series)


def after(pieces, others, cost=HINT):
    def nothing(*refs):
        pass

    return pl.pallas_call(
        nothing,
        in_specs=[ANY] * (len(pieces) + len(others)),
        out_specs=[ANY] * len(pieces),
        out_shape=[jax.ShapeDtypeStruct(piece.shape, piece.dtype) for piece in pieces],
        input_output_aliases={i: i for i in range(len(pieces))},
        cost_estimate=cost,
    )(*pieces, *others)


def combine_kernel(*refs, starts, scale):
    *in_refs, out_ref = refs
    total = jnp.zeros(out_ref.shape, jnp.float32)
    for ref, start in zip(in_refs, starts):
        if start is None:
            total = total + ref[...].astype(jnp.float32)
    out_ref[...] = total * scale
    for ref, start in zip(in_refs, starts):
        if start is not None:
            here = pl.ds(start, ref.shape[1])
            out_ref[:, here] = out_ref[:, here] + ref[...].astype(jnp.float32) * scale


def combine(terms, starts, slab, columns, scale):
    step = max(d for d in range(16, 161, 16) if slab % d == 0)
    return pl.pallas_call(
        functools.partial(combine_kernel, starts=starts, scale=scale),
        grid=(slab // step,),
        in_specs=[pl.BlockSpec((step, term.shape[1]), lambda i: (i, 0)) for term in terms],
        out_specs=pl.BlockSpec((step, columns), lambda i: (i, 0)),
        out_shape=jax.ShapeDtypeStruct((slab, columns), jnp.float32),
        compiler_params=pltpu.CompilerParams(vmem_limit_bytes=48 * 2**20),
        cost_estimate=HINT,
    )(*terms)


def finish_kernel(part_ref, before_ref, out_ref, *, scale):
    out_ref[...] = before_ref[...] + part_ref[...].astype(jnp.float32) * scale


def finish(part, before, first, scale):
    slab = before.shape[0]
    width = math.gcd(part.shape[1], first)
    block = (slab, width)
    there = pl.BlockSpec(block, lambda i, j: (i, first // width + j))
    return pl.pallas_call(
        functools.partial(finish_kernel, scale=scale),
        grid=(slab // block[0], part.shape[1] // width),
        in_specs=[pl.BlockSpec(block, lambda i, j: (i, j)), there],
        out_specs=there,
        out_shape=jax.ShapeDtypeStruct(before.shape, jnp.float32),
        input_output_aliases={1: 0},
        cost_estimate=HINT,
    )(part, before)


def scores_kernel(
    source_ref, block_start_ref, place_ref, *refs, subject, targets, cuts, slab, granule, block_rows, chips, chunk, duration
):
    count = source_ref.shape[0]
    bodies, tails = refs[: 2 * count], refs[2 * count : 4 * count]
    own_rows, products_a, products_b, place_of, sems = refs[-5:]
    refs = refs[-5 - 2 * len(targets) : -5]
    out_refs, columns_refs = refs[: len(targets)], refs[len(targets) :]
    body = duration // LANES * LANES
    tail = duration - body
    for a in range(block_start_ref.shape[0]):
        place_of[block_start_ref[a] // block_rows] = a

    position, subj = place_ref[0], place_ref[1]
    chip, core = subj // 2, subj % 2
    wanted = [(position * slab, own_rows)]
    for (away, flip, first, _), columns_ref in zip(targets, columns_refs):
        owner = (chip + away) % chips * 2 + (core + flip) % 2
        wanted.append((owner * chunk + first, columns_ref))

    for slot in range(count):
        for half in range(2):
            piece = 2 * slot + half
            low = source_ref[slot] * slab + cuts[half]

            def start(g, _, piece=piece, low=low):
                stored = low + g * granule
                block = stored // block_rows
                row = place_of[block] * block_rows + (stored - block * block_rows)
                here = pl.ds(pl.multiple_of(g * granule, granule), granule)
                for n, (begin, to_ref) in enumerate(wanted):

                    @pl.when((row >= begin) & (row < begin + to_ref.shape[0]))
                    def _():
                        there = pl.ds(pl.multiple_of(row - begin, granule), granule)
                        if subject == 0:
                            pltpu.make_async_copy(tails[piece].at[here], to_ref.at[there], sems.at[n]).start()
                        else:
                            pltpu.make_async_copy(
                                bodies[piece].at[here], to_ref.at[there, :body], sems.at[n]
                            ).start()
                            pltpu.make_async_copy(
                                tails[piece].at[here, body:], to_ref.at[there, body:], sems.at[n]
                            ).start()

                return 0

            lax.fori_loop(0, (cuts[half + 1] - cuts[half]) // granule, start, 0)

    def arrived(n):
        to_ref = wanted[n][1]
        pltpu.make_async_copy(to_ref, to_ref, sems.at[n]).wait()

    arrived(0)
    lane = lax.broadcasted_iota(jnp.int32, (slab, LANES), 1)
    kept = (lane >= subject * tail) & (lane < (subject + 1) * tail)
    own_rows[:, body:] = jnp.where(kept, own_rows[:, body:].astype(jnp.float32), 0.0).astype(jnp.bfloat16)

    limit = clip_limit * duration
    widest = products_a.shape[1]
    tiles = []
    for n, out_ref in enumerate(out_refs):
        columns = out_ref.shape[1]
        tiles += [(n + 1, k, min(widest, columns - k), out_ref) for k in range(0, columns, widest)]
    buffers = (products_a, products_b)

    def multiply(i):
        n, k, width, _ = tiles[i]
        if k == 0:
            arrived(n)
        buffers[i % 2][:, :width] = lax.dot_general(
            own_rows[...], wanted[n][1][pl.ds(k, width)], (((1,), (1,)), ((), ())), preferred_element_type=jnp.float32
        )

    def score(i):
        _, k, width, out_ref = tiles[i]
        products = jnp.clip(buffers[i % 2][:, :width], -limit, limit)
        fisher = 0.5 * (jnp.log(duration + products) - jnp.log(duration - products))
        out_ref[:, pl.ds(k, width)] = fisher.astype(jnp.bfloat16)

    multiply(0)
    for i in range(1, len(tiles)):
        multiply(i)
        score(i - 1)
    score(len(tiles) - 1)


def scores(source, block_start, place, subject, targets, bodies, tails, cuts, window, chips, duration, late=()):
    slab = cuts[-1]
    block_rows = window // block_start.shape[0]
    chunk = window // (2 * chips)
    sizes = [columns for _, _, _, columns in targets]
    granule = math.gcd(*cuts, *sizes, *(first for _, _, first, _ in targets), block_rows)
    widest = min(512, *sizes)
    padded = tails[0].shape[1]
    smem = pl.BlockSpec(memory_space=pltpu.SMEM)
    return pl.pallas_call(
        functools.partial(
            scores_kernel,
            subject=subject,
            targets=targets,
            cuts=cuts,
            slab=slab,
            granule=granule,
            block_rows=block_rows,
            chips=chips,
            chunk=chunk,
            duration=duration,
        ),
        in_specs=[smem, smem, smem] + [ANY] * (2 * len(tails) + len(late)),
        out_shape=[jax.ShapeDtypeStruct((slab, columns), jnp.bfloat16) for columns in sizes],
        scratch_shapes=[pltpu.VMEM((columns, padded), jnp.bfloat16) for columns in sizes]
        + [
            pltpu.VMEM((slab, padded), jnp.bfloat16),
            pltpu.VMEM((slab, widest), jnp.float32),
            pltpu.VMEM((slab, widest), jnp.float32),
            pltpu.SMEM((block_start.shape[0],), jnp.int32),
            pltpu.SemaphoreType.DMA((1 + len(targets),)),
        ],
        compiler_params=pltpu.CompilerParams(vmem_limit_bytes=48 * 2**20),
        cost_estimate=HINT,
    )(source, block_start, place, *bodies, *tails, *late)


def on_device(series, block_start):
    local_subjects, slab, duration = series.shape
    rows, cols = lax.axis_size("row"), lax.axis_size("col")
    count = rows * cols
    window = count * slab
    subjs = lax.axis_size("subj")
    chips = subjs // 2
    cuts = (0, slab // 2, slab)
    order = cycle(rows, cols)
    onward = [(order[i], order[(i + 1) % count]) for i in range(count)]
    backward = [(b, a) for a, b in onward]
    reach = count // 2
    offsets = [0]
    for d in range(1, reach):
        offsets += [d, -d]
    offsets.append(reach)
    table = np.zeros((count, count), np.int32)
    for i, device in enumerate(order):
        table[device] = [order[(i - d) % count] for d in offsets]
    position = lax.axis_index(SLABS)
    source = jnp.asarray(table)[position]
    place = jnp.stack([position, lax.axis_index("subj")]).astype(jnp.int32)

    def gather(a, gate=None):
        got = [[normed[0][a], normed[1][a]]]
        for d in range(1, reach):
            ahead, behind = got[max(2 * d - 3, 0)], got[max(2 * d - 2, 0)]
            got += [[None, None], [None, None]]
            for half in range(2):
                waits = gate(d, half, got) if gate else ()
                if d > 1:
                    ahead[half], behind[half] = after([ahead[half], behind[half]], waits)
                elif waits:
                    (ahead[half],) = after([ahead[half]], waits)
                got[-2][half] = lax.ppermute(ahead[half], SLABS, onward)
                got[-1][half] = lax.ppermute(behind[half], SLABS, backward)
        last = []
        for half, side, way in ((0, -2, onward), (1, -1, backward)):
            waits = gate(reach, half, got) if gate else ()
            (got[side][half],) = after([got[side][half]], [got[-3 - side][half], *waits])
            last.append(lax.ppermute(got[side][half], SLABS, way))
        got.append(last)
        return got

    def flat(pairs):
        return [piece for pair in pairs for piece in pair]

    swap = [(s, s ^ 1) for s in range(subjs)]
    columns = jnp.swapaxes(series, 1, 2)
    normed = [normalize(columns, cuts[half], cuts[half + 1]) for half in range(2)]
    everything = [gather(0)]
    chunk = window // subjs
    width = math.gcd(chunk, 256)
    early = -(-chunk // width // 2) * width
    cut = ((0, early), (early, chunk - early))
    aways = [*range(1, chips), 0]

    def share(a, targets, late=()):
        bodies, tails = flat(everything[a]), flat(everything[0])
        return scores(source, block_start, place, a, targets, bodies, tails, cuts, window, chips, duration, late)

    def cross(other, hold=()):
        if hold:
            (other,) = after([other], hold)
        return lax.ppermute(other, "subj", swap)

    def send(summed, d, cost, before=()):
        there = lax.ppermute(summed, "subj", [(s, (s + 2 * d) % subjs) for s in range(subjs)])
        return after([there], before, cost)[0]

    def added(same, crossed):
        return (same.astype(jnp.float32) + crossed.astype(jnp.float32)).astype(jnp.bfloat16)

    terms, starts = [], []
    for a in range(1, local_subjects):
        shares, sums, gone = [], [], []

        def gate(d, half, got, a=a, before=everything[-1], shares=shares, sums=sums, gone=gone):
            if d == 1:
                return [before[-3][half], before[-2][half]]
            n = d - 2
            if half == 0 and n < chips - 1:
                late = [*got[2 * n - 1], *got[2 * n]] if n else ()
                shares.append(share(a - 1, [(aways[n], flip, *part) for part in cut for flip in (0, 1)], late))
            waits = [shares[n][0]] if n < chips - 1 else []
            if d < reach:
                return waits
            if half == 0:
                for m, (away, arrays) in enumerate(zip(aways[:-1], shares)):
                    hold = [got[2 * m + 1][0], got[2 * m + 2][0]]
                    for (start, _), same, other in zip(cut, arrays[::2], arrays[1::2]):
                        sums.append(added(same, cross(other, hold)))
                        gone.append(send(sums[-1], away, SHORT))
                        starts.append(start)
                return sums
            return [*sums, *gone[1::2]]

        everything.append(gather(a, gate))
        terms += gone
        same, other = share(a - 1, [(0, flip, 0, chunk) for flip in (0, 1)], [everything[a][-3][0], everything[a][-2][1]])
        gone.append(same)
        terms += [same, cross(other)]
        starts += [None, None]
    last = local_subjects - 1
    scale = 1 / (local_subjects * subjs)
    late = gone
    for d in aways[:-2]:
        same, other = share(last, [(d, 0, 0, chunk), (d, 1, 0, chunk)], late)
        late = [added(same, cross(other))]
        terms.append(send(late[0], d, LONG))
        starts.append(None)
    d = aways[-2]
    same, other = share(last, [(d, 0, 0, early), (d, 1, 0, early)], late)
    leading = added(same, cross(other))
    rest = chunk - early
    other, same, others = share(last, [(d, 1, early, rest), (d, 0, early, rest), (0, 1, 0, chunk)], [leading])
    summed = added(same, cross(other))
    (same,) = share(last, [(0, 0, 0, chunk)], [summed])
    there = send(leading, d, LONG)
    terms += [same, cross(others, [there, summed]), there]
    starts += [None, None, 0]
    out = combine(terms, starts, slab, chunk, scale)
    return finish(send(summed, d, LONG, [out]), out, early, scale)


def solution(mesh):
    return jax.shard_map(
        on_device,
        mesh=mesh,
        in_specs=(P("subj", SLABS, None), P()),
        out_specs=P(SLABS, "subj"),
        check_vma=False,
    )
```

```python
import functools
import math

import jax
import jax.numpy as jnp
import numpy as np
from jax import lax
from jax.experimental import pallas as pl
from jax.experimental.pallas import tpu as pltpu
from jax.sharding import PartitionSpec as P

clip_limit = 0.99
epsilon = 1e-05
SLABS = ("row", "col")
LANES = 128
HINT = pl.CostEstimate(flops=0, bytes_accessed=1024, transcendentals=0)
SHORT = pl.CostEstimate(flops=0, bytes_accessed=1024, transcendentals=0)
LONG = pl.CostEstimate(flops=0, bytes_accessed=2**27, transcendentals=0)
ANY = pl.BlockSpec(memory_space=pl.ANY)


def cycle(rows, cols):
    if cols == 1:
        return list(range(rows))
    walk = [(r, 0) for r in range(rows)]
    for i, r in enumerate(reversed(range(rows))):
        back = list(range(1, cols))
        walk += [(r, c) for c in (back if i % 2 == 0 else back[::-1])]
    return [r * cols + c for r, c in walk]


def normalize_kernel(series_ref, first_ref, *refs, begin, lead):
    other_refs, (raw, columns, sems) = refs[:-3], refs[-3:]
    subjects, duration, lanes = raw.shape
    body = duration // LANES * LANES
    tail = duration - body
    rows = first_ref.shape[0]
    width = LANES if lanes % LANES == 0 else lanes
    steps = lanes // width

    def copy(i):
        a, here = i % subjects, pl.ds(i // subjects * width, width)
        there = pl.ds(begin + i // subjects * width, width)
        return pltpu.make_async_copy(series_ref.at[a, :, there], raw.at[a, :, here], sems.at[i])

    for i in range(subjects * steps):
        copy(i).start()
    columns[:, duration + (subjects - 1) * tail :] = jnp.zeros(
        (subjects, LANES - subjects * tail, width), jnp.float32
    )
    for n in range(steps):
        here = pl.ds(n * width, width)
        for a in range(subjects):
            copy(n * subjects + a).wait()
            values = raw[a, :, here]
            center = jnp.mean(values, axis=0, keepdims=True)
            away = values - center
            spread = jnp.mean(away * away, axis=0, keepdims=True)
            normed = away * lax.rsqrt(spread + epsilon)
            columns[a, :duration] = normed
            if a:
                columns[0, duration + (a - 1) * tail : duration + a * tail] = normed[body:]
        low, high = max(n * width, lead), min((n + 1) * width, lead + rows)
        for a, out_ref in enumerate((first_ref, *other_refs)):
            out = columns[a, : out_ref.shape[1]].astype(jnp.bfloat16).T
            out_ref[low - lead : high - lead] = out[low - n * width : high - n * width]


def normalize(series, begin, end):
    subjects, duration, slab = series.shape
    body = duration // LANES * LANES
    low, high = begin // LANES * LANES, min(-(-end // LANES) * LANES, slab)
    lanes = high - low
    width = LANES if lanes % LANES == 0 else lanes
    widths = [body + LANES] + [body] * (subjects - 1)
    return pl.pallas_call(
        functools.partial(normalize_kernel, begin=low, lead=begin - low),
        in_specs=[pl.BlockSpec(memory_space=pltpu.HBM)],
        out_shape=[jax.ShapeDtypeStruct((end - begin, w), jnp.bfloat16) for w in widths],
        scratch_shapes=[
            pltpu.VMEM((subjects, duration, lanes), jnp.float32),
            pltpu.VMEM((subjects, body + LANES, width), jnp.float32),
            pltpu.SemaphoreType.DMA((subjects * (lanes // width),)),
        ],
        compiler_params=pltpu.CompilerParams(vmem_limit_bytes=48 * 2**20),
        cost_estimate=HINT,
    )(series)


def after(pieces, others, cost=HINT):
    def nothing(*refs):
        pass

    return pl.pallas_call(
        nothing,
        in_specs=[ANY] * (len(pieces) + len(others)),
        out_specs=[ANY] * len(pieces),
        out_shape=[jax.ShapeDtypeStruct(piece.shape, piece.dtype) for piece in pieces],
        input_output_aliases={i: i for i in range(len(pieces))},
        cost_estimate=cost,
    )(*pieces, *others)


def combine_kernel(*refs, starts, width, scale):
    *in_refs, out_ref = refs
    for k in range(0, out_ref.shape[1], width):
        total = jnp.zeros((out_ref.shape[0], width), jnp.float32)
        for ref, start in zip(in_refs, starts):
            if start <= k < start + ref.shape[1]:
                total = total + ref[:, pl.ds(k - start, width)].astype(jnp.float32)
        out_ref[:, pl.ds(k, width)] = total * scale


def combine(terms, starts, slab, columns, width, scale):
    step = max(d for d in range(16, 161, 16) if slab % d == 0)
    return pl.pallas_call(
        functools.partial(combine_kernel, starts=starts, width=width, scale=scale),
        grid=(slab // step,),
        in_specs=[pl.BlockSpec((step, term.shape[1]), lambda i: (i, 0)) for term in terms],
        out_specs=pl.BlockSpec((step, columns), lambda i: (i, 0)),
        out_shape=jax.ShapeDtypeStruct((slab, columns), jnp.float32),
        compiler_params=pltpu.CompilerParams(vmem_limit_bytes=48 * 2**20),
        cost_estimate=HINT,
    )(*terms)


def finish_kernel(part_ref, before_ref, out_ref, *, scale):
    out_ref[...] = before_ref[...] + part_ref[...].astype(jnp.float32) * scale


def finish(part, before, first, scale):
    slab = before.shape[0]
    width = math.gcd(part.shape[1], first)
    block = (slab, width)
    there = pl.BlockSpec(block, lambda i, j: (i, first // width + j))
    return pl.pallas_call(
        functools.partial(finish_kernel, scale=scale),
        grid=(slab // block[0], part.shape[1] // width),
        in_specs=[pl.BlockSpec(block, lambda i, j: (i, j)), there],
        out_specs=there,
        out_shape=jax.ShapeDtypeStruct(before.shape, jnp.float32),
        input_output_aliases={1: 0},
        cost_estimate=HINT,
    )(part, before)


def scores_kernel(
    source_ref, block_start_ref, place_ref, *refs, subject, targets, cuts, slab, granule, block_rows, chips, chunk, duration
):
    count = source_ref.shape[0]
    bodies, tails = refs[: 2 * count], refs[2 * count : 4 * count]
    own_rows, products_a, products_b, place_of, sems = refs[-5:]
    refs = refs[-5 - 2 * len(targets) : -5]
    out_refs, columns_refs = refs[: len(targets)], refs[len(targets) :]
    body = duration // LANES * LANES
    tail = duration - body
    for a in range(block_start_ref.shape[0]):
        place_of[block_start_ref[a] // block_rows] = a

    position, subj = place_ref[0], place_ref[1]
    chip, core = subj // 2, subj % 2
    wanted = [(position * slab, own_rows)]
    for (away, flip, first, _), columns_ref in zip(targets, columns_refs):
        owner = (chip + away) % chips * 2 + (core + flip) % 2
        wanted.append((owner * chunk + first, columns_ref))

    for slot in range(count):
        for half in range(2):
            piece = 2 * slot + half
            low = source_ref[slot] * slab + cuts[half]

            def start(g, _, piece=piece, low=low):
                stored = low + g * granule
                block = stored // block_rows
                row = place_of[block] * block_rows + (stored - block * block_rows)
                here = pl.ds(pl.multiple_of(g * granule, granule), granule)
                for n, (begin, to_ref) in enumerate(wanted):

                    @pl.when((row >= begin) & (row < begin + to_ref.shape[0]))
                    def _():
                        there = pl.ds(pl.multiple_of(row - begin, granule), granule)
                        if subject == 0:
                            pltpu.make_async_copy(tails[piece].at[here], to_ref.at[there], sems.at[n]).start()
                        else:
                            pltpu.make_async_copy(
                                bodies[piece].at[here], to_ref.at[there, :body], sems.at[n]
                            ).start()
                            pltpu.make_async_copy(
                                tails[piece].at[here, body:], to_ref.at[there, body:], sems.at[n]
                            ).start()

                return 0

            lax.fori_loop(0, (cuts[half + 1] - cuts[half]) // granule, start, 0)

    def arrived(n):
        to_ref = wanted[n][1]
        pltpu.make_async_copy(to_ref, to_ref, sems.at[n]).wait()

    arrived(0)
    lane = lax.broadcasted_iota(jnp.int32, (slab, LANES), 1)
    kept = (lane >= subject * tail) & (lane < (subject + 1) * tail)
    own_rows[:, body:] = jnp.where(kept, own_rows[:, body:].astype(jnp.float32), 0.0).astype(jnp.bfloat16)

    limit = clip_limit * duration
    widest = products_a.shape[1]
    tiles = []
    for n, out_ref in enumerate(out_refs):
        columns = out_ref.shape[1]
        tiles += [(n + 1, k, min(widest, columns - k), out_ref) for k in range(0, columns, widest)]
    buffers = (products_a, products_b)

    def multiply(i):
        n, k, width, _ = tiles[i]
        if k == 0:
            arrived(n)
        buffers[i % 2][:, :width] = lax.dot_general(
            own_rows[...], wanted[n][1][pl.ds(k, width)], (((1,), (1,)), ((), ())), preferred_element_type=jnp.float32
        )

    def score(i):
        _, k, width, out_ref = tiles[i]
        products = jnp.clip(buffers[i % 2][:, :width], -limit, limit)
        fisher = 0.5 * (jnp.log(duration + products) - jnp.log(duration - products))
        out_ref[:, pl.ds(k, width)] = fisher.astype(jnp.bfloat16)

    multiply(0)
    for i in range(1, len(tiles)):
        multiply(i)
        score(i - 1)
    score(len(tiles) - 1)


def scores(source, block_start, place, subject, targets, bodies, tails, cuts, window, chips, duration, late=()):
    slab = cuts[-1]
    block_rows = window // block_start.shape[0]
    chunk = window // (2 * chips)
    sizes = [columns for _, _, _, columns in targets]
    granule = math.gcd(*cuts, *sizes, *(first for _, _, first, _ in targets), block_rows)
    widest = min(512, *sizes)
    padded = tails[0].shape[1]
    smem = pl.BlockSpec(memory_space=pltpu.SMEM)
    return pl.pallas_call(
        functools.partial(
            scores_kernel,
            subject=subject,
            targets=targets,
            cuts=cuts,
            slab=slab,
            granule=granule,
            block_rows=block_rows,
            chips=chips,
            chunk=chunk,
            duration=duration,
        ),
        in_specs=[smem, smem, smem] + [ANY] * (2 * len(tails) + len(late)),
        out_shape=[jax.ShapeDtypeStruct((slab, columns), jnp.bfloat16) for columns in sizes],
        scratch_shapes=[pltpu.VMEM((columns, padded), jnp.bfloat16) for columns in sizes]
        + [
            pltpu.VMEM((slab, padded), jnp.bfloat16),
            pltpu.VMEM((slab, widest), jnp.float32),
            pltpu.VMEM((slab, widest), jnp.float32),
            pltpu.SMEM((block_start.shape[0],), jnp.int32),
            pltpu.SemaphoreType.DMA((1 + len(targets),)),
        ],
        compiler_params=pltpu.CompilerParams(vmem_limit_bytes=48 * 2**20),
        cost_estimate=HINT,
    )(source, block_start, place, *bodies, *tails, *late)


def on_device(series, block_start):
    local_subjects, slab, duration = series.shape
    rows, cols = lax.axis_size("row"), lax.axis_size("col")
    count = rows * cols
    window = count * slab
    subjs = lax.axis_size("subj")
    chips = subjs // 2
    cuts = (0, slab // 2, slab)
    order = cycle(rows, cols)
    onward = [(order[i], order[(i + 1) % count]) for i in range(count)]
    backward = [(b, a) for a, b in onward]
    reach = count // 2
    offsets = [0]
    for d in range(1, reach):
        offsets += [d, -d]
    offsets.append(reach)
    table = np.zeros((count, count), np.int32)
    for i, device in enumerate(order):
        table[device] = [order[(i - d) % count] for d in offsets]
    position = lax.axis_index(SLABS)
    source = jnp.asarray(table)[position]
    place = jnp.stack([position, lax.axis_index("subj")]).astype(jnp.int32)

    def gather(a, gate=None):
        got = [[normed[0][a], normed[1][a]]]
        for d in range(1, reach):
            ahead, behind = got[max(2 * d - 3, 0)], got[max(2 * d - 2, 0)]
            got += [[None, None], [None, None]]
            for half in range(2):
                waits = gate(d, half, got) if gate else ()
                if d > 1:
                    ahead[half], behind[half] = after([ahead[half], behind[half]], waits)
                elif waits:
                    (ahead[half],) = after([ahead[half]], waits)
                got[-2][half] = lax.ppermute(ahead[half], SLABS, onward)
                got[-1][half] = lax.ppermute(behind[half], SLABS, backward)
        last = []
        for half, side, way in ((0, -2, onward), (1, -1, backward)):
            waits = gate(reach, half, got) if gate else ()
            (got[side][half],) = after([got[side][half]], [got[-3 - side][half], *waits])
            last.append(lax.ppermute(got[side][half], SLABS, way))
        got.append(last)
        return got

    def flat(pairs):
        return [piece for pair in pairs for piece in pair]

    swap = [(s, s ^ 1) for s in range(subjs)]
    columns = jnp.swapaxes(series, 1, 2)
    normed = [normalize(columns, cuts[half], cuts[half + 1]) for half in range(2)]
    everything = [gather(0)]
    chunk = window // subjs
    width = math.gcd(chunk, 256)
    early = -(-chunk // width // 2) * width
    cut = ((0, early), (early, chunk - early))
    aways = [*range(1, chips), 0]

    def share(a, targets, late=()):
        bodies, tails = flat(everything[a]), flat(everything[0])
        return scores(source, block_start, place, a, targets, bodies, tails, cuts, window, chips, duration, late)

    def cross(other, hold=()):
        if hold:
            (other,) = after([other], hold)
        return lax.ppermute(other, "subj", swap)

    def send(summed, d, cost, before=()):
        there = lax.ppermute(summed, "subj", [(s, (s + 2 * d) % subjs) for s in range(subjs)])
        return after([there], before, cost)[0]

    def added(same, crossed):
        return (same.astype(jnp.float32) + crossed.astype(jnp.float32)).astype(jnp.bfloat16)

    terms, starts, pending = [], [], []
    for a in range(1, local_subjects):
        shares, sums, gone = [], [], []

        def gate(d, half, got, a=a, before=everything[-1], shares=shares, sums=sums, gone=gone):
            if d == 1:
                return [before[-3][half], before[-2][half]]
            n = d - 2
            if half == 0 and n < chips - 1:
                late = [*got[2 * n - 1], *got[2 * n]] if n else ()
                shares.append(share(a - 1, [(aways[n], flip, *part) for part in cut for flip in (0, 1)], late))
            waits = [shares[n][0]] if n < chips - 1 else []
            if d < reach:
                return waits
            if half == 0:
                for m, (away, arrays) in enumerate(zip(aways[:-1], shares)):
                    hold = [got[2 * m + 1][0], got[2 * m + 2][0]]
                    for (start, _), same, other in zip(cut, arrays[::2], arrays[1::2]):
                        sums.append(added(same, cross(other, hold)))
                        gone.append(send(sums[-1], away, SHORT))
                        starts.append(start)
                return sums
            return [*sums, *gone[1::2]]

        everything.append(gather(a, gate))
        terms += gone
        same, other = share(a - 1, [(0, flip, 0, chunk) for flip in (0, 1)], [everything[a][-3][0], everything[a][-2][1]])
        gone.append(same)
        pending.append(other)
        terms.append(same)
        starts.append(0)
    last = local_subjects - 1
    scale = 1 / (local_subjects * subjs)
    late = gone
    for d in aways[:-2]:
        same, other = share(last, [(d, 0, 0, chunk), (d, 1, 0, chunk)], late)
        late = [added(same, cross(other))]
        terms.append(send(late[0], d, LONG))
        starts.append(0)
    d = aways[-2]
    same, other = share(last, [(d, 0, 0, early), (d, 1, 0, early)], late)
    leading = added(same, cross(other))
    pieces = [(d, 1, k, width) for k in range(early, chunk, width)]
    ends = [*range(0, chunk - width, 2 * width), chunk - width, chunk]
    others = [(0, 1, k, end - k) for k, end in zip(ends, ends[1:])]
    arrays = share(last, [*pieces, (d, 0, early, chunk - early), *others], [leading])
    crossed = jnp.concatenate([cross(array) for array in arrays[: len(pieces)]], axis=1)
    summed = added(arrays[len(pieces)], crossed)
    (same,) = share(last, [(0, 0, 0, chunk)], [summed])
    there = send(leading, d, LONG, [same])
    terms += [same, there, *(cross(other, [summed]) for other in pending)]
    starts += [0 for _ in terms[len(starts) :]]
    for array, (_, _, start, _) in zip(arrays[len(pieces) + 1 :], others):
        terms.append(cross(array, [there] if start == others[-1][2] else ()))
        starts.append(start)
    out = combine(terms, starts, slab, chunk, width, scale)
    return finish(send(summed, d, LONG, [out]), out, early, scale)


def solution(mesh):
    return jax.shard_map(
        on_device,
        mesh=mesh,
        in_specs=(P("subj", SLABS, None), P()),
        out_specs=P(SLABS, "subj"),
        check_vma=False,
    )
```

```python
import functools
import math

import jax
import jax.numpy as jnp
import numpy as np
from jax import lax
from jax.experimental import pallas as pl
from jax.experimental.pallas import tpu as pltpu
from jax.sharding import PartitionSpec as P

clip_limit = 0.99
epsilon = 1e-05
SLABS = ("row", "col")
LANES = 128
HINT = pl.CostEstimate(flops=0, bytes_accessed=1024, transcendentals=0)
SHORT = pl.CostEstimate(flops=0, bytes_accessed=1024, transcendentals=0)
LONG = pl.CostEstimate(flops=0, bytes_accessed=2**27, transcendentals=0)
ANY = pl.BlockSpec(memory_space=pl.ANY)


def cycle(rows, cols):
    if cols == 1:
        return list(range(rows))
    walk = [(r, 0) for r in range(rows)]
    for i, r in enumerate(reversed(range(rows))):
        back = list(range(1, cols))
        walk += [(r, c) for c in (back if i % 2 == 0 else back[::-1])]
    return [r * cols + c for r, c in walk]


def normalize_kernel(series_ref, first_ref, *refs, begin, lead):
    other_refs, (raw, columns, sems) = refs[:-3], refs[-3:]
    subjects, duration, lanes = raw.shape
    body = duration // LANES * LANES
    tail = duration - body
    rows = first_ref.shape[0]
    width = LANES if lanes % LANES == 0 else lanes
    steps = lanes // width

    def copy(i):
        a, here = i % subjects, pl.ds(i // subjects * width, width)
        there = pl.ds(begin + i // subjects * width, width)
        return pltpu.make_async_copy(series_ref.at[a, :, there], raw.at[a, :, here], sems.at[i])

    for i in range(subjects * steps):
        copy(i).start()
    columns[:, duration + (subjects - 1) * tail :] = jnp.zeros(
        (subjects, LANES - subjects * tail, width), jnp.float32
    )
    for n in range(steps):
        here = pl.ds(n * width, width)
        for a in range(subjects):
            copy(n * subjects + a).wait()
            values = raw[a, :, here]
            center = jnp.mean(values, axis=0, keepdims=True)
            away = values - center
            spread = jnp.mean(away * away, axis=0, keepdims=True)
            normed = away * lax.rsqrt(spread + epsilon)
            columns[a, :duration] = normed
            if a:
                columns[0, duration + (a - 1) * tail : duration + a * tail] = normed[body:]
        low, high = max(n * width, lead), min((n + 1) * width, lead + rows)
        for a, out_ref in enumerate((first_ref, *other_refs)):
            out = columns[a, : out_ref.shape[1]].astype(jnp.bfloat16).T
            out_ref[low - lead : high - lead] = out[low - n * width : high - n * width]


def normalize(series, begin, end):
    subjects, duration, slab = series.shape
    body = duration // LANES * LANES
    low, high = begin // LANES * LANES, min(-(-end // LANES) * LANES, slab)
    lanes = high - low
    width = LANES if lanes % LANES == 0 else lanes
    widths = [body + LANES] + [body] * (subjects - 1)
    return pl.pallas_call(
        functools.partial(normalize_kernel, begin=low, lead=begin - low),
        in_specs=[pl.BlockSpec(memory_space=pltpu.HBM)],
        out_shape=[jax.ShapeDtypeStruct((end - begin, w), jnp.bfloat16) for w in widths],
        scratch_shapes=[
            pltpu.VMEM((subjects, duration, lanes), jnp.float32),
            pltpu.VMEM((subjects, body + LANES, width), jnp.float32),
            pltpu.SemaphoreType.DMA((subjects * (lanes // width),)),
        ],
        compiler_params=pltpu.CompilerParams(vmem_limit_bytes=48 * 2**20),
        cost_estimate=HINT,
    )(series)


def after(pieces, others, cost=HINT):
    def nothing(*refs):
        pass

    return pl.pallas_call(
        nothing,
        in_specs=[ANY] * (len(pieces) + len(others)),
        out_specs=[ANY] * len(pieces),
        out_shape=[jax.ShapeDtypeStruct(piece.shape, piece.dtype) for piece in pieces],
        input_output_aliases={i: i for i in range(len(pieces))},
        cost_estimate=cost,
    )(*pieces, *others)


def combine_kernel(*refs, starts, width, scale):
    *in_refs, out_ref = refs
    for k in range(0, out_ref.shape[1], width):
        total = jnp.zeros((out_ref.shape[0], width), jnp.float32)
        for ref, start in zip(in_refs, starts):
            if start <= k < start + ref.shape[1]:
                total = total + ref[:, pl.ds(k - start, width)].astype(jnp.float32)
        out_ref[:, pl.ds(k, width)] = total * scale


def combine(terms, starts, slab, columns, width, scale):
    step = max(d for d in range(16, 161, 16) if slab % d == 0)
    return pl.pallas_call(
        functools.partial(combine_kernel, starts=starts, width=width, scale=scale),
        grid=(slab // step,),
        in_specs=[pl.BlockSpec((step, term.shape[1]), lambda i: (i, 0)) for term in terms],
        out_specs=pl.BlockSpec((step, columns), lambda i: (i, 0)),
        out_shape=jax.ShapeDtypeStruct((slab, columns), jnp.float32),
        compiler_params=pltpu.CompilerParams(vmem_limit_bytes=48 * 2**20),
        cost_estimate=HINT,
    )(*terms)


def finish_kernel(part_ref, before_ref, out_ref, *, scale):
    out_ref[...] = before_ref[...] + part_ref[...].astype(jnp.float32) * scale


def finish(part, before, first, scale):
    slab = before.shape[0]
    width = math.gcd(part.shape[1], first)
    block = (slab, width)
    there = pl.BlockSpec(block, lambda i, j: (i, first // width + j))
    return pl.pallas_call(
        functools.partial(finish_kernel, scale=scale),
        grid=(slab // block[0], part.shape[1] // width),
        in_specs=[pl.BlockSpec(block, lambda i, j: (i, j)), there],
        out_specs=there,
        out_shape=jax.ShapeDtypeStruct(before.shape, jnp.float32),
        input_output_aliases={1: 0},
        cost_estimate=HINT,
    )(part, before)


def scores_kernel(
    source_ref, block_start_ref, place_ref, *refs, subject, targets, cuts, slab, granule, block_rows, chips, chunk, duration
):
    count = source_ref.shape[0]
    bodies, tails = refs[: 2 * count], refs[2 * count : 4 * count]
    own_rows, products_a, products_b, place_of, sems = refs[-5:]
    refs = refs[-5 - 2 * len(targets) : -5]
    out_refs, columns_refs = refs[: len(targets)], refs[len(targets) :]
    body = duration // LANES * LANES
    tail = duration - body
    for a in range(block_start_ref.shape[0]):
        place_of[block_start_ref[a] // block_rows] = a

    position, subj = place_ref[0], place_ref[1]
    chip, core = subj // 2, subj % 2
    wanted = [(position * slab, own_rows)]
    for (away, flip, first, _), columns_ref in zip(targets, columns_refs):
        owner = (chip + away) % chips * 2 + (core + flip) % 2
        wanted.append((owner * chunk + first, columns_ref))

    for slot in range(count):
        for half in range(2):
            piece = 2 * slot + half
            low = source_ref[slot] * slab + cuts[half]

            def start(g, _, piece=piece, low=low):
                stored = low + g * granule
                block = stored // block_rows
                row = place_of[block] * block_rows + (stored - block * block_rows)
                here = pl.ds(pl.multiple_of(g * granule, granule), granule)
                for n, (begin, to_ref) in enumerate(wanted):

                    @pl.when((row >= begin) & (row < begin + to_ref.shape[0]))
                    def _():
                        there = pl.ds(pl.multiple_of(row - begin, granule), granule)
                        if subject == 0:
                            pltpu.make_async_copy(tails[piece].at[here], to_ref.at[there], sems.at[n]).start()
                        else:
                            pltpu.make_async_copy(
                                bodies[piece].at[here], to_ref.at[there, :body], sems.at[n]
                            ).start()
                            pltpu.make_async_copy(
                                tails[piece].at[here, body:], to_ref.at[there, body:], sems.at[n]
                            ).start()

                return 0

            lax.fori_loop(0, (cuts[half + 1] - cuts[half]) // granule, start, 0)

    def arrived(n):
        to_ref = wanted[n][1]
        pltpu.make_async_copy(to_ref, to_ref, sems.at[n]).wait()

    arrived(0)
    lane = lax.broadcasted_iota(jnp.int32, (slab, LANES), 1)
    kept = (lane >= subject * tail) & (lane < (subject + 1) * tail)
    own_rows[:, body:] = jnp.where(kept, own_rows[:, body:].astype(jnp.float32), 0.0).astype(jnp.bfloat16)

    limit = clip_limit * duration
    widest = products_a.shape[1]
    tiles = []
    for n, out_ref in enumerate(out_refs):
        columns = out_ref.shape[1]
        tiles += [(n + 1, k, min(widest, columns - k), out_ref) for k in range(0, columns, widest)]
    buffers = (products_a, products_b)

    def multiply(i):
        n, k, width, _ = tiles[i]
        if k == 0:
            arrived(n)
        buffers[i % 2][:, :width] = lax.dot_general(
            own_rows[...], wanted[n][1][pl.ds(k, width)], (((1,), (1,)), ((), ())), preferred_element_type=jnp.float32
        )

    def score(i):
        _, k, width, out_ref = tiles[i]
        products = jnp.clip(buffers[i % 2][:, :width], -limit, limit)
        fisher = 0.5 * (jnp.log(duration + products) - jnp.log(duration - products))
        out_ref[:, pl.ds(k, width)] = fisher.astype(jnp.bfloat16)

    multiply(0)
    for i in range(1, len(tiles)):
        multiply(i)
        score(i - 1)
    score(len(tiles) - 1)


def scores(source, block_start, place, subject, targets, bodies, tails, cuts, window, chips, duration, late=()):
    slab = cuts[-1]
    block_rows = window // block_start.shape[0]
    chunk = window // (2 * chips)
    sizes = [columns for _, _, _, columns in targets]
    granule = math.gcd(*cuts, *sizes, *(first for _, _, first, _ in targets), block_rows)
    widest = min(512, *sizes)
    padded = tails[0].shape[1]
    smem = pl.BlockSpec(memory_space=pltpu.SMEM)
    return pl.pallas_call(
        functools.partial(
            scores_kernel,
            subject=subject,
            targets=targets,
            cuts=cuts,
            slab=slab,
            granule=granule,
            block_rows=block_rows,
            chips=chips,
            chunk=chunk,
            duration=duration,
        ),
        in_specs=[smem, smem, smem] + [ANY] * (2 * len(tails) + len(late)),
        out_shape=[jax.ShapeDtypeStruct((slab, columns), jnp.bfloat16) for columns in sizes],
        scratch_shapes=[pltpu.VMEM((columns, padded), jnp.bfloat16) for columns in sizes]
        + [
            pltpu.VMEM((slab, padded), jnp.bfloat16),
            pltpu.VMEM((slab, widest), jnp.float32),
            pltpu.VMEM((slab, widest), jnp.float32),
            pltpu.SMEM((block_start.shape[0],), jnp.int32),
            pltpu.SemaphoreType.DMA((1 + len(targets),)),
        ],
        compiler_params=pltpu.CompilerParams(vmem_limit_bytes=48 * 2**20),
        cost_estimate=HINT,
    )(source, block_start, place, *bodies, *tails, *late)


def on_device(series, block_start):
    local_subjects, slab, duration = series.shape
    rows, cols = lax.axis_size("row"), lax.axis_size("col")
    count = rows * cols
    window = count * slab
    subjs = lax.axis_size("subj")
    chips = subjs // 2
    cuts = (0, slab // 2, slab)
    order = cycle(rows, cols)
    onward = [(order[i], order[(i + 1) % count]) for i in range(count)]
    backward = [(b, a) for a, b in onward]
    reach = count // 2
    offsets = [0]
    for d in range(1, reach):
        offsets += [d, -d]
    offsets.append(reach)
    table = np.zeros((count, count), np.int32)
    for i, device in enumerate(order):
        table[device] = [order[(i - d) % count] for d in offsets]
    position = lax.axis_index(SLABS)
    source = jnp.asarray(table)[position]
    place = jnp.stack([position, lax.axis_index("subj")]).astype(jnp.int32)

    def gather(a, gate=None):
        got = [[normed[0][a], normed[1][a]]]
        for d in range(1, reach):
            ahead, behind = got[max(2 * d - 3, 0)], got[max(2 * d - 2, 0)]
            got += [[None, None], [None, None]]
            for half in range(2):
                waits = gate(d, half, got) if gate else ()
                if d > 1:
                    ahead[half], behind[half] = after([ahead[half], behind[half]], waits)
                elif waits:
                    (ahead[half],) = after([ahead[half]], waits)
                got[-2][half] = lax.ppermute(ahead[half], SLABS, onward)
                got[-1][half] = lax.ppermute(behind[half], SLABS, backward)
        last = []
        for half, side, way in ((0, -2, onward), (1, -1, backward)):
            waits = gate(reach, half, got) if gate else ()
            (got[side][half],) = after([got[side][half]], [got[-3 - side][half], *waits])
            last.append(lax.ppermute(got[side][half], SLABS, way))
        got.append(last)
        return got

    def flat(pairs):
        return [piece for pair in pairs for piece in pair]

    swap = [(s, s ^ 1) for s in range(subjs)]
    columns = jnp.swapaxes(series, 1, 2)
    normed = [normalize(columns, cuts[half], cuts[half + 1]) for half in range(2)]
    everything = [gather(0)]
    chunk = window // subjs
    width = math.gcd(chunk, 256)
    early = -(-chunk // width // 2) * width
    cut = ((0, early), (early, chunk - early))
    aways = [*range(1, chips), 0]

    def share(a, targets, late=()):
        bodies, tails = flat(everything[a]), flat(everything[0])
        return scores(source, block_start, place, a, targets, bodies, tails, cuts, window, chips, duration, late)

    def cross(other, hold=()):
        if hold:
            (other,) = after([other], hold)
        return lax.ppermute(other, "subj", swap)

    def send(summed, d, cost, before=()):
        there = lax.ppermute(summed, "subj", [(s, (s + 2 * d) % subjs) for s in range(subjs)])
        return after([there], before, cost)[0]

    def added(same, crossed):
        return (same.astype(jnp.float32) + crossed.astype(jnp.float32)).astype(jnp.bfloat16)

    terms, starts = [], []
    for a in range(1, local_subjects):
        shares, sums, gone = [], [], []

        def gate(d, half, got, a=a, before=everything[-1], shares=shares, sums=sums, gone=gone):
            if d == 1:
                return [before[-3][half], before[-2][half]]
            n = d - 2
            if half == 0 and n < chips - 1:
                late = [*got[2 * n - 1], *got[2 * n]] if n else ()
                shares.append(share(a - 1, [(aways[n], flip, *part) for part in cut for flip in (0, 1)], late))
            waits = [shares[n][0]] if n < chips - 1 else []
            if d < reach:
                return waits
            if half == 0:
                for m, (away, arrays) in enumerate(zip(aways[:-1], shares)):
                    hold = [got[2 * m + 1][0], got[2 * m + 2][0]]
                    for (start, _), same, other in zip(cut, arrays[::2], arrays[1::2]):
                        sums.append(added(same, cross(other, hold)))
                        gone.append(send(sums[-1], away, SHORT))
                        starts.append(start)
                return sums
            return [*sums, *gone[1::2]]

        everything.append(gather(a, gate))
        terms += gone
        same, other = share(a - 1, [(0, flip, 0, chunk) for flip in (0, 1)], [everything[a][-3][0], everything[a][-2][1]])
        gone.append(same)
        terms += [same, cross(other)]
        starts += [0, 0]
    last = local_subjects - 1
    scale = 1 / (local_subjects * subjs)
    late = gone
    for d in aways[:-2]:
        same, other = share(last, [(d, 0, 0, chunk), (d, 1, 0, chunk)], late)
        late = [added(same, cross(other))]
        terms.append(send(late[0], d, LONG))
        starts.append(0)
    d = aways[-2]
    same, other = share(last, [(d, 0, 0, early), (d, 1, 0, early)], late)
    leading = added(same, cross(other))
    pieces = [(d, 1, k, width) for k in range(early, chunk, width)]
    ends = [*range(0, chunk - width, 2 * width), chunk - width, chunk]
    others = [(0, 1, k, end - k) for k, end in zip(ends, ends[1:])]
    arrays = share(last, [*pieces, (d, 0, early, chunk - early), *others], [leading])
    crossed = jnp.concatenate([cross(array) for array in arrays[: len(pieces)]], axis=1)
    summed = added(arrays[len(pieces)], crossed)
    (same,) = share(last, [(0, 0, 0, chunk)], [summed])
    there = send(leading, d, LONG, [same])
    terms += [same, there]
    starts += [0, 0]
    for array, (_, _, start, _) in zip(arrays[len(pieces) + 1 :], others):
        terms.append(cross(array, [there] if start == others[-1][2] else ()))
        starts.append(start)
    out = combine(terms, starts, slab, chunk, width, scale)
    return finish(send(summed, d, LONG, [out]), out, early, scale)


def solution(mesh):
    return jax.shard_map(
        on_device,
        mesh=mesh,
        in_specs=(P("subj", SLABS, None), P()),
        out_specs=P(SLABS, "subj"),
        check_vma=False,
    )
```

```python
import functools
import math

import jax
import jax.numpy as jnp
import numpy as np
from jax import lax
from jax.experimental import pallas as pl
from jax.experimental.pallas import tpu as pltpu
from jax.sharding import PartitionSpec as P

clip_limit = 0.99
epsilon = 1e-05
SLABS = ("row", "col")
LANES = 128
HINT = pl.CostEstimate(flops=0, bytes_accessed=1024, transcendentals=0)
SHORT = pl.CostEstimate(flops=0, bytes_accessed=1024, transcendentals=0)
LONG = pl.CostEstimate(flops=0, bytes_accessed=2**27, transcendentals=0)
ANY = pl.BlockSpec(memory_space=pl.ANY)


def cycle(rows, cols):
    if cols == 1:
        return list(range(rows))
    walk = [(r, 0) for r in range(rows)]
    for i, r in enumerate(reversed(range(rows))):
        back = list(range(1, cols))
        walk += [(r, c) for c in (back if i % 2 == 0 else back[::-1])]
    return [r * cols + c for r, c in walk]


def normalize_kernel(series_ref, first_ref, *refs, begin, lead):
    other_refs, (raw, columns, sems) = refs[:-3], refs[-3:]
    subjects, duration, lanes = raw.shape
    body = duration // LANES * LANES
    tail = duration - body
    rows = first_ref.shape[0]
    width = LANES if lanes % LANES == 0 else lanes
    steps = lanes // width

    def copy(i):
        a, here = i % subjects, pl.ds(i // subjects * width, width)
        there = pl.ds(begin + i // subjects * width, width)
        return pltpu.make_async_copy(series_ref.at[a, :, there], raw.at[a, :, here], sems.at[i])

    for i in range(subjects * steps):
        copy(i).start()
    columns[:, duration + (subjects - 1) * tail :] = jnp.zeros(
        (subjects, LANES - subjects * tail, width), jnp.float32
    )
    for n in range(steps):
        here = pl.ds(n * width, width)
        for a in range(subjects):
            copy(n * subjects + a).wait()
            values = raw[a, :, here]
            center = jnp.mean(values, axis=0, keepdims=True)
            away = values - center
            spread = jnp.mean(away * away, axis=0, keepdims=True)
            normed = away * lax.rsqrt(spread + epsilon)
            columns[a, :duration] = normed
            if a:
                columns[0, duration + (a - 1) * tail : duration + a * tail] = normed[body:]
        low, high = max(n * width, lead), min((n + 1) * width, lead + rows)
        for a, out_ref in enumerate((first_ref, *other_refs)):
            out = columns[a, : out_ref.shape[1]].astype(jnp.bfloat16).T
            out_ref[low - lead : high - lead] = out[low - n * width : high - n * width]


def normalize(series, begin, end):
    subjects, duration, slab = series.shape
    body = duration // LANES * LANES
    low, high = begin // LANES * LANES, min(-(-end // LANES) * LANES, slab)
    lanes = high - low
    width = LANES if lanes % LANES == 0 else lanes
    widths = [body + LANES] + [body] * (subjects - 1)
    return pl.pallas_call(
        functools.partial(normalize_kernel, begin=low, lead=begin - low),
        in_specs=[pl.BlockSpec(memory_space=pltpu.HBM)],
        out_shape=[jax.ShapeDtypeStruct((end - begin, w), jnp.bfloat16) for w in widths],
        scratch_shapes=[
            pltpu.VMEM((subjects, duration, lanes), jnp.float32),
            pltpu.VMEM((subjects, body + LANES, width), jnp.float32),
            pltpu.SemaphoreType.DMA((subjects * (lanes // width),)),
        ],
        compiler_params=pltpu.CompilerParams(vmem_limit_bytes=48 * 2**20),
        cost_estimate=HINT,
    )(series)


def after(pieces, others, cost=HINT):
    def nothing(*refs):
        pass

    return pl.pallas_call(
        nothing,
        in_specs=[ANY] * (len(pieces) + len(others)),
        out_specs=[ANY] * len(pieces),
        out_shape=[jax.ShapeDtypeStruct(piece.shape, piece.dtype) for piece in pieces],
        input_output_aliases={i: i for i in range(len(pieces))},
        cost_estimate=cost,
    )(*pieces, *others)


def combine_kernel(*refs, starts, width, scale):
    *in_refs, out_ref = refs
    for k in range(0, out_ref.shape[1], width):
        total = jnp.zeros((out_ref.shape[0], width), jnp.float32)
        for ref, start in zip(in_refs, starts):
            if start <= k < start + ref.shape[1]:
                total = total + ref[:, pl.ds(k - start, width)].astype(jnp.float32)
        out_ref[:, pl.ds(k, width)] = total * scale


def combine(terms, starts, slab, columns, width, scale):
    step = max(d for d in range(16, 161, 16) if slab % d == 0)
    return pl.pallas_call(
        functools.partial(combine_kernel, starts=starts, width=width, scale=scale),
        grid=(slab // step,),
        in_specs=[pl.BlockSpec((step, term.shape[1]), lambda i: (i, 0)) for term in terms],
        out_specs=pl.BlockSpec((step, columns), lambda i: (i, 0)),
        out_shape=jax.ShapeDtypeStruct((slab, columns), jnp.float32),
        compiler_params=pltpu.CompilerParams(vmem_limit_bytes=48 * 2**20),
        cost_estimate=HINT,
    )(*terms)


def finish_kernel(part_ref, before_ref, out_ref, *, scale):
    out_ref[...] = before_ref[...] + part_ref[...].astype(jnp.float32) * scale


def finish(part, before, first, scale):
    slab = before.shape[0]
    width = math.gcd(part.shape[1], first)
    block = (slab, width)
    there = pl.BlockSpec(block, lambda i, j: (i, first // width + j))
    return pl.pallas_call(
        functools.partial(finish_kernel, scale=scale),
        grid=(slab // block[0], part.shape[1] // width),
        in_specs=[pl.BlockSpec(block, lambda i, j: (i, j)), there],
        out_specs=there,
        out_shape=jax.ShapeDtypeStruct(before.shape, jnp.float32),
        input_output_aliases={1: 0},
        cost_estimate=HINT,
    )(part, before)


def spans(targets):
    areas = {}
    for away, flip, first, columns in targets:
        start, size = areas.get((away, flip), (first, 0))
        areas[away, flip] = (start, size + columns)
    return areas


def scores_kernel(
    source_ref, block_start_ref, place_ref, *refs, subject, targets, cuts, slab, granule, block_rows, chips, chunk, duration
):
    count = source_ref.shape[0]
    bodies, tails = refs[: 2 * count], refs[2 * count : 4 * count]
    areas = spans(targets)
    own_rows, products_a, products_b, place_of, sems = refs[-5:]
    refs = refs[-5 - len(areas) - len(targets) : -5]
    out_refs, columns_refs = refs[: len(targets)], refs[len(targets) :]
    body = duration // LANES * LANES
    tail = duration - body
    for a in range(block_start_ref.shape[0]):
        place_of[block_start_ref[a] // block_rows] = a

    position, subj = place_ref[0], place_ref[1]
    chip, core = subj // 2, subj % 2
    wanted = [(position * slab, own_rows)]
    for ((away, flip), (first, _)), columns_ref in zip(areas.items(), columns_refs):
        owner = (chip + away) % chips * 2 + (core + flip) % 2
        wanted.append((owner * chunk + first, columns_ref))

    def copy(piece, first, begin, end, n, to_ref, offset):
        def start(g, _):
            here = pl.ds(pl.multiple_of(g * granule - first, granule), granule)
            there = pl.ds(pl.multiple_of(g * granule - offset, granule), granule)
            if subject == 0:
                pltpu.make_async_copy(tails[piece].at[here], to_ref.at[there], sems.at[n]).start()
            else:
                pltpu.make_async_copy(bodies[piece].at[here], to_ref.at[there, :body], sems.at[n]).start()
                pltpu.make_async_copy(tails[piece].at[here, body:], to_ref.at[there, body:], sems.at[n]).start()
            return 0

        low = jnp.maximum(begin, offset)
        high = jnp.minimum(end, offset + to_ref.shape[0])
        lax.fori_loop(low // granule, jnp.maximum(low, high) // granule, start, 0)

    blocks = block_start_ref.shape[0]
    for slot in range(count):
        for half in range(2):
            low = source_ref[slot] * slab + cuts[half]
            length = cuts[half + 1] - cuts[half]
            block = low // block_rows
            before = jnp.minimum(length, (block + 1) * block_rows - low)
            first = place_of[block] * block_rows + low - block * block_rows
            follow = place_of[jnp.minimum(block + 1, blocks - 1)] * block_rows - before
            for n, (offset, to_ref) in enumerate(wanted):
                copy(2 * slot + half, first, first, first + before, n, to_ref, offset)
                copy(2 * slot + half, follow, follow + before, follow + length, n, to_ref, offset)

    def arrived(n):
        to_ref = wanted[n][1]
        pltpu.make_async_copy(to_ref, to_ref, sems.at[n]).wait()

    arrived(0)
    lane = lax.broadcasted_iota(jnp.int32, (slab, LANES), 1)
    kept = (lane >= subject * tail) & (lane < (subject + 1) * tail)
    own_rows[:, body:] = jnp.where(kept, own_rows[:, body:].astype(jnp.float32), 0.0).astype(jnp.bfloat16)

    limit = clip_limit * duration
    widest = products_a.shape[1]
    tiles = []
    for (away, flip, first, columns), out_ref in zip(targets, out_refs):
        n = list(areas).index((away, flip))
        start = first - areas[away, flip][0]
        tiles += [(n + 1, start, k, min(widest, columns - k), out_ref) for k in range(0, columns, widest)]
    buffers = (products_a, products_b)

    def multiply(i):
        n, first, k, width, _ = tiles[i]
        if n not in [tile[0] for tile in tiles[:i]]:
            arrived(n)
        buffers[i % 2][:, :width] = lax.dot_general(
            own_rows[...], wanted[n][1][pl.ds(first + k, width)], (((1,), (1,)), ((), ())), preferred_element_type=jnp.float32
        )

    def score(i):
        _, _, k, width, out_ref = tiles[i]
        products = jnp.clip(buffers[i % 2][:, :width], -limit, limit)
        fisher = jnp.log(duration + products) - jnp.log(duration - products)
        out_ref[:, pl.ds(k, width)] = fisher.astype(jnp.bfloat16)

    multiply(0)
    for i in range(1, len(tiles)):
        multiply(i)
        score(i - 1)
    score(len(tiles) - 1)


def scores(source, block_start, place, subject, targets, bodies, tails, cuts, window, chips, duration, late=()):
    slab = cuts[-1]
    block_rows = window // block_start.shape[0]
    chunk = window // (2 * chips)
    sizes = [columns for _, _, _, columns in targets]
    granule = math.gcd(*cuts, *sizes, *(first for _, _, first, _ in targets), block_rows)
    widest = min(512, *sizes)
    padded = tails[0].shape[1]
    smem = pl.BlockSpec(memory_space=pltpu.SMEM)
    return pl.pallas_call(
        functools.partial(
            scores_kernel,
            subject=subject,
            targets=targets,
            cuts=cuts,
            slab=slab,
            granule=granule,
            block_rows=block_rows,
            chips=chips,
            chunk=chunk,
            duration=duration,
        ),
        in_specs=[smem, smem, smem] + [ANY] * (2 * len(tails) + len(late)),
        out_shape=[jax.ShapeDtypeStruct((slab, columns), jnp.bfloat16) for columns in sizes],
        scratch_shapes=[pltpu.VMEM((columns, padded), jnp.bfloat16) for _, columns in spans(targets).values()]
        + [
            pltpu.VMEM((slab, padded), jnp.bfloat16),
            pltpu.VMEM((slab, widest), jnp.float32),
            pltpu.VMEM((slab, widest), jnp.float32),
            pltpu.SMEM((block_start.shape[0],), jnp.int32),
            pltpu.SemaphoreType.DMA((1 + len(spans(targets)),)),
        ],
        compiler_params=pltpu.CompilerParams(vmem_limit_bytes=48 * 2**20),
        cost_estimate=HINT,
    )(source, block_start, place, *bodies, *tails, *late)


def on_device(series, block_start):
    local_subjects, slab, duration = series.shape
    rows, cols = lax.axis_size("row"), lax.axis_size("col")
    count = rows * cols
    window = count * slab
    subjs = lax.axis_size("subj")
    chips = subjs // 2
    cuts = (0, slab // 2, slab)
    order = cycle(rows, cols)
    onward = [(order[i], order[(i + 1) % count]) for i in range(count)]
    backward = [(b, a) for a, b in onward]
    reach = count // 2
    offsets = [0]
    for d in range(1, reach):
        offsets += [d, -d]
    offsets.append(reach)
    table = np.zeros((count, count), np.int32)
    for i, device in enumerate(order):
        table[device] = [order[(i - d) % count] for d in offsets]
    position = lax.axis_index(SLABS)
    source = jnp.asarray(table)[position]
    place = jnp.stack([position, lax.axis_index("subj")]).astype(jnp.int32)

    def gather(a, gate=None):
        got = [[normed[0][a], normed[1][a]]]
        for d in range(1, reach):
            ahead, behind = got[max(2 * d - 3, 0)], got[max(2 * d - 2, 0)]
            got += [[None, None], [None, None]]
            for half in range(2):
                waits = gate(d, half, got) if gate else ()
                if d > 1:
                    ahead[half], behind[half] = after([ahead[half], behind[half]], waits)
                elif waits:
                    (ahead[half],) = after([ahead[half]], waits)
                got[-2][half] = lax.ppermute(ahead[half], SLABS, onward)
                got[-1][half] = lax.ppermute(behind[half], SLABS, backward)
        last = []
        for half, side, way in ((0, -2, onward), (1, -1, backward)):
            waits = gate(reach, half, got) if gate else ()
            (got[side][half],) = after([got[side][half]], [got[-3 - side][half], *waits])
            last.append(lax.ppermute(got[side][half], SLABS, way))
        got.append(last)
        return got

    def flat(pairs):
        return [piece for pair in pairs for piece in pair]

    swap = [(s, s ^ 1) for s in range(subjs)]
    columns = jnp.swapaxes(series, 1, 2)
    normed = [normalize(columns, cuts[half], cuts[half + 1]) for half in range(2)]
    everything = [gather(0)]
    chunk = window // subjs
    width = math.gcd(chunk, 256)
    early = -(-chunk // width // 2) * width
    cut = ((0, early), (early, chunk - early))
    aways = [*range(1, chips), 0]

    def share(a, targets, late=()):
        bodies, tails = flat(everything[a]), flat(everything[0])
        return scores(source, block_start, place, a, targets, bodies, tails, cuts, window, chips, duration, late)

    def cross(other, hold=()):
        if hold:
            (other,) = after([other], hold)
        return lax.ppermute(other, "subj", swap)

    def send(summed, d, cost, before=()):
        there = lax.ppermute(summed, "subj", [(s, (s + 2 * d) % subjs) for s in range(subjs)])
        return after([there], before, cost)[0]

    def added(same, crossed):
        return (same.astype(jnp.float32) + crossed.astype(jnp.float32)).astype(jnp.bfloat16)

    terms, starts = [], []
    for a in range(1, local_subjects):
        shares, sums, gone = [], [], []

        def gate(d, half, got, a=a, before=everything[-1], shares=shares, sums=sums, gone=gone):
            if d == 1:
                return [before[-3][half], before[-2][half]]
            n = d - 2
            if half == 0 and n < chips - 1:
                late = [*got[2 * n - 1], *got[2 * n]] if n else ()
                shares.append(share(a - 1, [(aways[n], flip, *part) for part in cut for flip in (0, 1)], late))
            waits = [shares[n][0]] if n < chips - 1 else []
            if d < reach:
                return waits
            if half == 0:
                for m, (away, arrays) in enumerate(zip(aways[:-1], shares)):
                    hold = [got[2 * m + 1][0], got[2 * m + 2][0]]
                    for (start, _), same, other in zip(cut, arrays[::2], arrays[1::2]):
                        sums.append(added(same, cross(other, hold)))
                        gone.append(send(sums[-1], away, SHORT))
                        starts.append(start)
                return sums
            return [*sums, *gone[1::2]]

        everything.append(gather(a, gate))
        terms += gone
        same, other = share(a - 1, [(0, flip, 0, chunk) for flip in (0, 1)], [everything[a][-3][0], everything[a][-2][1]])
        gone.append(same)
        terms += [same, cross(other)]
        starts += [0, 0]
    last = local_subjects - 1
    scale = 0.5 / (local_subjects * subjs)
    late = gone
    for d in aways[:-2]:
        same, other = share(last, [(d, 0, 0, chunk), (d, 1, 0, chunk)], late)
        late = [added(same, cross(other))]
        terms.append(send(late[0], d, LONG))
        starts.append(0)
    d = aways[-2]
    same, other = share(last, [(d, 0, 0, early), (d, 1, 0, early)], late)
    leading = added(same, cross(other))
    pieces = [(d, 1, k, width) for k in range(early, chunk, width)]
    ends = [*range(0, chunk - width, 2 * width), chunk - width, chunk]
    others = [(0, 1, k, end - k) for k, end in zip(ends, ends[1:])]
    arrays = share(last, [*pieces, (d, 0, early, chunk - early), *others], [leading])
    crossed = jnp.concatenate([cross(array) for array in arrays[: len(pieces)]], axis=1)
    summed = added(arrays[len(pieces)], crossed)
    (same,) = share(last, [(0, 0, 0, chunk)], [summed])
    there = send(leading, d, LONG, [same])
    terms += [same, there]
    starts += [0, 0]
    for array, (_, _, start, _) in zip(arrays[len(pieces) + 1 :], others):
        terms.append(cross(array, [there] if start == others[-1][2] else ()))
        starts.append(start)
    out = combine(terms, starts, slab, chunk, width, scale)
    return finish(send(summed, d, LONG, [out]), out, early, scale)


def solution(mesh):
    return jax.shard_map(
        on_device,
        mesh=mesh,
        in_specs=(P("subj", SLABS, None), P()),
        out_specs=P(SLABS, "subj"),
        check_vma=False,
    )
```

```python
import functools
import math

import jax
import jax.numpy as jnp
import numpy as np
from jax import lax
from jax.experimental import pallas as pl
from jax.experimental.pallas import tpu as pltpu
from jax.sharding import PartitionSpec as P

clip_limit = 0.99
epsilon = 1e-05
SLABS = ("row", "col")
LANES = 128
HINT = pl.CostEstimate(flops=0, bytes_accessed=1024, transcendentals=0)
SHORT = pl.CostEstimate(flops=0, bytes_accessed=1024, transcendentals=0)
LONG = pl.CostEstimate(flops=0, bytes_accessed=2**27, transcendentals=0)
ANY = pl.BlockSpec(memory_space=pl.ANY)


def cycle(rows, cols):
    if cols == 1:
        return list(range(rows))
    walk = [(r, 0) for r in range(rows)]
    for i, r in enumerate(reversed(range(rows))):
        back = list(range(1, cols))
        walk += [(r, c) for c in (back if i % 2 == 0 else back[::-1])]
    return [r * cols + c for r, c in walk]


def normalize_kernel(series_ref, first_ref, *refs, begin, lead):
    other_refs, (raw, columns, sems) = refs[:-3], refs[-3:]
    subjects, duration, lanes = raw.shape
    body = duration // LANES * LANES
    tail = duration - body
    rows = first_ref.shape[0]
    width = LANES if lanes % LANES == 0 else lanes
    steps = lanes // width

    def copy(i):
        a, here = i % subjects, pl.ds(i // subjects * width, width)
        there = pl.ds(begin + i // subjects * width, width)
        return pltpu.make_async_copy(series_ref.at[a, :, there], raw.at[a, :, here], sems.at[i])

    for i in range(subjects * steps):
        copy(i).start()
    columns[:, duration + (subjects - 1) * tail :] = jnp.zeros(
        (subjects, LANES - subjects * tail, width), jnp.float32
    )
    for n in range(steps):
        here = pl.ds(n * width, width)
        for a in range(subjects):
            copy(n * subjects + a).wait()
            values = raw[a, :, here]
            center = jnp.mean(values, axis=0, keepdims=True)
            away = values - center
            spread = jnp.mean(away * away, axis=0, keepdims=True)
            normed = away * lax.rsqrt(spread + epsilon)
            columns[a, :duration] = normed
            if a:
                columns[0, duration + (a - 1) * tail : duration + a * tail] = normed[body:]
        low, high = max(n * width, lead), min((n + 1) * width, lead + rows)
        for a, out_ref in enumerate((first_ref, *other_refs)):
            out = columns[a, : out_ref.shape[1]].astype(jnp.bfloat16).T
            out_ref[low - lead : high - lead] = out[low - n * width : high - n * width]


def normalize(series, begin, end):
    subjects, duration, slab = series.shape
    body = duration // LANES * LANES
    low, high = begin // LANES * LANES, min(-(-end // LANES) * LANES, slab)
    lanes = high - low
    width = LANES if lanes % LANES == 0 else lanes
    widths = [body + LANES] + [body] * (subjects - 1)
    return pl.pallas_call(
        functools.partial(normalize_kernel, begin=low, lead=begin - low),
        in_specs=[pl.BlockSpec(memory_space=pltpu.HBM)],
        out_shape=[jax.ShapeDtypeStruct((end - begin, w), jnp.bfloat16) for w in widths],
        scratch_shapes=[
            pltpu.VMEM((subjects, duration, lanes), jnp.float32),
            pltpu.VMEM((subjects, body + LANES, width), jnp.float32),
            pltpu.SemaphoreType.DMA((subjects * (lanes // width),)),
        ],
        compiler_params=pltpu.CompilerParams(vmem_limit_bytes=48 * 2**20),
        cost_estimate=HINT,
    )(series)


def after(pieces, others, cost=HINT):
    def nothing(*refs):
        pass

    return pl.pallas_call(
        nothing,
        in_specs=[ANY] * (len(pieces) + len(others)),
        out_specs=[ANY] * len(pieces),
        out_shape=[jax.ShapeDtypeStruct(piece.shape, piece.dtype) for piece in pieces],
        input_output_aliases={i: i for i in range(len(pieces))},
        cost_estimate=cost,
    )(*pieces, *others)


def combine_kernel(*refs, starts, width, scale):
    *in_refs, out_ref = refs
    for k in range(0, out_ref.shape[1], width):
        total = jnp.zeros((out_ref.shape[0], width), jnp.float32)
        for ref, start in zip(in_refs, starts):
            if start <= k < start + ref.shape[1]:
                total = total + ref[:, pl.ds(k - start, width)].astype(jnp.float32)
        out_ref[:, pl.ds(k, width)] = total * scale


def combine(terms, starts, slab, columns, width, scale):
    step = max(d for d in range(16, 161, 16) if slab % d == 0)
    return pl.pallas_call(
        functools.partial(combine_kernel, starts=starts, width=width, scale=scale),
        grid=(slab // step,),
        in_specs=[pl.BlockSpec((step, term.shape[1]), lambda i: (i, 0)) for term in terms],
        out_specs=pl.BlockSpec((step, columns), lambda i: (i, 0)),
        out_shape=jax.ShapeDtypeStruct((slab, columns), jnp.float32),
        compiler_params=pltpu.CompilerParams(vmem_limit_bytes=48 * 2**20),
        cost_estimate=HINT,
    )(*terms)


def finish_kernel(part_ref, before_ref, out_ref, *, scale):
    out_ref[...] = before_ref[...] + part_ref[...].astype(jnp.float32) * scale


def finish(part, before, first, scale):
    slab = before.shape[0]
    width = math.gcd(part.shape[1], first)
    block = (slab, width)
    there = pl.BlockSpec(block, lambda i, j: (i, first // width + j))
    return pl.pallas_call(
        functools.partial(finish_kernel, scale=scale),
        grid=(slab // block[0], part.shape[1] // width),
        in_specs=[pl.BlockSpec(block, lambda i, j: (i, j)), there],
        out_specs=there,
        out_shape=jax.ShapeDtypeStruct(before.shape, jnp.float32),
        input_output_aliases={1: 0},
        cost_estimate=HINT,
    )(part, before)


def scores_kernel(
    source_ref, block_start_ref, place_ref, *refs, subject, targets, cuts, slab, granule, block_rows, chips, chunk, duration
):
    count = source_ref.shape[0]
    bodies, tails = refs[: 2 * count], refs[2 * count : 4 * count]
    own_rows, products_a, products_b, place_of, sems = refs[-5:]
    refs = refs[-5 - 2 * len(targets) : -5]
    out_refs, columns_refs = refs[: len(targets)], refs[len(targets) :]
    body = duration // LANES * LANES
    tail = duration - body
    for a in range(block_start_ref.shape[0]):
        place_of[block_start_ref[a] // block_rows] = a

    position, subj = place_ref[0], place_ref[1]
    chip, core = subj // 2, subj % 2
    wanted = [(position * slab, own_rows)]
    for (away, flip, first, _), columns_ref in zip(targets, columns_refs):
        owner = (chip + away) % chips * 2 + (core + flip) % 2
        wanted.append((owner * chunk + first, columns_ref))

    for slot in range(count):
        for half in range(2):
            piece = 2 * slot + half
            low = source_ref[slot] * slab + cuts[half]

            def start(g, _, piece=piece, low=low):
                stored = low + g * granule
                block = stored // block_rows
                row = place_of[block] * block_rows + (stored - block * block_rows)
                here = pl.ds(pl.multiple_of(g * granule, granule), granule)
                for n, (begin, to_ref) in enumerate(wanted):

                    @pl.when((row >= begin) & (row < begin + to_ref.shape[0]))
                    def _():
                        there = pl.ds(pl.multiple_of(row - begin, granule), granule)
                        if subject == 0:
                            pltpu.make_async_copy(tails[piece].at[here], to_ref.at[there], sems.at[n]).start()
                        else:
                            pltpu.make_async_copy(
                                bodies[piece].at[here], to_ref.at[there, :body], sems.at[n]
                            ).start()
                            pltpu.make_async_copy(
                                tails[piece].at[here, body:], to_ref.at[there, body:], sems.at[n]
                            ).start()

                return 0

            lax.fori_loop(0, (cuts[half + 1] - cuts[half]) // granule, start, 0)

    def arrived(n):
        to_ref = wanted[n][1]
        pltpu.make_async_copy(to_ref, to_ref, sems.at[n]).wait()

    arrived(0)
    lane = lax.broadcasted_iota(jnp.int32, (slab, LANES), 1)
    kept = (lane >= subject * tail) & (lane < (subject + 1) * tail)
    own_rows[:, body:] = jnp.where(kept, own_rows[:, body:].astype(jnp.float32), 0.0).astype(jnp.bfloat16)

    limit = clip_limit * duration
    widest = products_a.shape[1]
    tiles = []
    for n, out_ref in enumerate(out_refs):
        columns = out_ref.shape[1]
        tiles += [(n + 1, k, min(widest, columns - k), out_ref) for k in range(0, columns, widest)]
    buffers = (products_a, products_b)

    def multiply(i):
        n, k, width, _ = tiles[i]
        if k == 0:
            arrived(n)
        buffers[i % 2][:, :width] = lax.dot_general(
            own_rows[...], wanted[n][1][pl.ds(k, width)], (((1,), (1,)), ((), ())), preferred_element_type=jnp.float32
        )

    def score(i):
        _, k, width, out_ref = tiles[i]
        step = math.gcd(slab, 64)
        for r in range(0, slab, step):
            products = jnp.clip(buffers[i % 2][r : r + step, :width], -limit, limit)
            fisher = jnp.log(duration + products) - jnp.log(duration - products)
            out_ref[r : r + step, pl.ds(k, width)] = fisher.astype(jnp.bfloat16)

    multiply(0)
    for i in range(1, len(tiles)):
        multiply(i)
        score(i - 1)
    score(len(tiles) - 1)


def scores(source, block_start, place, subject, targets, bodies, tails, cuts, window, chips, duration, late=()):
    slab = cuts[-1]
    block_rows = window // block_start.shape[0]
    chunk = window // (2 * chips)
    sizes = [columns for _, _, _, columns in targets]
    granule = math.gcd(*cuts, *sizes, *(first for _, _, first, _ in targets), block_rows)
    widest = min(512, *sizes)
    padded = tails[0].shape[1]
    smem = pl.BlockSpec(memory_space=pltpu.SMEM)
    return pl.pallas_call(
        functools.partial(
            scores_kernel,
            subject=subject,
            targets=targets,
            cuts=cuts,
            slab=slab,
            granule=granule,
            block_rows=block_rows,
            chips=chips,
            chunk=chunk,
            duration=duration,
        ),
        in_specs=[smem, smem, smem] + [ANY] * (2 * len(tails) + len(late)),
        out_shape=[jax.ShapeDtypeStruct((slab, columns), jnp.bfloat16) for columns in sizes],
        scratch_shapes=[pltpu.VMEM((columns, padded), jnp.bfloat16) for columns in sizes]
        + [
            pltpu.VMEM((slab, padded), jnp.bfloat16),
            pltpu.VMEM((slab, widest), jnp.float32),
            pltpu.VMEM((slab, widest), jnp.float32),
            pltpu.SMEM((block_start.shape[0],), jnp.int32),
            pltpu.SemaphoreType.DMA((1 + len(targets),)),
        ],
        compiler_params=pltpu.CompilerParams(vmem_limit_bytes=48 * 2**20),
        cost_estimate=HINT,
    )(source, block_start, place, *bodies, *tails, *late)


def on_device(series, block_start):
    local_subjects, slab, duration = series.shape
    rows, cols = lax.axis_size("row"), lax.axis_size("col")
    count = rows * cols
    window = count * slab
    subjs = lax.axis_size("subj")
    chips = subjs // 2
    cuts = (0, slab // 2, slab)
    order = cycle(rows, cols)
    onward = [(order[i], order[(i + 1) % count]) for i in range(count)]
    backward = [(b, a) for a, b in onward]
    reach = count // 2
    offsets = [0]
    for d in range(1, reach):
        offsets += [d, -d]
    offsets.append(reach)
    table = np.zeros((count, count), np.int32)
    for i, device in enumerate(order):
        table[device] = [order[(i - d) % count] for d in offsets]
    position = lax.axis_index(SLABS)
    source = jnp.asarray(table)[position]
    place = jnp.stack([position, lax.axis_index("subj")]).astype(jnp.int32)

    def gather(a, gate=None):
        got = [[normed[0][a], normed[1][a]]]
        for d in range(1, reach):
            ahead, behind = got[max(2 * d - 3, 0)], got[max(2 * d - 2, 0)]
            got += [[None, None], [None, None]]
            for half in range(2):
                waits = gate(d, half, got) if gate else ()
                if d > 1:
                    ahead[half], behind[half] = after([ahead[half], behind[half]], waits)
                elif waits:
                    (ahead[half],) = after([ahead[half]], waits)
                got[-2][half] = lax.ppermute(ahead[half], SLABS, onward)
                got[-1][half] = lax.ppermute(behind[half], SLABS, backward)
        last = []
        for half, side, way in ((0, -2, onward), (1, -1, backward)):
            waits = gate(reach, half, got) if gate else ()
            (got[side][half],) = after([got[side][half]], [got[-3 - side][half], *waits])
            last.append(lax.ppermute(got[side][half], SLABS, way))
        got.append(last)
        return got

    def flat(pairs):
        return [piece for pair in pairs for piece in pair]

    swap = [(s, s ^ 1) for s in range(subjs)]
    columns = jnp.swapaxes(series, 1, 2)
    normed = [normalize(columns, cuts[half], cuts[half + 1]) for half in range(2)]
    everything = [gather(0)]
    chunk = window // subjs
    width = math.gcd(chunk, 256)
    early = -(-chunk // width // 2) * width
    cut = ((0, early), (early, chunk - early))
    aways = [*range(1, chips), 0]

    def share(a, targets, late=()):
        bodies, tails = flat(everything[a]), flat(everything[0])
        return scores(source, block_start, place, a, targets, bodies, tails, cuts, window, chips, duration, late)

    def cross(other, hold=()):
        if hold:
            (other,) = after([other], hold)
        return lax.ppermute(other, "subj", swap)

    def send(summed, d, cost, before=()):
        there = lax.ppermute(summed, "subj", [(s, (s + 2 * d) % subjs) for s in range(subjs)])
        return after([there], before, cost)[0]

    def added(same, crossed):
        return (same.astype(jnp.float32) + crossed.astype(jnp.float32)).astype(jnp.bfloat16)

    terms, starts = [], []
    for a in range(1, local_subjects):
        shares, sums, gone = [], [], []

        def gate(d, half, got, a=a, before=everything[-1], shares=shares, sums=sums, gone=gone):
            if d == 1:
                return [before[-3][half], before[-2][half]]
            n = d - 2
            if half == 0 and n < chips - 1:
                late = [*got[2 * n - 1], *got[2 * n]] if n else ()
                shares.append(share(a - 1, [(aways[n], flip, *part) for part in cut for flip in (0, 1)], late))
            waits = [shares[n][0]] if n < chips - 1 else []
            if d < reach:
                return waits
            if half == 0:
                for m, (away, arrays) in enumerate(zip(aways[:-1], shares)):
                    hold = [got[2 * m + 1][0], got[2 * m + 2][0]]
                    for (start, _), same, other in zip(cut, arrays[::2], arrays[1::2]):
                        sums.append(added(same, cross(other, hold)))
                        gone.append(send(sums[-1], away, SHORT))
                        starts.append(start)
                return sums
            return [*sums, *gone[1::2]]

        everything.append(gather(a, gate))
        terms += gone
        same, other = share(a - 1, [(0, flip, 0, chunk) for flip in (0, 1)], [everything[a][-3][0], everything[a][-2][1]])
        gone.append(same)
        terms += [same, cross(other)]
        starts += [0, 0]
    last = local_subjects - 1
    scale = 0.5 / (local_subjects * subjs)
    late = gone
    for d in aways[:-2]:
        same, other = share(last, [(d, 0, 0, chunk), (d, 1, 0, chunk)], late)
        late = [added(same, cross(other))]
        terms.append(send(late[0], d, LONG))
        starts.append(0)
    d = aways[-2]
    same, other = share(last, [(d, 0, 0, early), (d, 1, 0, early)], late)
    leading = added(same, cross(other))
    pieces = [(d, 1, k, width) for k in range(early, chunk, width)]
    ends = [*range(0, chunk - width, 2 * width), chunk - width, chunk]
    others = [(0, 1, k, end - k) for k, end in zip(ends, ends[1:])]
    arrays = share(last, [*pieces, (d, 0, early, chunk - early), *others], [leading])
    crossed = jnp.concatenate([cross(array) for array in arrays[: len(pieces)]], axis=1)
    summed = added(arrays[len(pieces)], crossed)
    (same,) = share(last, [(0, 0, 0, chunk)], [summed])
    there = send(leading, d, LONG, [same])
    terms += [same, there]
    starts += [0, 0]
    for array, (_, _, start, _) in zip(arrays[len(pieces) + 1 :], others):
        terms.append(cross(array, [there] if start == others[-1][2] else ()))
        starts.append(start)
    out = combine(terms, starts, slab, chunk, width, scale)
    return finish(send(summed, d, LONG, [out]), out, early, scale)


def solution(mesh):
    return jax.shard_map(
        on_device,
        mesh=mesh,
        in_specs=(P("subj", SLABS, None), P()),
        out_specs=P(SLABS, "subj"),
        check_vma=False,
    )
```

```python
import functools
import math

import jax
import jax.numpy as jnp
import numpy as np
from jax import lax
from jax.experimental import pallas as pl
from jax.experimental.pallas import tpu as pltpu
from jax.sharding import PartitionSpec as P

clip_limit = 0.99
epsilon = 1e-05
SLABS = ("row", "col")
LANES = 128
HINT = pl.CostEstimate(flops=0, bytes_accessed=1024, transcendentals=0)
SHORT = pl.CostEstimate(flops=0, bytes_accessed=1024, transcendentals=0)
LONG = pl.CostEstimate(flops=0, bytes_accessed=2**27, transcendentals=0)
ANY = pl.BlockSpec(memory_space=pl.ANY)


def cycle(rows, cols):
    if cols == 1:
        return list(range(rows))
    walk = [(r, 0) for r in range(rows)]
    for i, r in enumerate(reversed(range(rows))):
        back = list(range(1, cols))
        walk += [(r, c) for c in (back if i % 2 == 0 else back[::-1])]
    return [r * cols + c for r, c in walk]


def normalize_kernel(series_ref, first_ref, *refs, begin, lead):
    other_refs, (raw, columns, sems) = refs[:-3], refs[-3:]
    subjects, duration, lanes = raw.shape
    body = duration // LANES * LANES
    tail = duration - body
    rows = first_ref.shape[0]
    width = LANES if lanes % LANES == 0 else lanes
    steps = lanes // width

    def copy(i):
        a, here = i % subjects, pl.ds(i // subjects * width, width)
        there = pl.ds(begin + i // subjects * width, width)
        return pltpu.make_async_copy(series_ref.at[a, :, there], raw.at[a, :, here], sems.at[i])

    for i in range(subjects * steps):
        copy(i).start()
    columns[:, duration + (subjects - 1) * tail :] = jnp.zeros(
        (subjects, LANES - subjects * tail, width), jnp.float32
    )
    for n in range(steps):
        here = pl.ds(n * width, width)
        for a in range(subjects):
            copy(n * subjects + a).wait()
            values = raw[a, :, here]
            center = jnp.mean(values, axis=0, keepdims=True)
            away = values - center
            spread = jnp.mean(away * away, axis=0, keepdims=True)
            normed = away * lax.rsqrt(spread + epsilon)
            columns[a, :duration] = normed
            if a:
                columns[0, duration + (a - 1) * tail : duration + a * tail] = normed[body:]
        low, high = max(n * width, lead), min((n + 1) * width, lead + rows)
        for a, out_ref in enumerate((first_ref, *other_refs)):
            out = columns[a, : out_ref.shape[1]].astype(jnp.bfloat16).T
            out_ref[low - lead : high - lead] = out[low - n * width : high - n * width]


def normalize(series, begin, end):
    subjects, duration, slab = series.shape
    body = duration // LANES * LANES
    low, high = begin // LANES * LANES, min(-(-end // LANES) * LANES, slab)
    lanes = high - low
    width = LANES if lanes % LANES == 0 else lanes
    widths = [body + LANES] + [body] * (subjects - 1)
    return pl.pallas_call(
        functools.partial(normalize_kernel, begin=low, lead=begin - low),
        in_specs=[pl.BlockSpec(memory_space=pltpu.HBM)],
        out_shape=[jax.ShapeDtypeStruct((end - begin, w), jnp.bfloat16) for w in widths],
        scratch_shapes=[
            pltpu.VMEM((subjects, duration, lanes), jnp.float32),
            pltpu.VMEM((subjects, body + LANES, width), jnp.float32),
            pltpu.SemaphoreType.DMA((subjects * (lanes // width),)),
        ],
        compiler_params=pltpu.CompilerParams(vmem_limit_bytes=48 * 2**20),
        cost_estimate=HINT,
    )(series)


def after(pieces, others, cost=HINT):
    def nothing(*refs):
        pass

    return pl.pallas_call(
        nothing,
        in_specs=[ANY] * (len(pieces) + len(others)),
        out_specs=[ANY] * len(pieces),
        out_shape=[jax.ShapeDtypeStruct(piece.shape, piece.dtype) for piece in pieces],
        input_output_aliases={i: i for i in range(len(pieces))},
        cost_estimate=cost,
    )(*pieces, *others)


def combine_kernel(*refs, starts, width, scale):
    *in_refs, out_ref = refs
    for k in range(0, out_ref.shape[1], width):
        total = jnp.zeros((out_ref.shape[0], width), jnp.float32)
        for ref, start in zip(in_refs, starts):
            if start <= k < start + ref.shape[1]:
                total = total + ref[:, pl.ds(k - start, width)].astype(jnp.float32)
        out_ref[:, pl.ds(k, width)] = total * scale


def combine(terms, starts, slab, columns, width, scale):
    step = max(d for d in range(16, 161, 16) if slab % d == 0)
    return pl.pallas_call(
        functools.partial(combine_kernel, starts=starts, width=width, scale=scale),
        grid=(slab // step,),
        in_specs=[pl.BlockSpec((step, term.shape[1]), lambda i: (i, 0)) for term in terms],
        out_specs=pl.BlockSpec((step, columns), lambda i: (i, 0)),
        out_shape=jax.ShapeDtypeStruct((slab, columns), jnp.float32),
        compiler_params=pltpu.CompilerParams(vmem_limit_bytes=48 * 2**20),
        cost_estimate=HINT,
    )(*terms)


def finish_kernel(part_ref, before_ref, out_ref, *, scale):
    out_ref[...] = before_ref[...] + part_ref[...].astype(jnp.float32) * scale


def finish(part, before, first, scale):
    slab = before.shape[0]
    width = math.gcd(part.shape[1], first)
    block = (slab, width)
    there = pl.BlockSpec(block, lambda i, j: (i, first // width + j))
    return pl.pallas_call(
        functools.partial(finish_kernel, scale=scale),
        grid=(slab // block[0], part.shape[1] // width),
        in_specs=[pl.BlockSpec(block, lambda i, j: (i, j)), there],
        out_specs=there,
        out_shape=jax.ShapeDtypeStruct(before.shape, jnp.float32),
        input_output_aliases={1: 0},
        cost_estimate=HINT,
    )(part, before)


def scores_kernel(
    source_ref, block_start_ref, place_ref, *refs, subject, targets, cuts, slab, granule, block_rows, chips, chunk, duration
):
    count = source_ref.shape[0]
    bodies, tails = refs[: 2 * count], refs[2 * count : 4 * count]
    own_rows, products_a, products_b, place_of, sems = refs[-5:]
    refs = refs[-5 - 2 * len(targets) : -5]
    out_refs, columns_refs = refs[: len(targets)], refs[len(targets) :]
    body = duration // LANES * LANES
    tail = duration - body
    for a in range(block_start_ref.shape[0]):
        place_of[block_start_ref[a] // block_rows] = a

    position, subj = place_ref[0], place_ref[1]
    chip, core = subj // 2, subj % 2
    wanted = [(position * slab, own_rows)]
    for (away, flip, first, _), columns_ref in zip(targets, columns_refs):
        owner = (chip + away) % chips * 2 + (core + flip) % 2
        wanted.append((owner * chunk + first, columns_ref))

    for slot in range(count):
        for half in range(2):
            piece = 2 * slot + half
            low = source_ref[slot] * slab + cuts[half]

            def start(g, _, piece=piece, low=low):
                stored = low + g * granule
                block = stored // block_rows
                row = place_of[block] * block_rows + (stored - block * block_rows)
                here = pl.ds(pl.multiple_of(g * granule, granule), granule)
                for n, (begin, to_ref) in enumerate(wanted):

                    @pl.when((row >= begin) & (row < begin + to_ref.shape[0]))
                    def _():
                        there = pl.ds(pl.multiple_of(row - begin, granule), granule)
                        if subject == 0:
                            pltpu.make_async_copy(tails[piece].at[here], to_ref.at[there], sems.at[n]).start()
                        else:
                            pltpu.make_async_copy(
                                bodies[piece].at[here], to_ref.at[there, :body], sems.at[n]
                            ).start()
                            pltpu.make_async_copy(
                                tails[piece].at[here, body:], to_ref.at[there, body:], sems.at[n]
                            ).start()

                return 0

            lax.fori_loop(0, (cuts[half + 1] - cuts[half]) // granule, start, 0)

    def arrived(n):
        to_ref = wanted[n][1]
        pltpu.make_async_copy(to_ref, to_ref, sems.at[n]).wait()

    arrived(0)
    lane = lax.broadcasted_iota(jnp.int32, (slab, LANES), 1)
    kept = (lane >= subject * tail) & (lane < (subject + 1) * tail)
    own_rows[:, body:] = jnp.where(kept, own_rows[:, body:].astype(jnp.float32), 0.0).astype(jnp.bfloat16)

    limit = clip_limit * duration
    widest = products_a.shape[0]
    tiles = []
    for n, out_ref in enumerate(out_refs):
        columns = out_ref.shape[1]
        tiles += [(n + 1, k, min(widest, columns - k), out_ref) for k in range(0, columns, widest)]
    buffers = (products_a, products_b)

    def multiply(i):
        n, k, width, _ = tiles[i]
        if k == 0:
            arrived(n)
        buffers[i % 2][:width] = lax.dot_general(
            wanted[n][1][pl.ds(k, width)], own_rows[...], (((1,), (1,)), ((), ())), preferred_element_type=jnp.float32
        )

    def score(i):
        _, k, width, out_ref = tiles[i]
        for r in range(0, width, LANES):
            products = jnp.clip(buffers[i % 2][r : r + LANES], -limit, limit)
            fisher = jnp.log(duration + products) - jnp.log(duration - products)
            out_ref[:, pl.ds(k + r, LANES)] = fisher.T.astype(jnp.bfloat16)

    multiply(0)
    for i in range(1, len(tiles)):
        multiply(i)
        score(i - 1)
    score(len(tiles) - 1)


def scores(source, block_start, place, subject, targets, bodies, tails, cuts, window, chips, duration, late=()):
    slab = cuts[-1]
    block_rows = window // block_start.shape[0]
    chunk = window // (2 * chips)
    sizes = [columns for _, _, _, columns in targets]
    granule = math.gcd(*cuts, *sizes, *(first for _, _, first, _ in targets), block_rows)
    widest = min(512, *sizes)
    padded = tails[0].shape[1]
    smem = pl.BlockSpec(memory_space=pltpu.SMEM)
    return pl.pallas_call(
        functools.partial(
            scores_kernel,
            subject=subject,
            targets=targets,
            cuts=cuts,
            slab=slab,
            granule=granule,
            block_rows=block_rows,
            chips=chips,
            chunk=chunk,
            duration=duration,
        ),
        in_specs=[smem, smem, smem] + [ANY] * (2 * len(tails) + len(late)),
        out_shape=[jax.ShapeDtypeStruct((slab, columns), jnp.bfloat16) for columns in sizes],
        scratch_shapes=[pltpu.VMEM((columns, padded), jnp.bfloat16) for columns in sizes]
        + [
            pltpu.VMEM((slab, padded), jnp.bfloat16),
            pltpu.VMEM((widest, slab), jnp.float32),
            pltpu.VMEM((widest, slab), jnp.float32),
            pltpu.SMEM((block_start.shape[0],), jnp.int32),
            pltpu.SemaphoreType.DMA((1 + len(targets),)),
        ],
        compiler_params=pltpu.CompilerParams(vmem_limit_bytes=48 * 2**20),
        cost_estimate=HINT,
    )(source, block_start, place, *bodies, *tails, *late)


def on_device(series, block_start):
    local_subjects, slab, duration = series.shape
    rows, cols = lax.axis_size("row"), lax.axis_size("col")
    count = rows * cols
    window = count * slab
    subjs = lax.axis_size("subj")
    chips = subjs // 2
    cuts = (0, slab // 2, slab)
    order = cycle(rows, cols)
    onward = [(order[i], order[(i + 1) % count]) for i in range(count)]
    backward = [(b, a) for a, b in onward]
    reach = count // 2
    offsets = [0]
    for d in range(1, reach):
        offsets += [d, -d]
    offsets.append(reach)
    table = np.zeros((count, count), np.int32)
    for i, device in enumerate(order):
        table[device] = [order[(i - d) % count] for d in offsets]
    position = lax.axis_index(SLABS)
    source = jnp.asarray(table)[position]
    place = jnp.stack([position, lax.axis_index("subj")]).astype(jnp.int32)

    def gather(a, gate=None):
        got = [[normed[0][a], normed[1][a]]]
        for d in range(1, reach):
            ahead, behind = got[max(2 * d - 3, 0)], got[max(2 * d - 2, 0)]
            got += [[None, None], [None, None]]
            for half in range(2):
                waits = gate(d, half, got) if gate else ()
                if d > 1:
                    ahead[half], behind[half] = after([ahead[half], behind[half]], waits)
                elif waits:
                    (ahead[half],) = after([ahead[half]], waits)
                got[-2][half] = lax.ppermute(ahead[half], SLABS, onward)
                got[-1][half] = lax.ppermute(behind[half], SLABS, backward)
        last = []
        for half, side, way in ((0, -2, onward), (1, -1, backward)):
            waits = gate(reach, half, got) if gate else ()
            (got[side][half],) = after([got[side][half]], [got[-3 - side][half], *waits])
            last.append(lax.ppermute(got[side][half], SLABS, way))
        got.append(last)
        return got

    def flat(pairs):
        return [piece for pair in pairs for piece in pair]

    swap = [(s, s ^ 1) for s in range(subjs)]
    columns = jnp.swapaxes(series, 1, 2)
    normed = [normalize(columns, cuts[half], cuts[half + 1]) for half in range(2)]
    everything = [gather(0)]
    chunk = window // subjs
    width = math.gcd(chunk, 256)
    early = -(-chunk // width // 2) * width
    cut = ((0, early), (early, chunk - early))
    aways = [*range(1, chips), 0]

    def share(a, targets, late=()):
        bodies, tails = flat(everything[a]), flat(everything[0])
        return scores(source, block_start, place, a, targets, bodies, tails, cuts, window, chips, duration, late)

    def cross(other, hold=()):
        if hold:
            (other,) = after([other], hold)
        return lax.ppermute(other, "subj", swap)

    def send(summed, d, cost, before=()):
        there = lax.ppermute(summed, "subj", [(s, (s + 2 * d) % subjs) for s in range(subjs)])
        return after([there], before, cost)[0]

    def added(same, crossed):
        return (same.astype(jnp.float32) + crossed.astype(jnp.float32)).astype(jnp.bfloat16)

    terms, starts = [], []
    for a in range(1, local_subjects):
        shares, sums, gone = [], [], []

        def gate(d, half, got, a=a, before=everything[-1], shares=shares, sums=sums, gone=gone):
            if d == 1:
                return [before[-3][half], before[-2][half]]
            n = d - 2
            if half == 0 and n < chips - 1:
                late = [*got[2 * n - 1], *got[2 * n]] if n else ()
                shares.append(share(a - 1, [(aways[n], flip, *part) for part in cut for flip in (0, 1)], late))
            waits = [shares[n][0]] if n < chips - 1 else []
            if d < reach:
                return waits
            if half == 0:
                for m, (away, arrays) in enumerate(zip(aways[:-1], shares)):
                    hold = [got[2 * m + 1][0], got[2 * m + 2][0]]
                    for (start, _), same, other in zip(cut, arrays[::2], arrays[1::2]):
                        sums.append(added(same, cross(other, hold)))
                        gone.append(send(sums[-1], away, SHORT))
                        starts.append(start)
                return sums
            return [*sums, *gone[1::2]]

        everything.append(gather(a, gate))
        terms += gone
        same, other = share(a - 1, [(0, flip, 0, chunk) for flip in (0, 1)], [everything[a][-3][0], everything[a][-2][1]])
        gone.append(same)
        terms += [same, cross(other)]
        starts += [0, 0]
    last = local_subjects - 1
    scale = 0.5 / (local_subjects * subjs)
    late = gone
    for d in aways[:-2]:
        same, other = share(last, [(d, 0, 0, chunk), (d, 1, 0, chunk)], late)
        late = [added(same, cross(other))]
        terms.append(send(late[0], d, LONG))
        starts.append(0)
    d = aways[-2]
    same, other = share(last, [(d, 0, 0, early), (d, 1, 0, early)], late)
    leading = added(same, cross(other))
    pieces = [(d, 1, k, width) for k in range(early, chunk, width)]
    ends = [*range(0, chunk - width, 2 * width), chunk - width, chunk]
    others = [(0, 1, k, end - k) for k, end in zip(ends, ends[1:])]
    arrays = share(last, [*pieces, (d, 0, early, chunk - early), *others], [leading])
    crossed = jnp.concatenate([cross(array) for array in arrays[: len(pieces)]], axis=1)
    summed = added(arrays[len(pieces)], crossed)
    (same,) = share(last, [(0, 0, 0, chunk)], [summed])
    there = send(leading, d, LONG, [same])
    terms += [same, there]
    starts += [0, 0]
    for array, (_, _, start, _) in zip(arrays[len(pieces) + 1 :], others):
        terms.append(cross(array, [there] if start == others[-1][2] else ()))
        starts.append(start)
    out = combine(terms, starts, slab, chunk, width, scale)
    return finish(send(summed, d, LONG, [out]), out, early, scale)


def solution(mesh):
    return jax.shard_map(
        on_device,
        mesh=mesh,
        in_specs=(P("subj", SLABS, None), P()),
        out_specs=P(SLABS, "subj"),
        check_vma=False,
    )
```
